32 devices in a mesh: wide: 8 (over y, x, core), narrow: 4 (over z).
Axes of the slice: x: 2, y: 2, z: 4, core: 2. Of those that a mesh axis runs over, the one named last changes fastest.
Arguments:
- patches: bfloat16 [64, 512, 768], P(('wide', 'narrow')), may hold values from -6 to 6
- lengths: int32 [64, 6], P(('wide', 'narrow')), may hold values from 1 to 196, 512 in all within a row
- w_qkv: bfloat16 [768, 2304], P('wide', 'narrow'), may hold values from -0.3125 to 0.3125
- w_out: bfloat16 [768, 768], P('wide', 'narrow'), may hold values from -0.625 to 0.625
- w_up: bfloat16 [768, 3072], P('wide', 'narrow'), may hold values from -0.21875 to 0.21875
- w_down: bfloat16 [3072, 768], P('wide', 'narrow'), may hold values from -0.109375 to 0.109375
- ln1_gain: bfloat16 [768], P(('wide', 'narrow')), may hold values from 0.25 to 1.75
- ln1_bias: bfloat16 [768], P(('wide', 'narrow')), may hold values from -3 to 3
- q_bias: bfloat16 [768], P(('wide', 'narrow')), may hold values from -3 to 3
- v_bias: bfloat16 [768], P(('wide', 'narrow')), may hold values from -3 to 3
- out_bias: bfloat16 [768], P(('wide', 'narrow')), may hold values from -3 to 3
- attn_scale: bfloat16 [768], P(('wide', 'narrow')), may hold values from 0.5 to 1.5
- ln2_gain: bfloat16 [768], P(('wide', 'narrow')), may hold values from 0.25 to 1.75
- ln2_bias: bfloat16 [768], P(('wide', 'narrow')), may hold values from -3 to 3
- up_bias: bfloat16 [3072], P(('wide', 'narrow')), may hold values from -3 to 3
- down_bias: bfloat16 [768], P(('wide', 'narrow')), may hold values from -3 to 3
- mlp_scale: bfloat16 [768], P(('wide', 'narrow')), may hold values from 0.5 to 1.5
- cotangent: bfloat16 [64, 512, 768], P(('wide', 'narrow')), may hold values from -6 to 6
Outputs:
- result_rows: bfloat16 [64, 512, 768], P(('wide', 'narrow'))
- grad_patches: float32 [64, 512, 768], P(('wide', 'narrow'))
- grad_w_qkv: float32 [768, 2304], P('wide', 'narrow')
- grad_w_out: float32 [768, 768], P('wide', 'narrow')
- grad_w_up: float32 [768, 3072], P('wide', 'narrow')
- grad_w_down: float32 [3072, 768], P('wide', 'narrow')
- grad_ln1_gain: float32 [768], P(('wide', 'narrow'))
- grad_ln1_bias: float32 [768], P(('wide', 'narrow'))
- grad_q_bias: float32 [768], P(('wide', 'narrow'))
- grad_v_bias: float32 [768], P(('wide', 'narrow'))
- grad_out_bias: float32 [768], P(('wide', 'narrow'))
- grad_attn_scale: float32 [768], P(('wide', 'narrow'))
- grad_ln2_gain: float32 [768], P(('wide', 'narrow'))
- grad_ln2_bias: float32 [768], P(('wide', 'narrow'))
- grad_up_bias: float32 [3072], P(('wide', 'narrow'))
- grad_down_bias: float32 [768], P(('wide', 'narrow'))
- grad_mlp_scale: float32 [768], P(('wide', 'narrow'))
The draws below stay inside these ranges and needn't reach their ends.
Inputs may be any that keep to these rules, and one draw needn't show every extreme that they name: `lengths`: in each pack the first 5 entries count the visible patches of its images, in order, and the last counts pad rows at its end; they sum to 512, and some entry equals 196 in every pack.
All inputs are finite; a program needn't handle non-finite values.
Results may differ from the reference program's by a relative error of at most 0.012.
The reference program's roundings to bfloat16 on the way count: a program that leaves them out, or rounds other values in their place, can miss the bound.
Values may be sent and summed in bfloat16 or wider, within the bound.
No kernel may reach another device: no remote copies, remote signals or barrier semaphores. Data moves between devices by JAX's collectives and lax.ppermute only.
A program may use at most 192 MiB of HBM per device.

```python
import math
import jax
import jax.numpy as jnp
import numpy as np
from jax import lax

D = 768
H = 12
HD = 64
FF = 3072
ROW = 512
SLOTS = 6
MOST = 196
PACKS = 64


def steps_of(key, extent, shards, smallest, top_value):
    factor_of = 1.0
    for axis_at, shards_of in shards:
        heights = jax.random.uniform(jax.random.fold_in(jax.random.fold_in(key, 6), axis_at), (shards_of,), jnp.float32, smallest / len(shards), top_value / len(shards))
        factor_of = factor_of * jnp.repeat(jnp.exp(heights), extent[axis_at] // shards_of).reshape((-1,) + (1,) * (len(extent) - 1 - axis_at))
    return factor_of


def profile(count, total, most, skew):
    loads = [(1 << 20) // math.isqrt(grade ** skew) + 1 for grade in range(2, count + 1)]
    surplus, given = total - most - (count - 1), [1] * (count - 1)
    while surplus > 0:
        movable = [i for i in range(count - 1) if given[i] < most]
        mass, left = sum([loads[i] for i in movable]), surplus
        for i in movable:
            addition = min(most - given[i], max(1, left * loads[i] // mass), surplus)
            given[i] = given[i] + addition
            surplus = surplus - addition
    return np.array([most] + given)


def ragged_sizes(rng, count, total, reach, slope):
    if count == 2:
        one = jax.random.randint(rng, (), max(1, total - reach), min(reach, total - 1) + 1)
        return jnp.stack([one, total - one])
    sizes = jnp.asarray(profile(count, total, reach, slope), jnp.int32)
    twos = (count - 1) // 2
    giver, taker = sizes[1:1 + 2 * twos:2], sizes[2:2 + 2 * twos:2]
    margin = jnp.minimum(giver - 1, reach - taker)
    shifted = jax.random.randint(jax.random.fold_in(rng, 1), (twos,), 0, 1 << 20) % (margin + 1)
    sizes = sizes.at[1:1 + 2 * twos:2].set(giver - shifted).at[2:2 + 2 * twos:2].set(taker + shifted)
    return sizes[jax.random.permutation(jax.random.fold_in(rng, 2), count)]


def gaussian(key, shape, deviation, bound, cuts=(), kind=jnp.bfloat16):
    values = jax.random.normal(key, shape, jnp.float32) * deviation
    if len(cuts) > 0:
        values = steps_of(key, shape, cuts, -0.22, 0.18) * values
    return jnp.clip(values, min=-bound, max=bound).astype(kind)


def setup_inputs(seed: int = 0) -> dict:
    arg_keys = jax.random.split(jax.random.key(seed), 19)
    return {
        "patches": gaussian(arg_keys[0], (PACKS, ROW, D), 1.0, 6.0, ((0, 32),)),
        "lengths": jax.vmap(lambda own: ragged_sizes(own, SLOTS, ROW, MOST, 1))(jax.random.split(arg_keys[1], PACKS)).reshape((PACKS, SLOTS)).astype(jnp.int32),
        "w_qkv": gaussian(arg_keys[2], (D, 3 * D), (D // 2) ** -0.5, 0.3125, ((0, 8), (1, 4))),
        "w_out": gaussian(arg_keys[3], (D, D), (D // 8) ** -0.5, 0.625, ((0, 8), (1, 4))),
        "w_up": gaussian(arg_keys[4], (D, FF), D ** -0.5, 0.21875, ((0, 8), (1, 4))),
        "w_down": gaussian(arg_keys[5], (FF, D), FF ** -0.5, 0.109375, ((0, 8), (1, 4))),
        "ln1_gain": jnp.clip(1.0 + 0.15 * jax.random.normal(arg_keys[6], (D,), jnp.float32), 0.25, 1.75).astype(jnp.bfloat16),
        "ln1_bias": gaussian(arg_keys[7], (D,), 0.5, 3.0, ((0, 32),)),
        "q_bias": gaussian(arg_keys[8], (D,), 0.5, 3.0, ((0, 32),)),
        "v_bias": gaussian(arg_keys[9], (D,), 0.5, 3.0, ((0, 32),)),
        "out_bias": gaussian(arg_keys[10], (D,), 0.5, 3.0, ((0, 32),)),
        "attn_scale": jnp.clip(0.5 + 1.0 * jax.random.uniform(arg_keys[11], (D,), jnp.float32) ** steps_of(arg_keys[11], (D,), ((0, 32),), -0.2, 0.2), 0.5, 1.5).astype(jnp.bfloat16),
        "ln2_gain": jnp.clip(1.0 + 0.15 * jax.random.normal(arg_keys[12], (D,), jnp.float32), 0.25, 1.75).astype(jnp.bfloat16),
        "ln2_bias": gaussian(arg_keys[13], (D,), 0.5, 3.0, ((0, 32),)),
        "up_bias": gaussian(arg_keys[14], (FF,), 0.5, 3.0, ((0, 32),)),
        "down_bias": gaussian(arg_keys[15], (D,), 0.5, 3.0, ((0, 32),)),
        "mlp_scale": jnp.clip(0.5 + 1.0 * jax.random.uniform(arg_keys[16], (D,), jnp.float32) ** steps_of(arg_keys[16], (D,), ((0, 32),), -0.2, 0.2), 0.5, 1.5).astype(jnp.bfloat16),
        "cotangent": gaussian(arg_keys[17], (PACKS, ROW, D), 1.0, 6.0, ((0, 32),)),
    }


@jax.custom_vjp
def low(v):
    return lax.optimization_barrier(v.astype(jnp.bfloat16)).astype(jnp.float32)

@jax.custom_vjp
def low_back(v):
    return v

def low_keep(v):
    return (low(v), None)

def low_pass(kept, grad):
    return (grad,)

def back_keep(v):
    return (v, None)

def back_low(kept, grad):
    return (low(grad),)
low.defvjp(low_keep, low_pass)
low_back.defvjp(back_keep, back_low)
LN_EPSILON = 1e-06
MASKED = -1e+30
HIGHEST = lax.Precision.HIGHEST

def layer_norm(values, scale_vec, shift_vec):
    row_mean = lax.optimization_barrier(jnp.mean(values, axis=-1, keepdims=True))
    centred = values - row_mean
    row_var = lax.optimization_barrier(jnp.mean(centred * centred, axis=-1, keepdims=True))
    return centred * lax.rsqrt(row_var + LN_EPSILON) * scale_vec + shift_vec

def segment_ids(lengths):
    boundary = jnp.cumsum(lengths, axis=1).astype(jnp.int32)
    position = jnp.arange(ROW, dtype=jnp.int32)
    segment = lax.optimization_barrier(jnp.sum((position[None, :, None] >= boundary[:, None, :]).astype(jnp.int32), axis=2)).astype(jnp.int32)
    live_rows = position[None, :] < boundary[:, SLOTS - 2][:, None]
    segment = jnp.where(live_rows, segment, SLOTS + position[None, :])
    return (segment, live_rows)

def mix_block(patch_rows, segment, live_rows, params):
    w_qkv, w_out, w_up, w_down, ln1_gain, ln1_bias, q_bias, v_bias, out_bias, attn_scale, ln2_gain, ln2_bias, up_bias, down_bias, mlp_scale = params
    group_size, row_count, model_width = patch_rows.shape
    normed = low(layer_norm(patch_rows, ln1_gain, ln1_bias))
    projected = jnp.einsum('grd,df->grf', normed, w_qkv, precision=HIGHEST)
    query_rows = low(low_back((projected[..., :model_width] + q_bias) * 0.125))
    key_rows = low(low_back(projected[..., model_width:2 * model_width]))
    value_rows = low(low_back(projected[..., 2 * model_width:] + v_bias))
    query_heads = query_rows.reshape(group_size, row_count, H, HD)
    key_heads = key_rows.reshape(group_size, row_count, H, HD)
    value_heads = value_rows.reshape(group_size, row_count, H, HD)
    scores = low_back(jnp.einsum('gqhe,gkhe->ghqk', query_heads, key_heads, precision=HIGHEST))
    allowed = (segment[:, :, None] == segment[:, None, :])[:, None]
    scores = jnp.where(allowed, scores, MASKED)
    row_top = lax.optimization_barrier(jnp.max(scores, axis=-1, keepdims=True))
    exp_scores = jnp.exp(scores - row_top)
    soft_probs = exp_scores / lax.optimization_barrier(jnp.sum(exp_scores, axis=-1, keepdims=True))
    attended = jnp.einsum('ghqk,gkhe->gqhe', low(soft_probs), value_heads, precision=HIGHEST)
    attended = low(low_back(attended.reshape(group_size, row_count, model_width)))
    branch = low_back(jnp.einsum('grd,df->grf', attended, w_out, precision=HIGHEST) + out_bias)
    middle = patch_rows + attn_scale * branch
    normed_second = low(layer_norm(middle, ln2_gain, ln2_bias))
    up_pre = low_back(jnp.einsum('grd,df->grf', normed_second, w_up, precision=HIGHEST) + up_bias)
    activated = low(jax.nn.gelu(up_pre, approximate=False))
    down_out = low_back(jnp.einsum('grf,fd->grd', activated, w_down, precision=HIGHEST) + down_bias)
    result_rows = middle + mlp_scale * down_out
    return jnp.where(live_rows[..., None], result_rows, 0.0)

def reference(patches, lengths, w_qkv, w_out, w_up, w_down, ln1_gain, ln1_bias, q_bias, v_bias, out_bias, attn_scale, ln2_gain, ln2_bias, up_bias, down_bias, mlp_scale, cotangent):
    segment, live_rows = segment_ids(lengths)
    params = tuple((weight_arg.astype(jnp.float32) for weight_arg in (w_qkv, w_out, w_up, w_down, ln1_gain, ln1_bias, q_bias, v_bias, out_bias, attn_scale, ln2_gain, ln2_bias, up_bias, down_bias, mlp_scale)))
    group_size = math.gcd(PACKS, 8)
    group_count = PACKS // group_size
    segment_groups = segment.reshape(group_count, group_size, ROW)
    live_groups = live_rows.reshape(group_count, group_size, ROW)

    def forward(inputs, weight_set):

        def one_group(pieces):
            return mix_block(pieces[0], pieces[1], pieces[2], weight_set)
        stacked = inputs.reshape(group_count, group_size, ROW, D)
        mixed_rows = lax.map(jax.checkpoint(one_group), (stacked, segment_groups, live_groups))
        return mixed_rows.reshape(PACKS, ROW, D)
    result_rows, pullback = jax.vjp(forward, patches.astype(jnp.float32), params)
    grad_inputs, grad_params = pullback(cotangent.astype(jnp.float32))
    return (result_rows.astype(jnp.bfloat16), grad_inputs, grad_params[0], grad_params[1], grad_params[2], grad_params[3], grad_params[4], grad_params[5], grad_params[6], grad_params[7], grad_params[8], grad_params[9], grad_params[10], grad_params[11], grad_params[12], grad_params[13], grad_params[14])
```

```python
import jax
import jax.numpy as jnp
from jax import lax
from jax.sharding import PartitionSpec as P

HD = 64


LN_EPSILON = 1e-06
MASKED = -1e30


def layer_norm(values, scale_vec, shift_vec):
    row_mean = jnp.mean(values, axis=-1, keepdims=True)
    centred = values - row_mean
    row_var = jnp.mean(centred * centred, axis=-1, keepdims=True)
    return centred * lax.rsqrt(row_var + LN_EPSILON) * scale_vec + shift_vec


def gelu_exact(values):
    return jax.nn.gelu(values, approximate=False)


def segment_ids(lengths, row_count):
    slot_count = lengths.shape[1]
    boundary = jnp.cumsum(lengths, axis=1)
    position = jnp.arange(row_count, dtype=jnp.int32)
    segment = jnp.sum((position[None, :, None] >= boundary[:, None, :]).astype(jnp.int32), axis=2)
    live_rows = position[None, :] < boundary[:, slot_count - 2][:, None]
    segment = jnp.where(live_rows, segment, slot_count + position[None, :])
    return (segment, live_rows)


def exchange(value, axis_name, partner):
    size = lax.axis_size(axis_name)
    return lax.ppermute(value, axis_name, [(i, partner(i) % size) for i in range(size)])


def cross(value, bit):
    return exchange(value, "wide", lambda i: i ^ (1 << bit))


def shift(value, step):
    return exchange(value, "narrow", lambda i: i + step)


def wide_bits():
    return lax.axis_size("wide").bit_length() - 1


def by_origin(pieces):
    size = len(pieces)
    backward = jnp.stack(pieces[::-1])
    twice = jnp.concatenate([backward, backward])
    return lax.dynamic_slice_in_dim(twice, size - 1 - lax.axis_index("narrow"), size)


def flip_own(stacked):
    here = lax.axis_index("wide")
    size = stacked.shape[0]
    for bit in range(size.bit_length() - 1):
        halves = stacked.reshape((size >> (bit + 1), 2, 1 << bit) + stacked.shape[1:])
        halves = jnp.where((here >> bit) & 1, halves[:, ::-1], halves)
        stacked = halves.reshape(stacked.shape)
    return stacked


def spread_wide(block):
    rows = block.shape[0]
    half = rows // 32 * 16
    held = block[None]
    for bit in range(3, wide_bits()):
        held = jnp.concatenate([held, cross(held, bit)])
    near = cross(held, 1)
    far = cross(held, 2)
    corner_one = cross(near[:, :half], 2)
    corner_two = cross(far[:, half:], 1)
    mine = [held, near, far, corner_one, corner_two]
    theirs = [cross(piece, 0) for piece in mine]
    quads = []
    for at in range(3):
        quads.append(jnp.stack([mine[at], theirs[at]], axis=1))
    quads.append(
        jnp.stack(
            [
                jnp.concatenate([mine[3], mine[4]], axis=1),
                jnp.concatenate([theirs[3], theirs[4]], axis=1),
            ],
            axis=1,
        )
    )
    stacked = jnp.stack(quads, axis=1).reshape((-1,) + block.shape)
    return flip_own(stacked)


def gather_narrow(shard):
    size = lax.axis_size("narrow")
    return by_origin([shard] + [shift(shard, step) for step in range(1, size)])


def side_by_side(stacked):
    return jnp.concatenate([stacked[i] for i in range(stacked.shape[0])], axis=1)


VECTORS = 11


def collect(w_qkv, w_out, w_up, w_down, *vectors):
    narrow_size = lax.axis_size("narrow")
    wide_size = lax.axis_size("wide")
    width = w_up.shape[1]
    short = w_up.shape[0]
    packed = jnp.concatenate(vectors)
    row = jnp.pad(packed[None], ((0, 15), (0, width - packed.shape[0])))
    one = jnp.concatenate([jnp.concatenate([w_qkv, w_out], axis=1), row])
    down = jnp.concatenate(jnp.split(w_down, narrow_size, axis=0), axis=1)
    one = gather_narrow(one)
    two = gather_narrow(w_up)
    three = gather_narrow(down)
    qkv = side_by_side(one[:, :short, : w_qkv.shape[1]])
    out = side_by_side(one[:, :short, w_qkv.shape[1] :])
    rows = jnp.pad(one[:, short], ((0, 16 - narrow_size), (0, 0)))
    one = jnp.concatenate([*jnp.split(qkv, 3, axis=1), out, rows])
    two = two.reshape(-1, width)
    quarter = w_down.shape[1]
    three = jnp.concatenate(
        [side_by_side(three[:, :, i * quarter : (i + 1) * quarter]) for i in range(narrow_size)]
    )
    one = spread_wide(one)
    two = spread_wide(two)
    three = spread_wide(three)
    square = one[:, : 4 * short].reshape(wide_size, 4, short, width)
    q, k, v, out = (square[:, i].reshape(-1, width) for i in range(4))
    qkv_full = jnp.concatenate([q, k, v], axis=1)
    up = two.reshape(wide_size, narrow_size, short, width).transpose(0, 2, 1, 3)
    up_full = up.reshape(-1, narrow_size * width)
    down_full = three.reshape(-1, width)
    rows = one[:, 4 * short : 4 * short + narrow_size, : packed.shape[0]]
    full, at = [], 0
    for vector in vectors:
        full.append(rows[:, :, at : at + vector.shape[0]].reshape(-1))
        at += vector.shape[0]
    return (qkv_full, out, up_full, down_full, *full)


def add_low(left, right):
    return (left.astype(jnp.float32) + right.astype(jnp.float32)).astype(left.dtype)


def meet_wide(stacked):
    stacked = flip_own(stacked)
    rows = stacked.shape[1]
    half = rows // 32 * 16
    pieces = stacked.reshape((-1, 4, 2) + stacked.shape[1:])
    held = add_low(pieces[:, :, 0], cross(pieces[:, :, 1], 0))
    own, near, far, corner = (held[:, i] for i in range(4))
    corner_one = cross(corner[:, :half], 1)
    corner_two = cross(corner[:, half:], 2)
    far = jnp.concatenate([add_low(far[:, :half], corner_one), far[:, half:]], axis=1)
    near = jnp.concatenate([near[:, :half], add_low(near[:, half:], corner_two)], axis=1)
    near = cross(near, 1).astype(jnp.float32)
    far = cross(far, 2).astype(jnp.float32)
    held = (own.astype(jnp.float32) + near + far).astype(stacked.dtype)
    for bit in reversed(range(3, wide_bits())):
        count = held.shape[0] // 2
        held = add_low(held[:count], cross(held[count:], bit))
    return held[0]


def meet_narrow(stacked):
    size = stacked.shape[0]
    here = lax.axis_index("narrow")
    total = lax.dynamic_index_in_dim(stacked, here, keepdims=False).astype(jnp.float32)
    for step in range(1, size):
        block = lax.dynamic_index_in_dim(stacked, lax.rem(here + step, size), keepdims=False)
        total = total + shift(block, step).astype(jnp.float32)
    return total


def reduce_grads(grad_set):
    wide_size = lax.axis_size("wide")
    narrow_size = lax.axis_size("narrow")
    qkv, out, up, down = (grad.astype(jnp.bfloat16) for grad in grad_set[:4])
    width = out.shape[0]
    short = width // wide_size
    three = meet_wide(down.reshape(wide_size, -1, width))
    three = meet_narrow(three.reshape(-1, narrow_size, width // narrow_size).transpose(1, 0, 2))
    up = up.reshape(wide_size, short, narrow_size, width).transpose(0, 2, 1, 3)
    two = meet_wide(up.reshape(wide_size, -1, width))
    two = meet_narrow(two.reshape(narrow_size, short, width))
    one = jnp.concatenate(
        [
            piece.reshape(wide_size, short, width)
            for piece in (*jnp.split(qkv, 3, axis=1), out)
        ],
        axis=1,
    )
    one = meet_wide(one)
    one_qkv = jnp.concatenate([one[i * short : (i + 1) * short] for i in range(3)], axis=1)
    one_out = one[3 * short :]
    one = jnp.concatenate(
        [
            one_qkv.reshape(short, narrow_size, -1).transpose(1, 0, 2),
            one_out.reshape(short, narrow_size, -1).transpose(1, 0, 2),
        ],
        axis=2,
    )
    one = meet_narrow(one)
    part = qkv.shape[1] // narrow_size
    sums = jnp.concatenate(
        [vector.reshape(wide_size, narrow_size, -1) for vector in grad_set[4:]], axis=2
    )
    sums = meet_narrow(meet_wide(sums).reshape(narrow_size, 1, -1))[0]
    vectors, at = [], 0
    for vector in grad_set[4:]:
        count = vector.shape[0] // (wide_size * narrow_size)
        vectors.append(sums[at : at + count])
        at += count
    return (one[:, :part], one[:, part:], two, three, *vectors)


def pack_scores(query_pack, key_pack, segment_pack):
    row_count = query_pack.shape[0]
    query_heads = query_pack.reshape(row_count, -1, HD)
    key_heads = key_pack.reshape(row_count, -1, HD)
    scores = jnp.einsum("qhe,khe->hqk", query_heads, key_heads, preferred_element_type=jnp.float32)
    allowed = segment_pack[:, None] == segment_pack[None, :]
    return jnp.where(allowed[None], scores, MASKED)


def attend(pieces):
    query_pack, key_pack, value_pack, segment_pack = pieces
    row_count, model_width = query_pack.shape
    scores = pack_scores(query_pack, key_pack, segment_pack)
    row_top = jnp.max(scores, axis=-1, keepdims=True)
    exp_scores = jnp.exp(scores - row_top)
    row_total = jnp.sum(exp_scores, axis=-1, keepdims=True)
    soft_probs = (exp_scores / row_total).astype(jnp.bfloat16)
    value_heads = value_pack.reshape(row_count, -1, HD)
    mixed_heads = jnp.einsum(
        "hqk,khe->qhe", soft_probs, value_heads, preferred_element_type=jnp.float32
    )
    log_total = row_top[..., 0] + jnp.log(row_total[..., 0])
    return (mixed_heads.reshape(row_count, model_width).astype(jnp.bfloat16), log_total)


def attend_back(pieces):
    query_pack, key_pack, value_pack, segment_pack, log_pack, grad_pack = pieces
    row_count, model_width = query_pack.shape
    scores = pack_scores(query_pack, key_pack, segment_pack)
    soft_probs = jnp.exp(scores - log_pack[..., None])
    weights = soft_probs.astype(jnp.bfloat16)
    query_heads = query_pack.reshape(row_count, -1, HD)
    key_heads = key_pack.reshape(row_count, -1, HD)
    value_heads = value_pack.reshape(row_count, -1, HD)
    grad_heads = grad_pack.reshape(row_count, -1, HD)
    grad_value = jnp.einsum("hqk,qhe->khe", weights, grad_heads, preferred_element_type=jnp.float32)
    grad_probs = jnp.einsum(
        "qhe,khe->hqk", grad_heads, value_heads, preferred_element_type=jnp.float32
    )
    centre = jnp.sum(grad_probs * soft_probs, axis=-1, keepdims=True)
    grad_scores = (soft_probs * (grad_probs - centre)).astype(jnp.bfloat16)
    grad_query = jnp.einsum(
        "hqk,khe->qhe", grad_scores, key_heads, preferred_element_type=jnp.float32
    )
    grad_key = jnp.einsum(
        "hqk,qhe->khe", grad_scores, query_heads, preferred_element_type=jnp.float32
    )
    grad_query = grad_query.reshape(row_count, model_width).astype(jnp.bfloat16) * 0.125
    grad_key = grad_key.reshape(row_count, model_width).astype(jnp.bfloat16)
    grad_value = grad_value.reshape(row_count, model_width).astype(jnp.bfloat16)
    return jnp.concatenate([grad_query, grad_key, grad_value], axis=-1)


def shards(
    patches,
    lengths,
    w_qkv,
    w_out,
    w_up,
    w_down,
    ln1_gain,
    ln1_bias,
    q_bias,
    v_bias,
    out_bias,
    attn_scale,
    ln2_gain,
    ln2_bias,
    up_bias,
    down_bias,
    mlp_scale,
    cotangent,
):
    gathered = collect(
        w_qkv,
        w_out,
        w_up,
        w_down,
        ln1_gain,
        ln1_bias,
        q_bias,
        v_bias,
        out_bias,
        attn_scale,
        ln2_gain,
        ln2_bias,
        up_bias,
        down_bias,
        mlp_scale,
    )
    qkv_full, out_full, up_full, down_full = gathered[:4]
    (
        gain_first,
        shift_first,
        query_bias,
        value_bias,
        branch_bias,
        attn_layer,
        gain_second,
        shift_second,
        hidden_bias,
        output_bias,
        mlp_layer,
    ) = tuple((vector_piece.astype(jnp.float32) for vector_piece in gathered[4:]))
    pack_count, row_count, model_width = patches.shape
    segment, live_rows = segment_ids(lengths, row_count)
    live_mask = live_rows[..., None]
    inputs = patches.astype(jnp.float32)
    normed_full, ln1_pull = jax.vjp(layer_norm, inputs, gain_first, shift_first)
    normed = normed_full.astype(jnp.bfloat16)
    projected = jnp.einsum("prd,df->prf", normed, qkv_full, preferred_element_type=jnp.float32)
    query_rows = ((projected[..., :model_width] + query_bias) * 0.125).astype(jnp.bfloat16)
    key_rows = projected[..., model_width : 2 * model_width].astype(jnp.bfloat16)
    value_rows = (projected[..., 2 * model_width :] + value_bias).astype(jnp.bfloat16)
    attended, log_total = lax.map(attend, (query_rows, key_rows, value_rows, segment))
    branch = (
        jnp.einsum("prd,df->prf", attended, out_full, preferred_element_type=jnp.float32)
        + branch_bias
    )
    middle = inputs + attn_layer * branch
    normed_two_full, ln2_pull = jax.vjp(layer_norm, middle, gain_second, shift_second)
    normed_two = normed_two_full.astype(jnp.bfloat16)
    up_pre = (
        jnp.einsum("prd,df->prf", normed_two, up_full, preferred_element_type=jnp.float32)
        + hidden_bias
    )
    activated_full, gelu_pull = jax.vjp(gelu_exact, up_pre)
    activated = activated_full.astype(jnp.bfloat16)
    down_out = (
        jnp.einsum("prf,fd->prd", activated, down_full, preferred_element_type=jnp.float32)
        + output_bias
    )
    result_rows = jnp.where(live_mask, middle + mlp_layer * down_out, 0.0).astype(jnp.bfloat16)
    qkv_back, out_back, up_back, down_back = gathered[:4]
    grad_out = jnp.where(live_mask, cotangent.astype(jnp.float32), 0.0)
    grad_mlp_layer = jnp.sum(grad_out * down_out, axis=(0, 1))
    grad_down = (grad_out * mlp_layer).astype(jnp.bfloat16)
    grad_output_bias = jnp.sum(grad_down.astype(jnp.float32), axis=(0, 1))
    grad_w_down = jnp.einsum(
        "prf,prd->fd", activated, grad_down, preferred_element_type=jnp.float32
    )
    grad_activated = jnp.einsum(
        "prd,fd->prf", grad_down, down_back, preferred_element_type=jnp.float32
    )
    grad_up = gelu_pull(grad_activated)[0].astype(jnp.bfloat16)
    grad_hidden_bias = jnp.sum(grad_up.astype(jnp.float32), axis=(0, 1))
    grad_w_up = jnp.einsum("prd,prf->df", normed_two, grad_up, preferred_element_type=jnp.float32)
    grad_normed_two = jnp.einsum(
        "prf,df->prd", grad_up, up_back, preferred_element_type=jnp.float32
    )
    grad_middle_norm, grad_gain_second, grad_shift_second = ln2_pull(grad_normed_two)
    grad_middle = grad_out + grad_middle_norm
    grad_attn_layer = jnp.sum(grad_middle * branch, axis=(0, 1))
    grad_branch = (grad_middle * attn_layer).astype(jnp.bfloat16)
    grad_branch_bias = jnp.sum(grad_branch.astype(jnp.float32), axis=(0, 1))
    grad_w_out = jnp.einsum(
        "prd,prf->df", attended, grad_branch, preferred_element_type=jnp.float32
    )
    grad_attended = jnp.einsum(
        "prf,df->prd", grad_branch, out_back, preferred_element_type=jnp.float32
    ).astype(jnp.bfloat16)
    grad_projected = lax.map(
        attend_back, (query_rows, key_rows, value_rows, segment, log_total, grad_attended)
    )
    grad_w_qkv = jnp.einsum(
        "prd,prf->df", normed, grad_projected, preferred_element_type=jnp.float32
    )
    grad_query_bias = jnp.sum(grad_projected[..., :model_width].astype(jnp.float32), axis=(0, 1))
    grad_value_bias = jnp.sum(
        grad_projected[..., 2 * model_width :].astype(jnp.float32), axis=(0, 1)
    )
    grad_normed = jnp.einsum(
        "prf,df->prd", grad_projected, qkv_back, preferred_element_type=jnp.float32
    )
    grad_input_norm, grad_gain_first, grad_shift_first = ln1_pull(grad_normed)
    grad_inputs = grad_middle + grad_input_norm
    reduced = reduce_grads(
        (
            grad_w_qkv,
            grad_w_out,
            grad_w_up,
            grad_w_down,
            grad_gain_first,
            grad_shift_first,
            grad_query_bias,
            grad_value_bias,
            grad_branch_bias,
            grad_attn_layer,
            grad_gain_second,
            grad_shift_second,
            grad_hidden_bias,
            grad_output_bias,
            grad_mlp_layer,
        )
    )
    return (
        result_rows,
        grad_inputs,
        reduced[0],
        reduced[1],
        reduced[2],
        reduced[3],
        reduced[4],
        reduced[5],
        reduced[6],
        reduced[7],
        reduced[8],
        reduced[9],
        reduced[10],
        reduced[11],
        reduced[12],
        reduced[13],
        reduced[14],
    )


def solution(mesh):
    return jax.shard_map(
        shards,
        mesh=mesh,
        in_specs=(
            P(("wide", "narrow"), None, None),
            P(("wide", "narrow"), None),
            P("wide", "narrow"),
            P("wide", "narrow"),
            P("wide", "narrow"),
            P("wide", "narrow"),
            P(("wide", "narrow")),
            P(("wide", "narrow")),
            P(("wide", "narrow")),
            P(("wide", "narrow")),
            P(("wide", "narrow")),
            P(("wide", "narrow")),
            P(("wide", "narrow")),
            P(("wide", "narrow")),
            P(("wide", "narrow")),
            P(("wide", "narrow")),
            P(("wide", "narrow")),
            P(("wide", "narrow"), None, None),
        ),
        out_specs=(
            P(("wide", "narrow"), None, None),
            P(("wide", "narrow"), None, None),
            P("wide", "narrow"),
            P("wide", "narrow"),
            P("wide", "narrow"),
            P("wide", "narrow"),
            P(("wide", "narrow")),
            P(("wide", "narrow")),
            P(("wide", "narrow")),
            P(("wide", "narrow")),
            P(("wide", "narrow")),
            P(("wide", "narrow")),
            P(("wide", "narrow")),
            P(("wide", "narrow")),
            P(("wide", "narrow")),
            P(("wide", "narrow")),
            P(("wide", "narrow")),
        ),
        check_vma=False,
    )
```

```python
import functools
import math

import jax
import jax.numpy as jnp
from jax import lax
from jax.experimental import pallas as pl
from jax.experimental.pallas import tpu as pltpu
from jax.sharding import PartitionSpec as P

HD = 64
LN_EPSILON = 1e-06
MASKED = -1e30
TILE = 256
F32 = jnp.float32
BF16 = jnp.bfloat16
MIB = 1 << 20


def exchange(value, axis_name, partner):
    size = lax.axis_size(axis_name)
    return lax.ppermute(value, axis_name, [(i, partner(i) % size) for i in range(size)])


def cross(value, bit):
    return exchange(value, "wide", lambda i: i ^ (1 << bit))


def shift(value, step):
    return exchange(value, "narrow", lambda i: i + step)


def wide_bits():
    return lax.axis_size("wide").bit_length() - 1


def by_origin(pieces):
    size = len(pieces)
    backward = jnp.stack(pieces[::-1])
    twice = jnp.concatenate([backward, backward])
    return lax.dynamic_slice_in_dim(twice, size - 1 - lax.axis_index("narrow"), size)


def flip_own(stacked):
    here = lax.axis_index("wide")
    size = stacked.shape[0]
    for bit in range(size.bit_length() - 1):
        halves = stacked.reshape((size >> (bit + 1), 2, 1 << bit) + stacked.shape[1:])
        halves = jnp.where((here >> bit) & 1, halves[:, ::-1], halves)
        stacked = halves.reshape(stacked.shape)
    return stacked


def after(value, *others):
    return lax.optimization_barrier((value, others))[0]


def beside(run, value, sends, moves):
    value, sends = lax.optimization_barrier((value, sends))
    moved = [move(send) for move, send in zip(moves, sends, strict=True)]
    return lax.optimization_barrier((run(value), moved))


def planes():
    return [lambda v: cross(v, 1), lambda v: cross(v, 2)]


def corners():
    return [lambda v: cross(v, 2), lambda v: cross(v, 1)]


def shifts(layers):
    return [lambda v, step=step: shift(v, step) for step in range(1, layers)]


def double(block):
    held = block[None]
    for bit in range(3, wide_bits()):
        held = jnp.concatenate([held, cross(held, bit)])
    return held


def side_by_side(stacked):
    return jnp.concatenate([stacked[i] for i in range(stacked.shape[0])], axis=1)


def direct():
    return lax.axis_size("wide") == 8


def matrices(planes, cores, parts):
    unit = planes[0].shape[1] // parts
    if not direct():
        other = [*jnp.split(cores[0], 3), cores[1]]
        stacked = jnp.stack([jnp.stack(pair, axis=1) for pair in zip(planes, other)], axis=1)
        stacked = flip_own(stacked.reshape((-1,) + planes[0].shape[1:]))
        stacked = stacked.reshape(stacked.shape[0], parts, unit, -1)
        arrays = [stacked[:, m].reshape(-1, stacked.shape[3]) for m in range(parts)]
        return arrays, [[(m, 0, 0, None, unit)] for m in range(parts)]
    spots = [(0, 0, 0), (1, 0, 2), (2, 0, 4), (3, 0, 6), (4, 0, 1), (4, 1, 3), (4, 2, 5), (5, 0, 7)]
    plans = [[(at, index, m * unit, rel, unit) for at, index, rel in spots] for m in range(parts)]
    return [*planes, *cores], plans


def copies(place, refs, plan, target, sems, first):
    made = []
    for at, index, row, rel, unit in plan:
        sem = sems.at[first + len(made)]
        if rel is None:
            made.append(pltpu.make_async_copy(refs[at], target, sem))
        else:
            start = pl.multiple_of((place ^ rel) * unit, 16)
            source = refs[at].at[index, pl.ds(row, unit)]
            made.append(pltpu.make_async_copy(source, target.at[pl.ds(start, unit)], sem))
    return made


def start_all(made):
    for copy in made:
        copy.start()


def wait_all(made):
    for copy in made:
        copy.wait()


def dot(left, right):
    return lax.dot_general(left, right, (((1,), (0,)), ((), ())), preferred_element_type=F32)


def dot_nt(left, right):
    return lax.dot_general(left, right, (((1,), (1,)), ((), ())), preferred_element_type=F32)


def centred_rows(values):
    row_mean = jnp.mean(values, axis=-1, keepdims=True)
    centred = values - row_mean
    row_var = jnp.mean(centred * centred, axis=-1, keepdims=True)
    inverse = lax.rsqrt(row_var + LN_EPSILON)
    return centred * inverse, inverse


def norm_back(grad, unit_rows, inverse, gain):
    scaled = grad * gain
    mean_one = jnp.mean(scaled, axis=-1, keepdims=True)
    mean_two = jnp.mean(scaled * unit_rows, axis=-1, keepdims=True)
    return (scaled - mean_one - unit_rows * mean_two) * inverse


def row_sum(values):
    return jnp.sum(values, axis=0, keepdims=True)


def gelu_pair(values):
    size = jnp.abs(values) * math.sqrt(0.5)
    bell = jnp.exp(values * values * -0.5)
    step = 1.0 / (1.0 + 0.3275911 * size)
    series = step * (-1.453152027 + step * 1.061405429) + 1.421413741
    series = step * (0.254829592 + step * (-0.284496736 + step * series))
    tail = 0.5 * series * bell
    share = jnp.where(values >= 0, 1.0 - tail, tail)
    return values * share, share + values * bell * (1.0 / math.sqrt(2.0 * math.pi))


ANY = pl.BlockSpec(memory_space=pl.ANY)
SMEM = pl.BlockSpec(memory_space=pltpu.SMEM)


def whole(shape):
    return pl.BlockSpec(shape, lambda *_: (0,) * len(shape))


def tile_of(columns):
    return pl.BlockSpec((TILE, columns), lambda i: (i, 0))


def cost(flops, moved, exps=0):
    return pl.CostEstimate(flops=flops, bytes_accessed=moved, transcendentals=exps)


def params(mib, dims=1):
    return pltpu.CompilerParams(
        vmem_limit_bytes=mib * MIB, dimension_semantics=("arbitrary",) * dims
    )


LN1_G, LN1_B, Q_B, V_B, OUT_B, ATTN_S, LN2_G, LN2_B, DOWN_B, MLP_S, UP_B = range(11)


def vector(table, row):
    return table[row : row + 1, :]


def project_kernel(plans, place, rows, table, *refs):
    count = len(refs) - 4 - 2
    sources, (normed, query, key, value, weights, sems) = refs[:count], refs[count:]
    made, first = [], 0
    for m in range(3):
        made.append(copies(place[0], sources, plans[m], weights.at[m], sems, first))
        first += len(plans[m])

    @pl.when(pl.program_id(0) == 0)
    def _():
        for group in made:
            start_all(group)

    unit_rows, _ = centred_rows(rows[...].astype(F32))
    low = (unit_rows * vector(table, LN1_G) + vector(table, LN1_B)).astype(BF16)
    normed[...] = low

    @pl.when(pl.program_id(0) == 0)
    def _():
        for group in made:
            wait_all(group)

    query[...] = ((dot(low, weights[0]) + vector(table, Q_B)) * 0.125).astype(BF16)
    key[...] = dot(low, weights[1]).astype(BF16)
    value[...] = (dot(low, weights[2]) + vector(table, V_B)).astype(BF16)


def project(place, rows, table, group):
    arrays, plans = group
    count, width = rows.shape
    return pl.pallas_call(
        functools.partial(project_kernel, plans),
        grid=(count // TILE,),
        in_specs=[SMEM, tile_of(width), whole(table.shape)] + [ANY] * len(arrays),
        out_specs=[tile_of(width)] * 4,
        out_shape=[jax.ShapeDtypeStruct(rows.shape, BF16)] * 4,
        scratch_shapes=[
            pltpu.VMEM((3, width, width), BF16),
            pltpu.SemaphoreType.DMA((sum(len(p) for p in plans[:3]),)),
        ],
        compiler_params=params(60),
        cost_estimate=cost(6 * count * width * width, 14 * count * width),
        name="project",
    )(place, rows, table, *arrays)


def segments(lengths, pack, position):
    end, segment = 0, jnp.zeros_like(position)
    for slot in range(lengths.shape[1] - 1):
        end = end + lengths[pack, slot]
        segment = segment + (position >= end).astype(jnp.int32)
    return jnp.where(position < end, segment, lengths.shape[1] + position)


def same_segment(lengths, pack, rows):
    down = lax.broadcasted_iota(jnp.int32, (rows, 128), 0)
    along = lax.broadcasted_iota(jnp.int32, (1, rows), 1)
    column = segments(lengths, pack, down)
    row = segments(lengths, pack, along)
    return jnp.concatenate([column] * (rows // 128), axis=1) == row


def head_lanes(shape, head):
    lane = lax.broadcasted_iota(jnp.int32, shape, 1)
    return (lane < HD) if head == 0 else (lane >= HD)


def only(values, head):
    return jnp.where(head_lanes(values.shape, head), values, jnp.zeros_like(values))


def attend_kernel(pack, lengths, query, key, value, *refs):
    attended, log_total = refs[-2:]
    rows = query.shape[0]
    same = same_segment(lengths, pack, rows)
    flat = jnp.transpose(value[...].astype(F32)).astype(BF16)
    mixed = []
    for head in range(2):
        scores = dot_nt(key[...], only(query[...], head))
        scores = jnp.where(same, scores, MASKED)
        top = jnp.max(scores, axis=0, keepdims=True)
        powers = jnp.exp(scores - top)
        total = jnp.sum(powers, axis=0, keepdims=True)
        weights = (powers * (1.0 / total)).astype(BF16)
        mixed.append(dot(flat[head * HD : (head + 1) * HD], weights))
        log_total[0, 0, head : head + 1, :] = top + jnp.log(total)
    attended[...] = jnp.transpose(jnp.concatenate(mixed, axis=0)).astype(BF16)


def pair_block(rows, pack):
    return pl.BlockSpec((rows, 2 * HD), lambda h: (pack, h))


def log_block(rows, pack):
    return pl.BlockSpec((1, 1, 2, rows), lambda h: (pack, h, 0, 0))


def attend(lengths, query, key, value, pack, earlier=()):
    packs = lengths.shape[0]
    count, width = query.shape
    rows, pairs = count // packs, width // (2 * HD)
    return pl.pallas_call(
        functools.partial(attend_kernel, pack),
        grid=(pairs,),
        in_specs=[SMEM] + [pair_block(rows, pack)] * 3 + [ANY] * len(earlier),
        out_specs=[pair_block(rows, pack), log_block(rows, pack)],
        out_shape=[
            jax.ShapeDtypeStruct(query.shape, BF16),
            jax.ShapeDtypeStruct((packs, pairs, 2, rows), F32),
        ],
        input_output_aliases={4 + i: i for i in range(len(earlier))},
        compiler_params=params(60),
        cost_estimate=cost(16 * rows * rows * width, 8 * rows * width, 12 * rows * rows),
        name="attend",
    )(lengths, query, key, value, *earlier)


def attend_back_kernel(pack, lengths, query, key, value, grad, log_total, *refs):
    grad_q, grad_k, grad_v = refs[-3:]
    rows = query.shape[0]
    same = same_segment(lengths, pack, rows)
    flat_key = jnp.transpose(key[...].astype(F32)).astype(BF16)
    by_query, by_key, by_value = [], [], []
    for head in range(2):
        scores = dot_nt(key[...], only(query[...], head))
        probs = jnp.exp(scores - log_total[0, 0, head : head + 1, :])
        probs = jnp.where(same, probs, 0.0)
        by_value.append(dot(probs.astype(BF16), grad[...]))
        grad_probs = dot_nt(value[...], only(grad[...], head))
        centre = jnp.sum(grad_probs * probs, axis=0, keepdims=True)
        grad_scores = (probs * (grad_probs - centre)).astype(BF16)
        by_key.append(dot(grad_scores, query[...]))
        by_query.append(dot(flat_key[head * HD : (head + 1) * HD], grad_scores))
    lanes = head_lanes(by_key[0].shape, 0)
    grad_k[...] = jnp.where(lanes, by_key[0], by_key[1]).astype(BF16)
    grad_v[...] = jnp.where(lanes, by_value[0], by_value[1]).astype(BF16)
    grad_q[...] = jnp.transpose(jnp.concatenate(by_query, axis=0)).astype(BF16) * 0.125


def attend_back(lengths, query, key, value, grad, log_total, pack, earlier=()):
    packs = lengths.shape[0]
    count, width = query.shape
    rows, pairs = count // packs, width // (2 * HD)
    return pl.pallas_call(
        functools.partial(attend_back_kernel, pack),
        grid=(pairs,),
        in_specs=[SMEM]
        + [pair_block(rows, pack)] * 4
        + [log_block(rows, pack)]
        + [ANY] * len(earlier),
        out_specs=[pair_block(rows, pack)] * 3,
        out_shape=[jax.ShapeDtypeStruct(query.shape, BF16)] * 3,
        input_output_aliases={6 + i: i for i in range(len(earlier))},
        compiler_params=params(60),
        cost_estimate=cost(40 * rows * rows * width, 14 * rows * width, 12 * rows * rows),
        name="attend_back",
    )(lengths, query, key, value, grad, log_total, *earlier)


def live_rows(lengths, shape):
    tiles = pl.num_programs(0) // lengths.shape[0]
    step = pl.program_id(0)
    pack = step // tiles
    end = 0
    for slot in range(lengths.shape[1] - 1):
        end = end + lengths[pack, slot]
    position = lax.broadcasted_iota(jnp.int32, shape, 0) + (step - pack * tiles) * shape[0]
    return position < end


def hidden_kernel(plans, size, place, lengths, rows, mixed, cotangent, table, *refs):
    two, refs = refs[:size], refs[size:]
    *up_plans, out_plan = plans
    branch_out, normed, active, slope, grad_down, out_w, up_w, sems = refs
    made = [copies(place[0], two, out_plan, out_w, sems, 0)]
    first = len(out_plan)
    for m, plan in enumerate(up_plans):
        made.append(copies(place[0], two, plan, up_w.at[m], sems, first))
        first += len(plan)

    @pl.when(pl.program_id(0) == 0)
    def _():
        for group in made:
            start_all(group)
        wait_all(made[0])

    branch = dot(mixed[...], out_w[...]) + vector(table, OUT_B)
    branch_out[...] = branch
    middle = rows[...].astype(F32) + vector(table, ATTN_S) * branch
    unit_rows, _ = centred_rows(middle)
    low = (unit_rows * vector(table, LN2_G) + vector(table, LN2_B)).astype(BF16)
    normed[...] = low
    live = live_rows(lengths, cotangent.shape)
    grad_out = jnp.where(live, cotangent[...].astype(F32), 0.0)
    grad_down[...] = (grad_out * vector(table, MLP_S)).astype(BF16)

    @pl.when(pl.program_id(0) == 0)
    def _():
        for group in made[1:]:
            wait_all(group)

    width = low.shape[1]
    for m in range(len(up_plans)):
        part = slice(m * width, (m + 1) * width)
        up = dot(low, up_w[m]) + vector(table, UP_B + m)
        value, rate = gelu_pair(up)
        active[:, part] = value.astype(BF16)
        slope[:, part] = rate.astype(BF16)


def hidden(place, lengths, rows, mixed, cotangent, table, group):
    count, width = rows.shape
    arrays, plans = group
    hidden_units = width * (len(plans) - 1)
    return pl.pallas_call(
        functools.partial(hidden_kernel, plans, len(arrays)),
        grid=(count // TILE,),
        in_specs=[SMEM, SMEM]
        + [tile_of(width)] * 3
        + [whole(table.shape)]
        + [ANY] * len(arrays),
        out_specs=[tile_of(width)] * 2 + [tile_of(hidden_units)] * 2 + [tile_of(width)],
        out_shape=[
            jax.ShapeDtypeStruct(rows.shape, F32),
            jax.ShapeDtypeStruct(rows.shape, BF16),
            jax.ShapeDtypeStruct((count, hidden_units), BF16),
            jax.ShapeDtypeStruct((count, hidden_units), BF16),
            jax.ShapeDtypeStruct(rows.shape, BF16),
        ],
        scratch_shapes=[
            pltpu.VMEM((width, width), BF16),
            pltpu.VMEM((len(plans) - 1, width, width), BF16),
            pltpu.SemaphoreType.DMA((sum(len(p) for p in plans),)),
        ],
        compiler_params=params(60),
        cost_estimate=cost(14 * count * width * hidden_units // 4, 26 * count * width, 2 * count * hidden_units),
        name="hidden",
    )(place, lengths, rows, mixed, cotangent, table, *arrays)


STATS_TWO = 7


def back_kernel(
    two_plans, down_plan, sizes, place, lengths, rows, branch_in, active, slope, grad_down, cotangent,
    table, *refs,
):
    sources, refs = refs[: sum(sizes)], refs[sum(sizes) :]
    two, three = sources[: sizes[0]], sources[sizes[0] :]
    *up_plans, out_plan = two_plans
    result, grad_hidden, grad_middle_out, grad_branch, grad_mixed, stats, hidden_stats = refs[:7]
    out_w, up_w, down_w, sems = refs[7:]
    made = [copies(place[0], three, down_plan, down_w, sems, 0)]
    first = len(down_plan)
    for m, plan in enumerate(up_plans):
        made.append(copies(place[0], two, plan, up_w.at[m], sems, first))
        first += len(plan)
    made.append(copies(place[0], two, out_plan, out_w, sems, first))

    @pl.when(pl.program_id(0) == 0)
    def _():
        for group in made:
            start_all(group)
        stats[...] = jnp.zeros_like(stats)
        hidden_stats[...] = jnp.zeros_like(hidden_stats)
        wait_all(made[0])

    live = live_rows(lengths, cotangent.shape)
    branch = branch_in[...]
    middle = rows[...].astype(F32) + vector(table, ATTN_S) * branch
    down_out = dot(active[...], down_w[...]) + vector(table, DOWN_B)
    result[...] = jnp.where(live, middle + vector(table, MLP_S) * down_out, 0.0).astype(BF16)
    grad_out = jnp.where(live, cotangent[...].astype(F32), 0.0)
    sums = [row_sum(grad_out * down_out), row_sum(grad_down[...].astype(F32))]

    @pl.when(pl.program_id(0) == 0)
    def _():
        for group in made[1:]:
            wait_all(group)

    width = middle.shape[1]
    grad_normed = jnp.zeros(middle.shape, F32)
    for m in range(len(up_plans)):
        part = slice(m * width, (m + 1) * width)
        grad_active = dot_nt(grad_down[...], down_w[part, :])
        low = (grad_active * slope[:, part].astype(F32)).astype(BF16)
        grad_hidden[:, part] = low
        hidden_stats[m : m + 1, :] += row_sum(low.astype(F32))
        grad_normed += dot_nt(low, up_w[m])
    unit_rows, inverse = centred_rows(middle)
    sums += [row_sum(grad_normed * unit_rows), row_sum(grad_normed)]
    grad_middle = grad_out + norm_back(grad_normed, unit_rows, inverse, vector(table, LN2_G))
    grad_middle_out[...] = grad_middle
    low = (grad_middle * vector(table, ATTN_S)).astype(BF16)
    grad_branch[...] = low
    sums += [row_sum(grad_middle * branch), row_sum(low.astype(F32))]
    grad_mixed[...] = dot_nt(low, out_w[...]).astype(BF16)
    for at, total in enumerate(sums):
        stats[at : at + 1, :] += total


def back(place, lengths, rows, branch, active, slope, grad_down, cotangent, table, two, three):
    count, width = rows.shape
    hidden_units = active.shape[1]
    plans = (two[1], three[1][0])
    sizes = (len(two[0]), len(three[0]))
    return pl.pallas_call(
        functools.partial(back_kernel, *plans, sizes),
        grid=(count // TILE,),
        in_specs=[SMEM, SMEM]
        + [tile_of(width)] * 2
        + [tile_of(hidden_units)] * 2
        + [tile_of(width)] * 2
        + [whole(table.shape)]
        + [ANY] * sum(sizes),
        out_specs=[tile_of(width), tile_of(hidden_units)]
        + [tile_of(width)] * 3
        + [whole((8, width)), whole((8, width))],
        out_shape=[
            jax.ShapeDtypeStruct(rows.shape, BF16),
            jax.ShapeDtypeStruct(active.shape, BF16),
            jax.ShapeDtypeStruct(rows.shape, F32),
            jax.ShapeDtypeStruct(rows.shape, BF16),
            jax.ShapeDtypeStruct(rows.shape, BF16),
            jax.ShapeDtypeStruct((8, width), F32),
            jax.ShapeDtypeStruct((8, width), F32),
        ],
        scratch_shapes=[
            pltpu.VMEM((width, width), BF16),
            pltpu.VMEM((len(plans[0]) - 1, width, width), BF16),
            pltpu.VMEM((hidden_units, width), BF16),
            pltpu.SemaphoreType.DMA((sum(len(p) for p in plans[0]) + len(plans[1]),)),
        ],
        compiler_params=params(60),
        cost_estimate=cost(26 * count * width * hidden_units // 4, 40 * count * width),
        name="back",
    )(place, lengths, rows, branch, active, slope, grad_down, cotangent, table, *two[0], *three[0])


def outer_kernel(spread, steps, place, *refs):
    pairs = len(steps)
    lefts, rights, refs = refs[:pairs], refs[pairs : 2 * pairs], refs[2 * pairs :]
    flat = refs[-1]
    step = pl.program_id(0)
    first = 0
    for left, count in zip(lefts, steps):

        @pl.when(step == first)
        def _(left=left):
            for at in range(0, flat.shape[0], 128):
                block = left[:, at : at + 128].astype(F32)
                flat[at : at + 128, :] = jnp.transpose(block).astype(BF16)

        first += count

    def put(right):
        value = dot(flat[...], right[...])
        if not spread:
            refs[0][...] = value.astype(BF16)
            return
        mine, theirs, held = refs[:3]
        plane, core = place[0] // 2, place[0] % 2
        held[...] = value
        unit = flat.shape[0] // 8
        for at in range(4):
            one = pl.multiple_of((2 * at + core) * unit, 8)
            other = pl.multiple_of((2 * at + 1 - core) * unit, 8)
            mine[at ^ plane, 0] = held[pl.ds(one, unit), :].astype(BF16)
            theirs[at ^ plane, 0] = held[pl.ds(other, unit), :].astype(BF16)

    first = 0
    for right, count in zip(rights, steps):

        @pl.when((step >= first) & (step < first + count))
        def _(right=right):
            put(right)

        first += count


def outer(place, pairs, width):
    count, height = pairs[0][0].shape
    steps = [right.shape[1] // width for _, right in pairs]
    total = sum(steps)
    right_specs, first = [], 0
    for own in steps:
        right_specs.append(
            pl.BlockSpec(
                (count, width),
                lambda i, first=first, own=own: (0, jnp.clip(i - first, 0, own - 1)),
            )
        )
        first += own
    scratch = [pltpu.VMEM((height, count), BF16)]
    if direct():
        block = pl.BlockSpec((4, 1, height // 8, width), lambda i: (0, i, 0, 0))
        shape = jax.ShapeDtypeStruct((4, total, height // 8, width), BF16)
        specs, shapes = [block, block], [shape, shape]
        scratch = [pltpu.VMEM((height, width), F32)] + scratch
    else:
        specs = pl.BlockSpec((height, width), lambda i: (0, i))
        shapes = jax.ShapeDtypeStruct((height, total * width), BF16)
    return pl.pallas_call(
        functools.partial(outer_kernel, direct(), steps),
        grid=(total,),
        in_specs=[SMEM] + [whole((count, height))] * len(pairs) + right_specs,
        out_specs=specs,
        out_shape=shapes,
        scratch_shapes=scratch,
        compiler_params=params(60),
        cost_estimate=cost(2 * count * height * total * width, 2 * (count + height) * total * width),
        name="outer",
    )(place, *(left for left, _ in pairs), *(right for _, right in pairs))


def wide_outer_kernel(place, left, right, out, flat):
    @pl.when(pl.program_id(0) == 0)
    def _():
        for at in range(0, flat.shape[0], 128):
            block = left[:, at : at + 128].astype(F32)
            flat[at : at + 128, :] = jnp.transpose(block).astype(BF16)

    out[0] = dot(flat[...], right[...]).astype(BF16)


def wide_outer(place, left, right):
    count, height = left.shape
    columns = right.shape[1]
    steps = 8
    step = columns // steps
    return pl.pallas_call(
        wide_outer_kernel,
        grid=(steps,),
        in_specs=[SMEM, whole(left.shape), pl.BlockSpec((count, step), lambda i: (0, i))],
        out_specs=pl.BlockSpec((1, height, step), lambda i: (i, 0, 0)),
        out_shape=jax.ShapeDtypeStruct((steps, height, step), BF16),
        scratch_shapes=[pltpu.VMEM((height, count), BF16)],
        compiler_params=params(60),
        cost_estimate=cost(2 * count * height * columns, 2 * (count + height) * (height + columns)),
        name="wide_outer",
    )(place, left, right)


def inputs_kernel(plans, place, rows, grad_middle, grad_q, grad_k, grad_v, table, *refs):
    count = len(refs) - 2 - 2
    sources, (grad_rows, stats, weights, sems) = refs[:count], refs[count:]
    made, first = [], 0
    for m in range(3):
        made.append(copies(place[0], sources, plans[m], weights.at[m], sems, first))
        first += len(plans[m])

    @pl.when(pl.program_id(0) == 0)
    def _():
        for group in made:
            start_all(group)
        stats[...] = jnp.zeros_like(stats)
        for group in made:
            wait_all(group)

    grad = dot_nt(grad_q[...], weights[0])
    grad += dot_nt(grad_k[...], weights[1])
    grad += dot_nt(grad_v[...], weights[2])
    unit_rows, inverse = centred_rows(rows[...].astype(F32))
    grad_rows[...] = grad_middle[...] + norm_back(grad, unit_rows, inverse, vector(table, LN1_G))
    sums = [row_sum(grad * unit_rows), row_sum(grad)]
    sums += [row_sum(grad_q[...].astype(F32)), row_sum(grad_v[...].astype(F32))]
    for at, total in enumerate(sums):
        stats[at : at + 1, :] += total


def inputs_back(place, rows, grad_middle, grad_q, grad_k, grad_v, table, group):
    arrays, plans = group
    count, width = rows.shape
    return pl.pallas_call(
        functools.partial(inputs_kernel, plans),
        grid=(count // TILE,),
        in_specs=[SMEM] + [tile_of(width)] * 5 + [whole(table.shape)] + [ANY] * len(arrays),
        out_specs=[tile_of(width), whole((8, width))],
        out_shape=[
            jax.ShapeDtypeStruct(rows.shape, F32),
            jax.ShapeDtypeStruct((8, width), F32),
        ],
        scratch_shapes=[
            pltpu.VMEM((3, width, width), BF16),
            pltpu.SemaphoreType.DMA((sum(len(p) for p in plans[:3]),)),
        ],
        compiler_params=params(60),
        cost_estimate=cost(6 * count * width * width, 20 * count * width),
        name="inputs_back",
    )(place, rows, grad_middle, grad_q, grad_k, grad_v, table, *arrays)


def add_low(left, right):
    return (left.astype(F32) + right.astype(F32)).astype(left.dtype)


def split_cores(stacked):
    stacked = flip_own(stacked)
    pieces = stacked.reshape((-1, 2) + stacked.shape[1:])
    return pieces[:, 0], pieces[:, 1]


def quarters(held):
    held = held.reshape((-1, 4) + held.shape[1:])
    return tuple(held[:, i] for i in range(4))


def halve(total):
    for bit in reversed(range(3, wide_bits())):
        count = total.shape[0] // 2
        total = add_low(total[:count], cross(total[count:], bit))
    return total[0]


def spread_blocks(stacked):
    size = stacked.shape[0]
    here = lax.axis_index("narrow")
    steps = sorted(range(1, size), key=lambda step: min(step, size - step))
    blocks = [
        lax.dynamic_index_in_dim(stacked, lax.rem(here + step, size), keepdims=False)
        for step in steps
    ]
    return blocks, [lambda v, step=step: shift(v, step) for step in steps]


def add_blocks(stacked, moved):
    total = lax.dynamic_index_in_dim(stacked, lax.axis_index("narrow"), keepdims=False)
    total = total.astype(F32)
    for block in moved:
        total = total + block.astype(F32)
    return total


def by_core(grad, parts):
    if direct():
        return tuple(piece.reshape(4, -1, piece.shape[3]) for piece in grad)
    places = lax.axis_size("wide")
    height, columns = grad.shape
    stacked = grad.reshape(places, height // places, parts, columns // parts).transpose(0, 2, 1, 3)
    return split_cores(stacked.reshape(places, -1, columns // parts))


def all_stages():
    stages = []
    for bit in range(lax.axis_size("narrow").bit_length() - 1):
        stages.append(lambda v, bit=bit: exchange(v, "narrow", lambda i: i ^ (1 << bit)))
    for bit in reversed(range(wide_bits())):
        stages.append(lambda v, bit=bit: cross(v, bit))
    return stages


def own_spot(places, layers, piece, width):
    start = (lax.axis_index("wide") * layers + lax.axis_index("narrow")) * piece
    return start // width, start % width


def shards(
    patches, lengths, w_qkv, w_out, w_up, w_down, ln1_gain, ln1_bias, q_bias, v_bias, out_bias, attn_scale,
    ln2_gain, ln2_bias, up_bias, down_bias, mlp_scale, cotangent,
):
    places, layers = lax.axis_size("wide"), lax.axis_size("narrow")
    place = lax.axis_index("wide").astype(jnp.int32).reshape(1)
    short, width = w_up.shape
    part = w_qkv.shape[1]
    quarter = w_out.shape[1]
    packs, pack_rows, _ = patches.shape
    rows = patches.reshape(-1, width)
    cotangent = cotangent.reshape(-1, width)

    small = [ln1_gain, ln1_bias, q_bias, v_bias, out_bias, attn_scale, ln2_gain, ln2_bias, down_bias, mlp_scale]
    small_spot = own_spot(places, layers, ln1_gain.shape[0], width)
    up_spot = own_spot(places, layers, up_bias.shape[0], width)
    table = jnp.zeros((16, width), BF16)
    table = lax.dynamic_update_slice(table, jnp.stack(small), (0, small_spot[1]))
    table = lax.dynamic_update_slice(table, up_bias[None], (UP_B + up_spot[0], up_spot[1]))
    stages = all_stages()

    def spread_table(table, stages):
        for stage in stages:
            table = table + stage(table)
        return table

    one = [w_qkv] * (layers - 1), shifts(layers)
    table, one = beside(lambda v: spread_table(v, stages[2:]), table, *one)
    one = by_origin([w_qkv, *one])
    one = jnp.concatenate(jnp.split(side_by_side(one), 3, axis=1))
    held = double(one)
    up_out = jnp.concatenate([w_up, w_out], axis=1)
    sends = [held, held] + [up_out] * (layers - 1)
    table, moved = beside(
        lambda v: spread_table(v, stages[:2]).astype(F32), table, sends, planes() + shifts(layers)
    )
    near, far, *two = moved
    half = near.shape[1] // 32 * 16
    sends = [near[:, :half], far[:, half:], jnp.concatenate([held, near, far])]
    two, moved = beside(
        lambda v: v, by_origin([up_out, *two]), sends, corners() + [lambda v: cross(v, 0)]
    )
    planes_one = held, near, far, jnp.concatenate(moved[:2], axis=1)
    other_three = moved[2]
    two = jnp.concatenate([two[:, :, :width].reshape(-1, width), side_by_side(two[:, :, width:])])
    held_two = double(two)
    half = two.shape[0] // 32 * 16
    one = matrices(planes_one, (other_three, cross(planes_one[3], 0)), 3)

    first, second = held_two[:, :half], held_two[:, half:]
    (normed, query, key, value), (near_one, far_one) = beside(
        lambda v: project(place, v, table, one), rows, [first, first], planes()
    )
    side_down = jnp.concatenate(jnp.split(w_down, layers, axis=0), axis=1)
    sends = [second, second] + [side_down] * (layers - 1)
    attention, (near_two, far_two, *three) = beside(
        lambda v: attend(lengths, v, key, value, 0), query, sends, planes() + shifts(layers)
    )
    near = jnp.concatenate([near_one, near_two], axis=1)
    far = jnp.concatenate([far_one, far_two], axis=1)
    sends = [near_one, far_two, jnp.concatenate([held_two, near, far])]
    for pack in range(1, packs):
        run = functools.partial(attend, lengths, query, key, value, pack)
        if pack == packs - 1:
            attention, moved = beside(run, attention, sends, corners() + [lambda v: cross(v, 0)])
        else:
            attention = run(attention)
    mixed, log_total = attention
    planes_two = held_two, near, far, jnp.concatenate(moved[:2], axis=1)
    two = matrices(planes_two, (moved[2], cross(planes_two[3], 0)), layers + 1)
    three = by_origin([side_down, *three])
    three = jnp.concatenate(
        [side_by_side(three[:, :, i * quarter : (i + 1) * quarter]) for i in range(layers)]
    )
    held = double(three)
    (branch, normed_two, active, slope, grad_down), (near, far) = beside(
        lambda v: hidden(place, lengths, rows, v, cotangent, table, two), mixed, [held, held], planes()
    )
    half = near.shape[1] // 32 * 16
    sends = [near[:, :half], far[:, half:], jnp.concatenate([held, near, far])]
    grad_w_down, moved = beside(
        lambda v: wide_outer(place, v, active), grad_down, sends, corners() + [lambda v: cross(v, 0)]
    )
    planes_three = held, near, far, jnp.concatenate(moved[:2], axis=1)
    three = matrices(planes_three, (moved[2], cross(planes_three[3], 0)), 1)
    active = after(active, grad_w_down)
    if places != 8:
        grad_w_down = grad_w_down.reshape(8, width, places // 8, -1).transpose(0, 2, 1, 3)
    total_down = lax.psum_scatter(grad_w_down.reshape(places, width, -1), "wide")

    result, grad_hidden, grad_middle, grad_branch, grad_mixed, stats_two, hidden_stats = back(
        place, lengths, rows, branch, active, slope, grad_down, cotangent, table, two, three
    )
    mine, theirs = by_core(
        outer(place, [(normed_two, grad_hidden), (mixed, grad_branch)], width), layers + 1
    )
    grads, (moved,) = beside(
        lambda v: attend_back(lengths, query, key, value, v, log_total, 0),
        grad_mixed,
        [theirs],
        [lambda v: cross(v, 0)],
    )
    own, near, far, corner = quarters(add_low(mine, moved))
    half = own.shape[1] // 32 * 16
    for pack in range(1, packs):
        run = functools.partial(attend_back, lengths, query, key, value, grad_mixed, log_total, pack)
        if pack == packs - 1:
            sends = [corner[:, :half], corner[:, half:]]
            grads, moved = beside(run, grads, sends, planes())
        else:
            grads = run(grads)
    far_part = add_low(far[:, :half], moved[0])
    near_part = add_low(near[:, half:], moved[1])
    grad_w_qkv, (near, far) = beside(
        lambda v: outer(place, [(normed, v)], width),
        jnp.concatenate(grads, axis=1),
        [near[:, :half], far[:, half:]],
        planes(),
    )
    mine, theirs = by_core(grad_w_qkv, 3)
    grad_q, grad_k, grad_v = grads
    near_part, far_part, theirs, total_down, mine = lax.optimization_barrier(
        (near_part, far_part, theirs, total_down, mine)
    )
    sends, moves = spread_blocks(total_down.reshape(layers, quarter, -1))
    (grad_rows, stats_one), moved = beside(
        lambda v: inputs_back(place, rows, grad_middle, v, grad_k, grad_v, table, one),
        grad_q,
        [near_part, far_part, theirs, *sends],
        planes() + [lambda v: cross(v, 0)] + moves,
    )
    near_part, far_part, other, *down = moved

    sums = jnp.concatenate([stats_one, stats_two, hidden_stats])
    total_down = add_blocks(total_down.reshape(layers, quarter, -1), down).T
    near = jnp.concatenate([near, near_part], axis=1).astype(F32)
    far = jnp.concatenate([far_part, far], axis=1).astype(F32)
    total_up = halve((own.astype(F32) + near + far).astype(BF16))
    total_out = total_up[layers * short :].reshape(short, layers, quarter).transpose(1, 0, 2)
    total_up = total_up[: layers * short].reshape(layers, short, width)
    total_up = jnp.concatenate([total_up, total_out], axis=2)
    up_sends, up_moves = spread_blocks(total_up)
    own, near, far, corner = quarters(add_low(mine, other))
    half = own.shape[1] // 32 * 16
    split = len(up_sends) - 1
    sums, moved = beside(
        lambda v: v + stages[-1](v),
        sums,
        [corner[:, :half], corner[:, half:]] + up_sends[:split],
        planes() + up_moves[:split],
    )
    up_parts = moved[2:]
    far = jnp.concatenate([add_low(far[:, :half], moved[0]), far[:, half:]], axis=1)
    near = jnp.concatenate([near[:, :half], add_low(near[:, half:], moved[1])], axis=1)
    sums, moved = beside(
        lambda v: spread_table(v, stages[:-3]), sums, [near, far] + up_sends[split:], planes() + up_moves[split:]
    )
    total_qkv = own.astype(F32) + moved[0].astype(F32) + moved[1].astype(F32)
    total_qkv = halve(total_qkv.astype(BF16))
    total_qkv = jnp.concatenate([total_qkv[i * short : (i + 1) * short] for i in range(3)], axis=1)
    total_qkv = total_qkv.reshape(short, layers, part).transpose(1, 0, 2)
    sends, moves = spread_blocks(total_qkv)
    up_parts += moved[2:]
    sums, moved = beside(lambda v: spread_table(v, stages[-3:-1]), sums, sends, moves)
    total_qkv = add_blocks(total_qkv, moved)
    total_up = add_blocks(total_up, up_parts)

    own = lax.dynamic_slice(sums, (0, small_spot[1]), (16, ln1_gain.shape[0]))
    own_up = lax.dynamic_slice(sums, (16 + up_spot[0], up_spot[1]), (1, up_bias.shape[0]))[0]
    return (
        result.reshape(patches.shape),
        grad_rows.reshape(patches.shape),
        total_qkv,
        total_up[:, width:],
        total_up[:, :width],
        total_down,
        own[0],
        own[1],
        own[2],
        own[3],
        own[13],
        own[12],
        own[10],
        own[11],
        own_up,
        own[9],
        own[8],
    )


def solution(mesh):
    return jax.shard_map(
        shards,
        mesh=mesh,
        in_specs=(
            P(("wide", "narrow"), None, None),
            P(("wide", "narrow"), None),
            P("wide", "narrow"),
            P("wide", "narrow"),
            P("wide", "narrow"),
            P("wide", "narrow"),
            P(("wide", "narrow")),
            P(("wide", "narrow")),
            P(("wide", "narrow")),
            P(("wide", "narrow")),
            P(("wide", "narrow")),
            P(("wide", "narrow")),
            P(("wide", "narrow")),
            P(("wide", "narrow")),
            P(("wide", "narrow")),
            P(("wide", "narrow")),
            P(("wide", "narrow")),
            P(("wide", "narrow"), None, None),
        ),
        out_specs=(
            P(("wide", "narrow"), None, None),
            P(("wide", "narrow"), None, None),
            P("wide", "narrow"),
            P("wide", "narrow"),
            P("wide", "narrow"),
            P("wide", "narrow"),
            P(("wide", "narrow")),
            P(("wide", "narrow")),
            P(("wide", "narrow")),
            P(("wide", "narrow")),
            P(("wide", "narrow")),
            P(("wide", "narrow")),
            P(("wide", "narrow")),
            P(("wide", "narrow")),
            P(("wide", "narrow")),
            P(("wide", "narrow")),
            P(("wide", "narrow")),
        ),
        check_vma=False,
    )
```

```python
import functools
import math

import jax
import jax.numpy as jnp
from jax import lax
from jax.experimental import pallas as pl
from jax.experimental.pallas import tpu as pltpu
from jax.sharding import PartitionSpec as P

HD = 64
LN_EPSILON = 1e-06
MASKED = -1e30
TILE = 256
F32 = jnp.float32
BF16 = jnp.bfloat16
MIB = 1 << 20


def exchange(value, axis_name, partner):
    size = lax.axis_size(axis_name)
    return lax.ppermute(value, axis_name, [(i, partner(i) % size) for i in range(size)])


def cross(value, bit):
    return exchange(value, "wide", lambda i: i ^ (1 << bit))


def shift(value, step):
    return exchange(value, "narrow", lambda i: i + step)


def wide_bits():
    return lax.axis_size("wide").bit_length() - 1


def by_origin(pieces):
    size = len(pieces)
    backward = jnp.stack(pieces[::-1])
    twice = jnp.concatenate([backward, backward])
    return lax.dynamic_slice_in_dim(twice, size - 1 - lax.axis_index("narrow"), size)


def flip_own(stacked):
    here = lax.axis_index("wide")
    size = stacked.shape[0]
    for bit in range(size.bit_length() - 1):
        halves = stacked.reshape((size >> (bit + 1), 2, 1 << bit) + stacked.shape[1:])
        halves = jnp.where((here >> bit) & 1, halves[:, ::-1], halves)
        stacked = halves.reshape(stacked.shape)
    return stacked


def after(value, *others):
    return lax.optimization_barrier((value, others))[0]


def beside(run, value, sends, moves):
    value, sends = lax.optimization_barrier((value, sends))
    moved = [move(send) for move, send in zip(moves, sends, strict=True)]
    return lax.optimization_barrier((run(value), moved))


def beside_loose(run, value, sends, moves):
    return beside(run, value, sends, moves)


def planes():
    return [lambda v: cross(v, 1), lambda v: cross(v, 2)]


def corners():
    return [lambda v: cross(v, 2), lambda v: cross(v, 1)]


def shifts(layers):
    return [lambda v, step=step: shift(v, step) for step in range(1, layers)]


def double(block):
    held = block[None]
    for bit in range(3, wide_bits()):
        held = jnp.concatenate([held, cross(held, bit)])
    return held


def side_by_side(stacked):
    return jnp.concatenate([stacked[i] for i in range(stacked.shape[0])], axis=1)


def direct():
    return lax.axis_size("wide") == 8


def in_order(stacked, parts):
    places, rows, columns = stacked.shape
    unit = rows // parts
    if parts == 1 or not direct():
        stacked = stacked.reshape(places, parts, unit, columns)
        arrays = [stacked[:, m].reshape(-1, columns) for m in range(parts)]
        return arrays, [[(m, 0, 0, None, unit)] for m in range(parts)]
    return [stacked], [[(0, at, m * unit, at, -unit) for at in range(places)] for m in range(parts)]


def matrices(planes, cores, parts, short, long):
    unit = (planes[0].shape[1] - 16) // parts
    behind = parts * unit
    if not direct():
        other = [*jnp.split(cores[0], 3), cores[1]]
        stacked = jnp.stack([jnp.stack(pair, axis=1) for pair in zip(planes, other)], axis=1)
        stacked = flip_own(stacked.reshape((-1,) + planes[0].shape[1:]))
        width = stacked.shape[2]
        rows = stacked[:, behind:].transpose(1, 0, 2)
        table = rows[:10, :, :short].reshape(10, width)
        up = rows[10, :, :long].reshape(-1, width)
        table = jnp.concatenate([table, up])
        table = jnp.pad(table, ((0, 16 - table.shape[0]), (0, 0)))
        stacked = stacked[:, :behind].reshape(stacked.shape[0], parts, unit, -1)
        arrays = [stacked[:, m].reshape(-1, stacked.shape[3]) for m in range(parts)]
        plans = [[(m, 0, 0, None, unit)] for m in range(parts)]
        return (arrays, plans), (table, None)
    spots = [(0, 0, 0), (1, 0, 2), (2, 0, 4), (3, 0, 6), (4, 0, 1), (4, 1, 3), (4, 2, 5), (5, 0, 7)]
    plans = [[(at, index, m * unit, rel, unit) for at, index, rel in spots] for m in range(parts)]
    rows = jnp.concatenate([piece[:, behind:] for piece in (*planes, *cores)])
    order = (0, 2, 4, 6, 1, 3, 5, 7)
    return ([*planes, *cores], plans), (rows, (order, short, long))


def copies(place, refs, plan, target, sems, first):
    made = []
    for at, index, row, rel, unit in plan:
        sem = sems.at[first + len(made)]
        if rel is None:
            made.append(pltpu.make_async_copy(refs[at], target, sem))
        else:
            start = -rel * unit if unit < 0 else pl.multiple_of((place ^ rel) * unit, 16)
            unit = abs(unit)
            source = refs[at].at[index, pl.ds(row, unit)]
            made.append(pltpu.make_async_copy(source, target.at[pl.ds(start, unit)], sem))
    return made


def start_all(made):
    for copy in made:
        copy.start()


def wait_all(made):
    for copy in made:
        copy.wait()


def dot(left, right):
    return lax.dot_general(left, right, (((1,), (0,)), ((), ())), preferred_element_type=F32)


def dot_nt(left, right):
    return lax.dot_general(left, right, (((1,), (1,)), ((), ())), preferred_element_type=F32)


def centred_rows(values):
    row_mean = jnp.mean(values, axis=-1, keepdims=True)
    centred = values - row_mean
    row_var = jnp.mean(centred * centred, axis=-1, keepdims=True)
    inverse = lax.rsqrt(row_var + LN_EPSILON)
    return centred * inverse, inverse


def norm_back(grad, unit_rows, inverse, gain):
    scaled = grad * gain
    mean_one = jnp.mean(scaled, axis=-1, keepdims=True)
    mean_two = jnp.mean(scaled * unit_rows, axis=-1, keepdims=True)
    return (scaled - mean_one - unit_rows * mean_two) * inverse


def row_sum(values):
    return jnp.sum(values, axis=0, keepdims=True)


def gelu_pair(values):
    bell = jnp.exp(values * values * -0.5)
    share = 0.5 + 0.5 * lax.erf(values * math.sqrt(0.5))
    return values * share, share + values * bell * (1.0 / math.sqrt(2.0 * math.pi))


ANY = pl.BlockSpec(memory_space=pl.ANY)
SMEM = pl.BlockSpec(memory_space=pltpu.SMEM)


def whole(shape):
    return pl.BlockSpec(shape, lambda *_: (0,) * len(shape))


def tile_of(columns):
    return pl.BlockSpec((TILE, columns), lambda i: (i, 0))


def cost(flops, moved, exps=0):
    return pl.CostEstimate(flops=flops, bytes_accessed=moved, transcendentals=exps)


def params(mib, dims=1):
    return pltpu.CompilerParams(
        vmem_limit_bytes=mib * MIB, dimension_semantics=("arbitrary",) * dims
    )


LN1_G, LN1_B, Q_B, V_B, OUT_B, ATTN_S, LN2_G, LN2_B, DOWN_B, MLP_S, UP_B = range(11)


def vector(table, row):
    return table[row : row + 1, :]


def make_table(place, rows, layout):
    if layout is None:
        return rows[...].astype(F32)
    order, short, long = layout
    shape = rows.shape[1:]
    lane = lax.broadcasted_iota(jnp.int32, shape, 1)
    row = lax.broadcasted_iota(jnp.int32, shape, 0)
    table = jnp.zeros(shape, F32)
    for at, rel in enumerate(order):
        spot = place ^ rel
        piece = rows[at].astype(F32)
        table += pltpu.roll(jnp.where((row < UP_B) & (lane < short), piece, 0.0), spot * short, 1)
        start = spot * long
        up = jnp.where(lane[:1] < long, piece[UP_B : UP_B + 1], 0.0)
        up = pltpu.roll(jnp.broadcast_to(up, shape), lax.rem(start, shape[1]), 1)
        table += jnp.where(row == UP_B + start // shape[1], up, 0.0)
    return table


def project_kernel(plans, layout, place, rows, extras, *refs):
    count = len(refs) - 5 - 2
    sources, (normed, query, key, value, table, weights, sems) = refs[:count], refs[count:]
    made, first = [], 0
    for m in range(3):
        made.append(copies(place[0], sources, plans[m], weights.at[m], sems, first))
        first += len(plans[m])

    @pl.when(pl.program_id(0) == 0)
    def _():
        for group in made:
            start_all(group)
        table[...] = make_table(place[0], extras, layout)

    unit_rows, _ = centred_rows(rows[...].astype(F32))
    low = (unit_rows * vector(table, LN1_G) + vector(table, LN1_B)).astype(BF16)
    normed[...] = low

    @pl.when(pl.program_id(0) == 0)
    def _():
        for group in made:
            wait_all(group)

    query[...] = ((dot(low, weights[0]) + vector(table, Q_B)) * 0.125).astype(BF16)
    key[...] = dot(low, weights[1]).astype(BF16)
    value[...] = (dot(low, weights[2]) + vector(table, V_B)).astype(BF16)


def project(place, rows, extras, group):
    arrays, plans = group
    extras, layout = extras
    count, width = rows.shape
    return pl.pallas_call(
        functools.partial(project_kernel, plans, layout),
        grid=(count // TILE,),
        in_specs=[SMEM, tile_of(width), whole(extras.shape)] + [ANY] * len(arrays),
        out_specs=[tile_of(width)] * 4 + [whole((16, width))],
        out_shape=[jax.ShapeDtypeStruct(rows.shape, BF16)] * 4
        + [jax.ShapeDtypeStruct((16, width), F32)],
        scratch_shapes=[
            pltpu.VMEM((3, width, width), BF16),
            pltpu.SemaphoreType.DMA((sum(len(p) for p in plans[:3]),)),
        ],
        compiler_params=params(60),
        cost_estimate=cost(6 * count * width * width, 14 * count * width),
        name="project",
    )(place, rows, extras, *arrays)


def segments(lengths, pack, position):
    end, segment = 0, jnp.zeros_like(position)
    for slot in range(lengths.shape[1] - 1):
        end = end + lengths[pack, slot]
        segment = segment + (position >= end).astype(jnp.int32)
    return jnp.where(position < end, segment, lengths.shape[1] + position)


def same_segment(lengths, pack, rows):
    down = lax.broadcasted_iota(jnp.int32, (rows, 128), 0)
    along = lax.broadcasted_iota(jnp.int32, (1, rows), 1)
    column = segments(lengths, pack, down)
    row = segments(lengths, pack, along)
    return jnp.concatenate([column] * (rows // 128), axis=1) == row


def head_lanes(shape, head):
    lane = lax.broadcasted_iota(jnp.int32, shape, 1)
    return (lane < HD) if head == 0 else (lane >= HD)


def only(values, head):
    return jnp.where(head_lanes(values.shape, head), values, jnp.zeros_like(values))


def attend_kernel(pack, lengths, query, key, value, *refs):
    attended, log_total = refs[-2:]
    rows = query.shape[0]
    same = same_segment(lengths, pack, rows)
    flat = jnp.transpose(value[...].astype(F32)).astype(BF16)
    mixed = []
    for head in range(2):
        scores = dot_nt(key[...], only(query[...], head))
        scores = jnp.where(same, scores, MASKED)
        top = jnp.max(scores, axis=0, keepdims=True)
        powers = jnp.exp(scores - top)
        total = jnp.sum(powers, axis=0, keepdims=True)
        weights = (powers * (1.0 / total)).astype(BF16)
        mixed.append(dot(flat[head * HD : (head + 1) * HD], weights))
        log_total[0, 0, head : head + 1, :] = top + jnp.log(total)
    attended[...] = jnp.transpose(jnp.concatenate(mixed, axis=0)).astype(BF16)


def pair_block(rows, pack):
    return pl.BlockSpec((rows, 2 * HD), lambda h: (pack, h))


def log_block(rows, pack):
    return pl.BlockSpec((1, 1, 2, rows), lambda h: (pack, h, 0, 0))


def attend(lengths, query, key, value, pack, earlier=()):
    packs = lengths.shape[0]
    count, width = query.shape
    rows, pairs = count // packs, width // (2 * HD)
    return pl.pallas_call(
        functools.partial(attend_kernel, pack),
        grid=(pairs,),
        in_specs=[SMEM] + [pair_block(rows, pack)] * 3 + [ANY] * len(earlier),
        out_specs=[pair_block(rows, pack), log_block(rows, pack)],
        out_shape=[
            jax.ShapeDtypeStruct(query.shape, BF16),
            jax.ShapeDtypeStruct((packs, pairs, 2, rows), F32),
        ],
        input_output_aliases={4 + i: i for i in range(len(earlier))},
        compiler_params=params(60),
        cost_estimate=cost(16 * rows * rows * width, 8 * rows * width) if earlier else cost(0, 0),
        name="attend",
    )(lengths, query, key, value, *earlier)


def attend_back_kernel(pack, lengths, query, key, value, grad, log_total, *refs):
    grad_q, grad_k, grad_v = refs[-3:]
    rows = query.shape[0]
    same = same_segment(lengths, pack, rows)
    flat_key = jnp.transpose(key[...].astype(F32)).astype(BF16)
    by_query, by_key, by_value = [], [], []
    for head in range(2):
        scores = dot_nt(key[...], only(query[...], head))
        probs = jnp.exp(scores - log_total[0, 0, head : head + 1, :])
        probs = jnp.where(same, probs, 0.0)
        by_value.append(dot(probs.astype(BF16), grad[...]))
        grad_probs = dot_nt(value[...], only(grad[...], head))
        centre = jnp.sum(grad_probs * probs, axis=0, keepdims=True)
        grad_scores = (probs * (grad_probs - centre)).astype(BF16)
        by_key.append(dot(grad_scores, query[...]))
        by_query.append(dot(flat_key[head * HD : (head + 1) * HD], grad_scores))
    lanes = head_lanes(by_key[0].shape, 0)
    grad_k[...] = jnp.where(lanes, by_key[0], by_key[1]).astype(BF16)
    grad_v[...] = jnp.where(lanes, by_value[0], by_value[1]).astype(BF16)
    grad_q[...] = jnp.transpose(jnp.concatenate(by_query, axis=0)).astype(BF16) * 0.125


def attend_back(lengths, query, key, value, grad, log_total, pack, earlier=()):
    packs = lengths.shape[0]
    count, width = query.shape
    rows, pairs = count // packs, width // (2 * HD)
    return pl.pallas_call(
        functools.partial(attend_back_kernel, pack),
        grid=(pairs,),
        in_specs=[SMEM]
        + [pair_block(rows, pack)] * 4
        + [log_block(rows, pack)]
        + [ANY] * len(earlier),
        out_specs=[pair_block(rows, pack)] * 3,
        out_shape=[jax.ShapeDtypeStruct(query.shape, BF16)] * 3,
        input_output_aliases={6 + i: i for i in range(len(earlier))},
        compiler_params=params(60),
        cost_estimate=cost(40 * rows * rows * width, 14 * rows * width, 12 * rows * rows),
        name="attend_back",
    )(lengths, query, key, value, grad, log_total, *earlier)


def live_rows(lengths, shape):
    tiles = pl.num_programs(0) // lengths.shape[0]
    step = pl.program_id(0)
    pack = step // tiles
    end = 0
    for slot in range(lengths.shape[1] - 1):
        end = end + lengths[pack, slot]
    position = lax.broadcasted_iota(jnp.int32, shape, 0) + (step - pack * tiles) * shape[0]
    return position < end


def hidden_kernel(plans, size, place, lengths, rows, mixed, cotangent, table, *refs):
    two, refs = refs[:size], refs[size:]
    *up_plans, out_plan = plans
    branch_out, normed, active, slope, grad_down, out_w, up_w, sems = refs
    made = [copies(place[0], two, out_plan, out_w, sems, 0)]
    first = len(out_plan)
    for m, plan in enumerate(up_plans):
        made.append(copies(place[0], two, plan, up_w.at[m], sems, first))
        first += len(plan)

    @pl.when(pl.program_id(0) == 0)
    def _():
        for group in made:
            start_all(group)
        wait_all(made[0])

    branch = dot(mixed[...], out_w[...]) + vector(table, OUT_B)
    branch_out[...] = branch
    middle = rows[...].astype(F32) + vector(table, ATTN_S) * branch
    unit_rows, _ = centred_rows(middle)
    low = (unit_rows * vector(table, LN2_G) + vector(table, LN2_B)).astype(BF16)
    normed[...] = low
    live = live_rows(lengths, cotangent.shape)
    grad_out = jnp.where(live, cotangent[...].astype(F32), 0.0)
    grad_down[...] = (grad_out * vector(table, MLP_S)).astype(BF16)

    width = low.shape[1]
    for m in range(len(up_plans)):

        @pl.when(pl.program_id(0) == 0)
        def _(m=m):
            wait_all(made[m + 1])

        part = slice(m * width, (m + 1) * width)
        up = dot(low, up_w[m]) + vector(table, UP_B + m)
        value, rate = gelu_pair(up)
        active[:, part] = value.astype(BF16)
        slope[:, part] = rate.astype(BF16)


def hidden(place, lengths, rows, mixed, cotangent, table, group):
    count, width = rows.shape
    arrays, plans = group
    hidden_units = width * (len(plans) - 1)
    return pl.pallas_call(
        functools.partial(hidden_kernel, plans, len(arrays)),
        grid=(count // TILE,),
        in_specs=[SMEM, SMEM]
        + [tile_of(width)] * 3
        + [whole(table.shape)]
        + [ANY] * len(arrays),
        out_specs=[tile_of(width)] * 2 + [tile_of(hidden_units)] * 2 + [tile_of(width)],
        out_shape=[
            jax.ShapeDtypeStruct(rows.shape, F32),
            jax.ShapeDtypeStruct(rows.shape, BF16),
            jax.ShapeDtypeStruct((count, hidden_units), BF16),
            jax.ShapeDtypeStruct((count, hidden_units), BF16),
            jax.ShapeDtypeStruct(rows.shape, BF16),
        ],
        scratch_shapes=[
            pltpu.VMEM((width, width), BF16),
            pltpu.VMEM((len(plans) - 1, width, width), BF16),
            pltpu.SemaphoreType.DMA((sum(len(p) for p in plans),)),
        ],
        compiler_params=params(60),
        cost_estimate=cost(14 * count * width * hidden_units // 4, 26 * count * width, 2 * count * hidden_units),
        name="hidden",
    )(place, lengths, rows, mixed, cotangent, table, *arrays)


STATS_TWO = 7


def back_kernel(
    two_plans, down_plan, sizes, place, lengths, rows, branch_in, active, slope, grad_down, cotangent,
    table, *refs,
):
    sources, refs = refs[: sum(sizes)], refs[sum(sizes) :]
    two, three = sources[: sizes[0]], sources[sizes[0] :]
    *up_plans, out_plan = two_plans
    result, grad_hidden, grad_middle_out, grad_branch, grad_mixed, stats, hidden_stats = refs[:7]
    out_w, up_w, down_w, sems = refs[7:]
    made = [copies(place[0], three, down_plan, down_w, sems, 0)]
    first = len(down_plan)
    for m, plan in enumerate(up_plans):
        made.append(copies(place[0], two, plan, up_w.at[m], sems, first))
        first += len(plan)
    made.append(copies(place[0], two, out_plan, out_w, sems, first))

    @pl.when(pl.program_id(0) == 0)
    def _():
        for group in made:
            start_all(group)
        stats[...] = jnp.zeros_like(stats)
        hidden_stats[...] = jnp.zeros_like(hidden_stats)
        wait_all(made[0])

    live = live_rows(lengths, cotangent.shape)
    branch = branch_in[...]
    middle = rows[...].astype(F32) + vector(table, ATTN_S) * branch
    down_out = dot(active[...], down_w[...]) + vector(table, DOWN_B)
    result[...] = jnp.where(live, middle + vector(table, MLP_S) * down_out, 0.0).astype(BF16)
    grad_out = jnp.where(live, cotangent[...].astype(F32), 0.0)
    sums = [row_sum(grad_out * down_out), row_sum(grad_down[...].astype(F32))]

    @pl.when(pl.program_id(0) == 0)
    def _():
        for group in made[1:]:
            wait_all(group)

    width = middle.shape[1]
    grad_normed = jnp.zeros(middle.shape, F32)
    for m in range(len(up_plans)):
        part = slice(m * width, (m + 1) * width)
        grad_active = dot_nt(grad_down[...], down_w[part, :])
        low = (grad_active * slope[:, part].astype(F32)).astype(BF16)
        grad_hidden[:, part] = low
        hidden_stats[m : m + 1, :] += row_sum(low.astype(F32))
        grad_normed += dot_nt(low, up_w[m])
    unit_rows, inverse = centred_rows(middle)
    sums += [row_sum(grad_normed * unit_rows), row_sum(grad_normed)]
    grad_middle = grad_out + norm_back(grad_normed, unit_rows, inverse, vector(table, LN2_G))
    grad_middle_out[...] = grad_middle
    low = (grad_middle * vector(table, ATTN_S)).astype(BF16)
    grad_branch[...] = low
    sums += [row_sum(grad_middle * branch), row_sum(low.astype(F32))]
    grad_mixed[...] = dot_nt(low, out_w[...]).astype(BF16)
    for at, total in enumerate(sums):
        stats[at : at + 1, :] += total


def back(place, lengths, rows, branch, active, slope, grad_down, cotangent, table, two, three):
    count, width = rows.shape
    hidden_units = active.shape[1]
    plans = (two[1], three[1][0])
    sizes = (len(two[0]), len(three[0]))
    return pl.pallas_call(
        functools.partial(back_kernel, *plans, sizes),
        grid=(count // TILE,),
        in_specs=[SMEM, SMEM]
        + [tile_of(width)] * 2
        + [tile_of(hidden_units)] * 2
        + [tile_of(width)] * 2
        + [whole(table.shape)]
        + [ANY] * sum(sizes),
        out_specs=[tile_of(width), tile_of(hidden_units)]
        + [tile_of(width)] * 3
        + [whole((8, width)), whole((8, width))],
        out_shape=[
            jax.ShapeDtypeStruct(rows.shape, BF16),
            jax.ShapeDtypeStruct(active.shape, BF16),
            jax.ShapeDtypeStruct(rows.shape, F32),
            jax.ShapeDtypeStruct(rows.shape, BF16),
            jax.ShapeDtypeStruct(rows.shape, BF16),
            jax.ShapeDtypeStruct((8, width), F32),
            jax.ShapeDtypeStruct((8, width), F32),
        ],
        scratch_shapes=[
            pltpu.VMEM((width, width), BF16),
            pltpu.VMEM((len(plans[0]) - 1, width, width), BF16),
            pltpu.VMEM((hidden_units, width), BF16),
            pltpu.SemaphoreType.DMA((sum(len(p) for p in plans[0]) + len(plans[1]),)),
        ],
        compiler_params=params(60),
        cost_estimate=cost(26 * count * width * hidden_units // 4, 40 * count * width),
        name="back",
    )(place, lengths, rows, branch, active, slope, grad_down, cotangent, table, *two[0], *three[0])


def outer_kernel(spread, steps, place, *refs):
    pairs = len(steps)
    lefts, rights, refs = refs[:pairs], refs[pairs : 2 * pairs], refs[2 * pairs :]
    flat = refs[-1]
    step = pl.program_id(0)
    first = 0
    for left, count in zip(lefts, steps):

        @pl.when(step == first)
        def _(left=left):
            for at in range(0, flat.shape[0], 128):
                block = left[:, at : at + 128].astype(F32)
                flat[at : at + 128, :] = jnp.transpose(block).astype(BF16)

        first += count

    def put(right):
        value = dot(flat[...], right[...])
        if not spread:
            refs[0][...] = value.astype(BF16)
            return
        mine, theirs, held = refs[:3]
        plane, core = place[0] // 2, place[0] % 2
        held[...] = value
        unit = flat.shape[0] // 8
        for at in range(4):
            one = pl.multiple_of((2 * at + core) * unit, 8)
            other = pl.multiple_of((2 * at + 1 - core) * unit, 8)
            mine[at ^ plane, 0] = held[pl.ds(one, unit), :].astype(BF16)
            theirs[at ^ plane, 0] = held[pl.ds(other, unit), :].astype(BF16)

    first = 0
    for right, count in zip(rights, steps):

        @pl.when((step >= first) & (step < first + count))
        def _(right=right):
            put(right)

        first += count


def outer(place, pairs, width):
    count, height = pairs[0][0].shape
    steps = [right.shape[1] // width for _, right in pairs]
    total = sum(steps)
    right_specs, first = [], 0
    for own in steps:
        right_specs.append(
            pl.BlockSpec(
                (count, width),
                lambda i, first=first, own=own: (0, jnp.clip(i - first, 0, own - 1)),
            )
        )
        first += own
    scratch = [pltpu.VMEM((height, count), BF16)]
    if direct():
        block = pl.BlockSpec((4, 1, height // 8, width), lambda i: (0, i, 0, 0))
        shape = jax.ShapeDtypeStruct((4, total, height // 8, width), BF16)
        specs, shapes = [block, block], [shape, shape]
        scratch = [pltpu.VMEM((height, width), F32)] + scratch
    else:
        specs = pl.BlockSpec((height, width), lambda i: (0, i))
        shapes = jax.ShapeDtypeStruct((height, total * width), BF16)
    return pl.pallas_call(
        functools.partial(outer_kernel, direct(), steps),
        grid=(total,),
        in_specs=[SMEM] + [whole((count, height))] * len(pairs) + right_specs,
        out_specs=specs,
        out_shape=shapes,
        scratch_shapes=scratch,
        compiler_params=params(60),
        cost_estimate=cost(2 * count * height * total * width, 2 * (count + height) * total * width),
        name="outer",
    )(place, *(left for left, _ in pairs), *(right for _, right in pairs))


def plain_kernel(steps, *refs):
    lefts, rights = refs[: len(steps)], refs[len(steps) : -2]
    out, flat = refs[-2:]
    step = pl.program_id(0)
    first, at_right = 0, 0
    for left, counts in zip(lefts, steps):

        @pl.when(step == first)
        def _(left=left):
            for at in range(0, flat.shape[0], 128):
                block = left[:, at : at + 128].astype(F32)
                flat[at : at + 128, :] = jnp.transpose(block).astype(BF16)

        for count in counts:

            @pl.when((step >= first) & (step < first + count))
            def _(right=rights[at_right]):
                out[...] = dot(flat[...], right[...]).astype(BF16).reshape(out.shape)

            first += count
            at_right += 1


def plain_outer(pairs, width):
    count, height = pairs[0][0].shape
    steps = [[right.shape[1] // width for right in rights] for _, rights in pairs]
    total = sum(sum(counts) for counts in steps)
    places = lax.axis_size("wide")
    right_specs, first = [], 0
    for own in sum(steps, []):
        right_specs.append(
            pl.BlockSpec(
                (count, width),
                lambda i, first=first, own=own: (0, jnp.clip(i - first, 0, own - 1)),
            )
        )
        first += own
    if direct():
        spec = pl.BlockSpec((8, 1, height // 8, width), lambda i: (0, i, 0, 0))
        shape = jax.ShapeDtypeStruct((8, total, height // 8, width), BF16)
    else:
        spec = pl.BlockSpec((height, width), lambda i: (0, i))
        shape = jax.ShapeDtypeStruct((height, total * width), BF16)
    out = pl.pallas_call(
        functools.partial(plain_kernel, steps),
        grid=(total,),
        in_specs=[whole((count, height))] * len(pairs) + right_specs,
        out_specs=spec,
        out_shape=shape,
        scratch_shapes=[pltpu.VMEM((height, count), BF16)],
        compiler_params=params(60),
        cost_estimate=cost(2 * count * height * total * width, 2 * (count + height) * total * width),
        name="plain_outer",
    )(*(left for left, _ in pairs), *(right for _, rights in pairs for right in rights))
    if not direct():
        out = out.reshape(places, height // places, total, width).transpose(0, 2, 1, 3)
    return out.reshape(places, -1, width)


def wide_outer_kernel(place, left, right, out, flat):
    @pl.when(pl.program_id(0) == 0)
    def _():
        for at in range(0, flat.shape[0], 128):
            block = left[:, at : at + 128].astype(F32)
            flat[at : at + 128, :] = jnp.transpose(block).astype(BF16)

    value = dot(flat[...], right[...]).astype(BF16)
    half = value.shape[1] // 2
    out[0] = value[:, :half]
    out[1] = value[:, half:]


def wide_outer(place, left, right):
    count, height = left.shape
    columns = right.shape[1]
    steps = 8
    step = columns // steps
    return pl.pallas_call(
        wide_outer_kernel,
        grid=(steps // 2,),
        in_specs=[SMEM, whole(left.shape), pl.BlockSpec((count, 2 * step), lambda i: (0, i))],
        out_specs=pl.BlockSpec((2, height, step), lambda i: (i, 0, 0)),
        out_shape=jax.ShapeDtypeStruct((steps, height, step), BF16),
        scratch_shapes=[pltpu.VMEM((height, count), BF16)],
        compiler_params=params(60),
        cost_estimate=cost(2 * count * height * columns, 2 * (count + height) * (height + columns)),
        name="wide_outer",
    )(place, left, right)


def inputs_kernel(plans, place, rows, grad_middle, grad_q, grad_k, grad_v, table, *refs):
    count = len(refs) - 2 - 2
    sources, (grad_rows, stats, weights, sems) = refs[:count], refs[count:]
    made, first = [], 0
    for m in range(3):
        made.append(copies(place[0], sources, plans[m], weights.at[m], sems, first))
        first += len(plans[m])

    @pl.when(pl.program_id(0) == 0)
    def _():
        for group in made:
            start_all(group)
        stats[...] = jnp.zeros_like(stats)
        for group in made:
            wait_all(group)

    grad = dot_nt(grad_q[...], weights[0])
    grad += dot_nt(grad_k[...], weights[1])
    grad += dot_nt(grad_v[...], weights[2])
    unit_rows, inverse = centred_rows(rows[...].astype(F32))
    grad_rows[...] = grad_middle[...] + norm_back(grad, unit_rows, inverse, vector(table, LN1_G))
    sums = [row_sum(grad * unit_rows), row_sum(grad)]
    sums += [row_sum(grad_q[...].astype(F32)), row_sum(grad_v[...].astype(F32))]
    for at, total in enumerate(sums):
        stats[at : at + 1, :] += total


def inputs_back(place, rows, grad_middle, grad_q, grad_k, grad_v, table, group):
    arrays, plans = group
    count, width = rows.shape
    return pl.pallas_call(
        functools.partial(inputs_kernel, plans),
        grid=(count // TILE,),
        in_specs=[SMEM] + [tile_of(width)] * 5 + [whole(table.shape)] + [ANY] * len(arrays),
        out_specs=[tile_of(width), whole((8, width))],
        out_shape=[
            jax.ShapeDtypeStruct(rows.shape, F32),
            jax.ShapeDtypeStruct((8, width), F32),
        ],
        scratch_shapes=[
            pltpu.VMEM((3, width, width), BF16),
            pltpu.SemaphoreType.DMA((sum(len(p) for p in plans[:3]),)),
        ],
        compiler_params=params(60),
        cost_estimate=cost(6 * count * width * width, 20 * count * width),
        name="inputs_back",
    )(place, rows, grad_middle, grad_q, grad_k, grad_v, table, *arrays)


def add_low(left, right):
    return (left.astype(F32) + right.astype(F32)).astype(left.dtype)


def split_cores(stacked):
    stacked = flip_own(stacked)
    pieces = stacked.reshape((-1, 2) + stacked.shape[1:])
    return pieces[:, 0], pieces[:, 1]


def quarters(held):
    held = held.reshape((-1, 4) + held.shape[1:])
    return tuple(held[:, i] for i in range(4))


def add_kernel(mine, other, own, *halves):
    for quarter in range(4):
        total = (mine[quarter].astype(F32) + other[quarter].astype(F32)).astype(BF16)
        if quarter == 0:
            own[0] = total
            continue
        one, two = halves[2 * quarter - 2], halves[2 * quarter - 1]
        one[0] = total[: one.shape[1]]
        two[0] = total[one.shape[1] :]


def quarters_added(mine, other):
    rows, columns = mine.shape[1:]
    half = rows // 32 * 16
    if not direct():
        own, *rest = quarters(add_low(mine, other))
        return [own] + [(piece[:, :half], piece[:, half:]) for piece in rest]
    shapes = [jax.ShapeDtypeStruct((1, rows, columns), BF16)]
    for _ in range(3):
        shapes.append(jax.ShapeDtypeStruct((1, half, columns), BF16))
        shapes.append(jax.ShapeDtypeStruct((1, rows - half, columns), BF16))
    step = columns // 6
    own, *parts = pl.pallas_call(
        add_kernel,
        grid=(6,),
        in_specs=[pl.BlockSpec((4, rows, step), lambda i: (0, 0, i))] * 2,
        out_specs=[pl.BlockSpec((1, s.shape[1], step), lambda i: (0, 0, i)) for s in shapes],
        out_shape=shapes,
        compiler_params=params(60),
        cost_estimate=cost(4 * rows * columns, 24 * rows * columns),
        name="core_add",
    )(mine, other)
    return own, parts[0:2], parts[2:4], parts[4:6]


def halve(total):
    for bit in reversed(range(3, wide_bits())):
        count = total.shape[0] // 2
        total = add_low(total[:count], cross(total[count:], bit))
    return total[0]


def spread_blocks(stacked):
    size = stacked.shape[0]
    here = lax.axis_index("narrow")
    steps = sorted(range(1, size), key=lambda step: min(step, size - step))
    blocks = [
        lax.dynamic_index_in_dim(stacked, lax.rem(here + step, size), keepdims=False)
        for step in steps
    ]
    return blocks, [lambda v, step=step: shift(v, step) for step in steps]


def add_blocks(stacked, moved):
    total = lax.dynamic_index_in_dim(stacked, lax.axis_index("narrow"), keepdims=False)
    total = total.astype(F32)
    for block in moved:
        total = total + block.astype(F32)
    return total


def column_starts(columns, part, layers):
    starts = [at * part // 128 * 128 for at in range(layers)]
    room = max(-(-(at + 1) * part // 128) * 128 - starts[at] for at in range(layers))
    return [min(start, columns - room) for start in starts], room


def columns_blocks(blocks, part, layers):
    here = lax.axis_index("narrow")
    starts, room = column_starts(blocks.shape[1], part, layers)
    choices = [blocks[:, start : start + room] for start in starts]

    def block_of(index):
        chosen = choices[-1]
        for at in reversed(range(layers - 1)):
            chosen = jnp.where(index == at, choices[at], chosen)
        return chosen

    own, *sends = [block_of(lax.rem(here + step, layers)) for step in range(layers)]
    return own, sends, shifts(layers)


def own_columns(own, moved, part, columns):
    layers = len(moved) + 1
    here = lax.axis_index("narrow")
    starts, _ = column_starts(columns, part, layers)
    total = own.astype(F32)
    for block in moved:
        total = total + block.astype(F32)
    cuts = [total[:, at * part - start : (at + 1) * part - start] for at, start in enumerate(starts)]
    result = cuts[-1]
    for at in reversed(range(layers - 1)):
        result = jnp.where(here == at, cuts[at], result)
    return result


def by_core(grad, parts):
    if direct():
        return tuple(piece.reshape(4, -1, piece.shape[3]) for piece in grad)
    places = lax.axis_size("wide")
    height, columns = grad.shape
    stacked = grad.reshape(places, height // places, parts, columns // parts).transpose(0, 2, 1, 3)
    return split_cores(stacked.reshape(places, -1, columns // parts))


def all_stages():
    stages = []
    for bit in range(lax.axis_size("narrow").bit_length() - 1):
        stages.append(lambda v, bit=bit: exchange(v, "narrow", lambda i: i ^ (1 << bit)))
    for bit in reversed(range(wide_bits())):
        stages.append(lambda v, bit=bit: cross(v, bit))
    return stages


def own_spot(places, layers, piece, width):
    start = (lax.axis_index("wide") * layers + lax.axis_index("narrow")) * piece
    return start // width, start % width


def shards(
    patches, lengths, w_qkv, w_out, w_up, w_down, ln1_gain, ln1_bias, q_bias, v_bias, out_bias, attn_scale,
    ln2_gain, ln2_bias, up_bias, down_bias, mlp_scale, cotangent,
):
    places, layers = lax.axis_size("wide"), lax.axis_size("narrow")
    place = lax.axis_index("wide").astype(jnp.int32).reshape(1)
    short, width = w_up.shape
    part = w_qkv.shape[1]
    quarter = w_out.shape[1]
    packs, pack_rows, _ = patches.shape
    rows = patches.reshape(-1, width)
    cotangent = cotangent.reshape(-1, width)

    small = [ln1_gain, ln1_bias, q_bias, v_bias, out_bias, attn_scale, ln2_gain, ln2_bias, down_bias, mlp_scale]
    piece, long = ln1_gain.shape[0], up_bias.shape[0]
    small_spot = own_spot(places, layers, piece, width)
    up_spot = own_spot(places, layers, long, width)
    stages = all_stages()

    def spread_table(table, stages):
        for stage in stages:
            table = table + stage(table)
        return table

    extra = jnp.pad(jnp.stack(small), ((0, 0), (0, part - piece)))
    extra = jnp.concatenate([extra, jnp.pad(up_bias[None], ((0, 5), (0, part - long)))])
    early = jnp.concatenate([w_qkv, extra])

    moved = [move(early) for move in shifts(layers)]
    one = by_origin([early, *moved])
    extra = side_by_side(one[:, short : short + 10, :piece])
    extra = jnp.pad(extra, ((0, 6), (0, width - layers * piece)))
    long_row = side_by_side(one[:, short + 10 : short + 11, :long])
    long_row = jnp.pad(long_row, ((10, 5), (0, width - layers * long)))
    one = side_by_side(one[:, :short])
    one = jnp.concatenate([*jnp.split(one, 3, axis=1), extra + long_row])
    held = double(one)
    up_out = jnp.concatenate([w_up, w_out], axis=1)
    sends = [held, held] + [up_out] * (layers - 1)
    (up_out,), (near, far, *two) = beside(lambda v: v, (up_out,), sends, planes() + shifts(layers))
    half = near.shape[1] // 32 * 16
    sends = [near[:, :half], far[:, half:], jnp.concatenate([held, near, far])]
    two = by_origin([up_out, *two])
    two = jnp.concatenate([two[:, :, :width].reshape(-1, width), side_by_side(two[:, :, width:])])
    two, sends = lax.optimization_barrier((two, sends))
    two = in_order(lax.all_gather(two, "wide"), layers + 1)
    moves = corners() + [lambda v: cross(v, 0)]
    moved = lax.optimization_barrier([move(send) for move, send in zip(moves, sends)])
    planes_one = held, near, far, jnp.concatenate(moved[:2], axis=1)
    one, extras = matrices(planes_one, (moved[2], cross(planes_one[3], 0)), 3, layers * piece, layers * long)
    side_down = jnp.concatenate(jnp.split(w_down, layers, axis=0), axis=1)

    (normed, query, key, value, table), three = beside(
        lambda v: project(place, v, extras, one), rows, [side_down] * (layers - 1), shifts(layers)
    )
    three = by_origin([side_down, *three])
    three = jnp.concatenate(
        [side_by_side(three[:, :, i * quarter : (i + 1) * quarter]) for i in range(layers)]
    )
    query, three = lax.optimization_barrier((query, three))
    three = in_order(lax.all_gather(three, "wide"), 1)
    attention = attend(lengths, query, key, value, 0)
    for pack in range(1, packs):
        attention = attend(lengths, query, key, value, pack, attention)
    mixed, log_total = attention
    branch, normed_two, active, slope, grad_down = hidden(
        place, lengths, rows, mixed, cotangent, table, two
    )
    grad_w_down = wide_outer(place, grad_down, active)
    active = after(active, grad_w_down)
    if places != 8:
        grad_w_down = grad_w_down.reshape(8, width, places // 8, -1).transpose(0, 2, 1, 3)
    total_down = lax.psum_scatter(grad_w_down.reshape(places, width, -1), "wide")

    result, grad_hidden, grad_middle, grad_branch, grad_mixed, stats_two, hidden_stats = back(
        place, lengths, rows, branch, active, slope, grad_down, cotangent, table, two, three
    )
    mine, theirs = by_core(
        outer(place, [(normed_two, grad_hidden), (mixed, grad_branch)], width), layers + 1
    )
    grads, (other,) = beside(
        lambda v: attend_back(lengths, query, key, value, v, log_total, 0),
        grad_mixed,
        [theirs],
        [lambda v: cross(v, 0)],
    )
    own_up, near, far, corner = quarters_added(mine, other)
    for pack in range(1, packs):
        run = functools.partial(attend_back, lengths, query, key, value, grad_mixed, log_total, pack)
        if pack == packs - 1:
            sends = [corner[0], corner[1], near[0], far[1]]
            grads, moved = beside(run, grads, sends, planes() + planes())
        else:
            grads = run(grads)
    near_one, far_two = moved[2:]
    sends = [add_low(near[1], moved[1]), add_low(far[0], moved[0])]
    grads, sends = lax.optimization_barrier((grads, sends))
    grad_w_qkv, (near_two, far_one) = beside(
        lambda v: plain_outer([(normed, v)], width), grads, sends, planes()
    )
    total_qkv = lax.psum_scatter(grad_w_qkv, "wide")
    own_up = own_up.astype(F32) + jnp.concatenate([near_one, near_two], axis=1).astype(F32)
    own_up = own_up + jnp.concatenate([far_one, far_two], axis=1).astype(F32)
    total_up = halve(own_up.astype(BF16))
    total_out = total_up[layers * short :].reshape(short, layers, quarter).transpose(1, 0, 2)
    total_up = total_up[: layers * short].reshape(layers, short, width)
    total_up = jnp.concatenate([total_up, total_out], axis=2)
    total_down = total_down.reshape(layers, quarter, -1)
    sends, moves = spread_blocks(total_up)
    down_sends, down_moves = spread_blocks(total_down)
    grad_q, grad_k, grad_v = grads
    (grad_rows, stats_one), moved = beside(
        lambda v: inputs_back(place, rows, grad_middle, v, grad_k, grad_v, table, one),
        grad_q,
        sends + down_sends,
        moves + down_moves,
    )
    up_parts, down_parts = moved[: len(sends)], moved[len(sends) :]
    total_up = add_blocks(total_up, up_parts)
    total_down = add_blocks(total_down, down_parts).T
    sums = spread_table(jnp.concatenate([stats_one, stats_two, hidden_stats]), stages[2:])
    total_qkv = after(total_qkv, sums)
    blocks = jnp.concatenate([total_qkv[i * short : (i + 1) * short] for i in range(3)], axis=1)
    own_block, sends, moves = columns_blocks(blocks, part, layers)
    sums, moved = beside(lambda v: spread_table(v, stages[:2]), sums, sends, moves)
    total_qkv = own_columns(own_block, moved, part, blocks.shape[1])

    own = lax.dynamic_slice(sums, (0, small_spot[1]), (16, ln1_gain.shape[0]))
    own_up = lax.dynamic_slice(sums, (16 + up_spot[0], up_spot[1]), (1, up_bias.shape[0]))[0]
    return (
        result.reshape(patches.shape),
        grad_rows.reshape(patches.shape),
        total_qkv,
        total_up[:, width:],
        total_up[:, :width],
        total_down,
        own[0],
        own[1],
        own[2],
        own[3],
        own[13],
        own[12],
        own[10],
        own[11],
        own_up,
        own[9],
        own[8],
    )


def solution(mesh):
    return jax.shard_map(
        shards,
        mesh=mesh,
        in_specs=(
            P(("wide", "narrow"), None, None),
            P(("wide", "narrow"), None),
            P("wide", "narrow"),
            P("wide", "narrow"),
            P("wide", "narrow"),
            P("wide", "narrow"),
            P(("wide", "narrow")),
            P(("wide", "narrow")),
            P(("wide", "narrow")),
            P(("wide", "narrow")),
            P(("wide", "narrow")),
            P(("wide", "narrow")),
            P(("wide", "narrow")),
            P(("wide", "narrow")),
            P(("wide", "narrow")),
            P(("wide", "narrow")),
            P(("wide", "narrow")),
            P(("wide", "narrow"), None, None),
        ),
        out_specs=(
            P(("wide", "narrow"), None, None),
            P(("wide", "narrow"), None, None),
            P("wide", "narrow"),
            P("wide", "narrow"),
            P("wide", "narrow"),
            P("wide", "narrow"),
            P(("wide", "narrow")),
            P(("wide", "narrow")),
            P(("wide", "narrow")),
            P(("wide", "narrow")),
            P(("wide", "narrow")),
            P(("wide", "narrow")),
            P(("wide", "narrow")),
            P(("wide", "narrow")),
            P(("wide", "narrow")),
            P(("wide", "narrow")),
            P(("wide", "narrow")),
        ),
        check_vma=False,
    )
```

```python
import functools
import math

import jax
import jax.numpy as jnp
from jax import lax
from jax.experimental import pallas as pl
from jax.experimental.pallas import tpu as pltpu
from jax.sharding import PartitionSpec as P

HD = 64
LN_EPSILON = 1e-06
MASKED = -1e30
TILE = 256
F32 = jnp.float32
BF16 = jnp.bfloat16
MIB = 1 << 20


def exchange(value, axis_name, partner):
    size = lax.axis_size(axis_name)
    return lax.ppermute(value, axis_name, [(i, partner(i) % size) for i in range(size)])


def cross(value, bit):
    return exchange(value, "wide", lambda i: i ^ (1 << bit))


def shift(value, step):
    return exchange(value, "narrow", lambda i: i + step)


def wide_bits():
    return lax.axis_size("wide").bit_length() - 1


def by_origin(pieces):
    size = len(pieces)
    backward = jnp.stack(pieces[::-1])
    twice = jnp.concatenate([backward, backward])
    return lax.dynamic_slice_in_dim(twice, size - 1 - lax.axis_index("narrow"), size)


def flip_own(stacked):
    here = lax.axis_index("wide")
    size = stacked.shape[0]
    for bit in range(size.bit_length() - 1):
        halves = stacked.reshape((size >> (bit + 1), 2, 1 << bit) + stacked.shape[1:])
        halves = jnp.where((here >> bit) & 1, halves[:, ::-1], halves)
        stacked = halves.reshape(stacked.shape)
    return stacked


def after(value, *others):
    return lax.optimization_barrier((value, others))[0]


def beside(run, value, sends, moves):
    value, sends = lax.optimization_barrier((value, sends))
    moved = [move(send) for move, send in zip(moves, sends, strict=True)]
    return lax.optimization_barrier((run(value), moved))


def beside_loose(run, value, sends, moves):
    return beside(run, value, sends, moves)


def planes():
    return [lambda v: cross(v, 1), lambda v: cross(v, 2)]


def corners():
    return [lambda v: cross(v, 2), lambda v: cross(v, 1)]


def shifts(layers):
    return [lambda v, step=step: shift(v, step) for step in range(1, layers)]


def double(block):
    held = block[None]
    for bit in range(3, wide_bits()):
        held = jnp.concatenate([held, cross(held, bit)])
    return held


def side_by_side(stacked):
    return jnp.concatenate([stacked[i] for i in range(stacked.shape[0])], axis=1)


def direct():
    return lax.axis_size("wide") == 8


def in_order(stacked, parts):
    places, rows, columns = stacked.shape
    unit = rows // parts
    if parts == 1 or not direct():
        stacked = stacked.reshape(places, parts, unit, columns)
        arrays = [stacked[:, m].reshape(-1, columns) for m in range(parts)]
        return arrays, [[(m, 0, 0, None, unit)] for m in range(parts)]
    return [stacked], [[(0, at, m * unit, at, -unit) for at in range(places)] for m in range(parts)]


def matrices(planes, cores, parts, short, long):
    unit = (planes[0].shape[1] - 16) // parts
    behind = parts * unit
    if not direct():
        other = [*jnp.split(cores[0], 3), cores[1]]
        stacked = jnp.stack([jnp.stack(pair, axis=1) for pair in zip(planes, other)], axis=1)
        stacked = flip_own(stacked.reshape((-1,) + planes[0].shape[1:]))
        width = stacked.shape[2]
        rows = stacked[:, behind:].transpose(1, 0, 2)
        table = rows[:10, :, :short].reshape(10, width)
        up = rows[10, :, :long].reshape(-1, width)
        table = jnp.concatenate([table, up])
        table = jnp.pad(table, ((0, 16 - table.shape[0]), (0, 0)))
        stacked = stacked[:, :behind].reshape(stacked.shape[0], parts, unit, -1)
        arrays = [stacked[:, m].reshape(-1, stacked.shape[3]) for m in range(parts)]
        plans = [[(m, 0, 0, None, unit)] for m in range(parts)]
        return (arrays, plans), (table, None)
    spots = [(0, 0, 0), (1, 0, 2), (2, 0, 4), (3, 0, 6), (4, 0, 1), (4, 1, 3), (4, 2, 5), (5, 0, 7)]
    plans = [[(at, index, m * unit, rel, unit) for at, index, rel in spots] for m in range(parts)]
    return ([*planes, *cores], plans), (None, (spots, behind, short, long))


def copies(place, refs, plan, target, sems, first):
    made = []
    for at, index, row, rel, unit in plan:
        sem = sems.at[first + len(made)]
        if rel is None:
            made.append(pltpu.make_async_copy(refs[at], target, sem))
        else:
            start = -rel * unit if unit < 0 else pl.multiple_of((place ^ rel) * unit, 16)
            unit = abs(unit)
            source = refs[at].at[index, pl.ds(row, unit)]
            made.append(pltpu.make_async_copy(source, target.at[pl.ds(start, unit)], sem))
    return made


def start_all(made):
    for copy in made:
        copy.start()


def wait_all(made):
    for copy in made:
        copy.wait()


def dot(left, right):
    return lax.dot_general(left, right, (((1,), (0,)), ((), ())), preferred_element_type=F32)


def dot_nt(left, right):
    return lax.dot_general(left, right, (((1,), (1,)), ((), ())), preferred_element_type=F32)


def centred_rows(values):
    row_mean = jnp.mean(values, axis=-1, keepdims=True)
    centred = values - row_mean
    row_var = jnp.mean(centred * centred, axis=-1, keepdims=True)
    inverse = lax.rsqrt(row_var + LN_EPSILON)
    return centred * inverse, inverse


def norm_back(grad, unit_rows, inverse, gain):
    scaled = grad * gain
    mean_one = jnp.mean(scaled, axis=-1, keepdims=True)
    mean_two = jnp.mean(scaled * unit_rows, axis=-1, keepdims=True)
    return (scaled - mean_one - unit_rows * mean_two) * inverse


def row_sum(values):
    return jnp.sum(values, axis=0, keepdims=True)


def gelu_pair(values):
    bell = jnp.exp(values * values * -0.5)
    share = 0.5 + 0.5 * lax.erf(values * math.sqrt(0.5))
    return values * share, share + values * bell * (1.0 / math.sqrt(2.0 * math.pi))


ANY = pl.BlockSpec(memory_space=pl.ANY)
SMEM = pl.BlockSpec(memory_space=pltpu.SMEM)


def whole(shape):
    return pl.BlockSpec(shape, lambda *_: (0,) * len(shape))


def tile_of(columns):
    return pl.BlockSpec((TILE, columns), lambda i: (i, 0))


def cost(flops, moved, exps=0):
    return pl.CostEstimate(flops=flops, bytes_accessed=moved, transcendentals=exps)


def params(mib, dims=1):
    return pltpu.CompilerParams(
        vmem_limit_bytes=mib * MIB, dimension_semantics=("arbitrary",) * dims
    )


LN1_G, LN1_B, Q_B, V_B, OUT_B, ATTN_S, LN2_G, LN2_B, DOWN_B, MLP_S, UP_B = range(11)


def vector(table, row):
    return table[row : row + 1, :]


def make_table(place, pieces, layout):
    spots, _, short, long = layout
    shape = pieces.shape[1:]
    lane = lax.broadcasted_iota(jnp.int32, shape, 1)
    row = lax.broadcasted_iota(jnp.int32, shape, 0)
    table = jnp.zeros(shape, F32)
    for at, (_, _, rel) in enumerate(spots):
        spot = place ^ rel
        piece = pieces[at].astype(F32)
        table += pltpu.roll(jnp.where((row < UP_B) & (lane < short), piece, 0.0), spot * short, 1)
        start = spot * long
        up = jnp.where(lane[:1] < long, piece[UP_B : UP_B + 1], 0.0)
        up = pltpu.roll(jnp.broadcast_to(up, shape), lax.rem(start, shape[1]), 1)
        table += jnp.where(row == UP_B + start // shape[1], up, 0.0)
    return table


def project_kernel(plans, layout, place, rows, extras, *refs):
    count = len(refs) - 5 - 4
    sources, refs = refs[:count], refs[count:]
    normed, query, key, value, table, weights, pieces, sems, piece_sems = refs
    made, first = [], 0
    for m in range(3):
        made.append(copies(place[0], sources, plans[m], weights.at[m], sems, first))
        first += len(plans[m])

    @pl.when(pl.program_id(0) == 0)
    def _():
        for group in made:
            start_all(group)
        if layout is None:
            table[...] = extras[...].astype(F32)
            return
        brought = []
        for at, (source, index, _) in enumerate(layout[0]):
            piece = sources[source].at[index, pl.ds(layout[1], 16)]
            brought.append(pltpu.make_async_copy(piece, pieces.at[at], piece_sems.at[at]))
        start_all(brought)
        wait_all(brought)
        table[...] = make_table(place[0], pieces, layout)

    unit_rows, _ = centred_rows(rows[...].astype(F32))
    low = (unit_rows * vector(table, LN1_G) + vector(table, LN1_B)).astype(BF16)
    normed[...] = low

    @pl.when(pl.program_id(0) == 0)
    def _():
        for group in made:
            wait_all(group)

    query[...] = ((dot(low, weights[0]) + vector(table, Q_B)) * 0.125).astype(BF16)
    key[...] = dot(low, weights[1]).astype(BF16)
    value[...] = (dot(low, weights[2]) + vector(table, V_B)).astype(BF16)


def project(place, rows, extras, group):
    arrays, plans = group
    extras, layout = extras
    count, width = rows.shape
    if extras is None:
        extras = jnp.zeros((16, width), BF16)
    return pl.pallas_call(
        functools.partial(project_kernel, plans, layout),
        grid=(count // TILE,),
        in_specs=[SMEM, tile_of(width), whole(extras.shape)] + [ANY] * len(arrays),
        out_specs=[tile_of(width)] * 4 + [whole((16, width))],
        out_shape=[jax.ShapeDtypeStruct(rows.shape, BF16)] * 4
        + [jax.ShapeDtypeStruct((16, width), F32)],
        scratch_shapes=[
            pltpu.VMEM((3, width, width), BF16),
            pltpu.VMEM((8, 16, width), BF16),
            pltpu.SemaphoreType.DMA((sum(len(p) for p in plans[:3]),)),
            pltpu.SemaphoreType.DMA((8,)),
        ],
        compiler_params=params(60),
        cost_estimate=cost(6 * count * width * width, 14 * count * width),
        name="project",
    )(place, rows, extras, *arrays)


def segments(lengths, pack, position):
    end, segment = 0, jnp.zeros_like(position)
    for slot in range(lengths.shape[1] - 1):
        end = end + lengths[pack, slot]
        segment = segment + (position >= end).astype(jnp.int32)
    return jnp.where(position < end, segment, lengths.shape[1] + position)


def same_segment(lengths, pack, rows):
    down = lax.broadcasted_iota(jnp.int32, (rows, 128), 0)
    along = lax.broadcasted_iota(jnp.int32, (1, rows), 1)
    column = segments(lengths, pack, down)
    row = segments(lengths, pack, along)
    return jnp.concatenate([column] * (rows // 128), axis=1) == row


def head_lanes(shape, head):
    lane = lax.broadcasted_iota(jnp.int32, shape, 1)
    return (lane < HD) if head == 0 else (lane >= HD)


def only(values, head):
    return jnp.where(head_lanes(values.shape, head), values, jnp.zeros_like(values))


def attend_kernel(pack, lengths, query, key, value, *refs):
    attended, kept = refs[-2:]
    rows = query.shape[0]
    same = same_segment(lengths, pack, rows)
    flat = jnp.transpose(value[...].astype(F32)).astype(BF16)
    mixed = []
    for head in range(2):
        scores = dot_nt(key[...], only(query[...], head))
        scores = jnp.where(same, scores, MASKED)
        top = jnp.max(scores, axis=0, keepdims=True)
        powers = jnp.exp(scores - top)
        total = jnp.sum(powers, axis=0, keepdims=True)
        weights = (powers * (1.0 / total)).astype(BF16)
        mixed.append(dot(flat[head * HD : (head + 1) * HD], weights))
        kept[head] = weights
    attended[...] = jnp.transpose(jnp.concatenate(mixed, axis=0)).astype(BF16)


def pair_block(rows, pack):
    return pl.BlockSpec((rows, 2 * HD), lambda h: (pack, h))


def kept_block(rows):
    return pl.BlockSpec((2, rows, rows), lambda h: (h, 0, 0))


def attend(lengths, query, key, value, pack, earlier=()):
    packs = lengths.shape[0]
    count, width = query.shape
    rows, pairs = count // packs, width // (2 * HD)
    return pl.pallas_call(
        functools.partial(attend_kernel, pack),
        grid=(pairs,),
        in_specs=[SMEM] + [pair_block(rows, pack)] * 3 + [ANY] * len(earlier),
        out_specs=[pair_block(rows, pack), kept_block(rows)],
        out_shape=[
            jax.ShapeDtypeStruct(query.shape, BF16),
            jax.ShapeDtypeStruct((2 * pairs, rows, rows), BF16),
        ],
        input_output_aliases={4 + i: i for i in range(len(earlier))},
        compiler_params=params(60),
        cost_estimate=cost(16 * rows * rows * width, 8 * rows * width) if earlier else cost(0, 0),
        name="attend",
    )(lengths, query, key, value, *earlier)


def attend_back_kernel(query, key, value, grad, kept, *refs):
    grad_q, grad_k, grad_v = refs[-3:]
    flat_key = jnp.transpose(key[...].astype(F32)).astype(BF16)
    by_query, by_key, by_value = [], [], []
    for head in range(2):
        weights = kept[head]
        probs = weights.astype(F32)
        by_value.append(dot(weights, grad[...]))
        grad_probs = dot_nt(value[...], only(grad[...], head))
        centre = jnp.sum(grad_probs * probs, axis=0, keepdims=True)
        grad_scores = (probs * (grad_probs - centre)).astype(BF16)
        by_key.append(dot(grad_scores, query[...]))
        by_query.append(dot(flat_key[head * HD : (head + 1) * HD], grad_scores))
    lanes = head_lanes(by_key[0].shape, 0)
    grad_k[...] = jnp.where(lanes, by_key[0], by_key[1]).astype(BF16)
    grad_v[...] = jnp.where(lanes, by_value[0], by_value[1]).astype(BF16)
    grad_q[...] = jnp.transpose(jnp.concatenate(by_query, axis=0)).astype(BF16) * 0.125


def attend_back(query, key, value, grad, kept, pack, earlier=()):
    pairs, rows = kept.shape[0] // 2, kept.shape[1]
    width = query.shape[1]
    return pl.pallas_call(
        attend_back_kernel,
        grid=(pairs,),
        in_specs=[pair_block(rows, pack)] * 4 + [kept_block(rows)] + [ANY] * len(earlier),
        out_specs=[pair_block(rows, pack)] * 3,
        out_shape=[jax.ShapeDtypeStruct(query.shape, BF16)] * 3,
        input_output_aliases={5 + i: i for i in range(len(earlier))},
        compiler_params=params(60),
        cost_estimate=cost(32 * rows * rows * width, 14 * rows * width, 0),
        name="attend_back",
    )(query, key, value, grad, kept, *earlier)


def live_rows(lengths, shape):
    tiles = pl.num_programs(0) // lengths.shape[0]
    step = pl.program_id(0)
    pack = step // tiles
    end = 0
    for slot in range(lengths.shape[1] - 1):
        end = end + lengths[pack, slot]
    position = lax.broadcasted_iota(jnp.int32, shape, 0) + (step - pack * tiles) * shape[0]
    return position < end


def hidden_kernel(out_plan, up_plans, sizes, place, lengths, rows, mixed, cotangent, table, *refs):
    sources, refs = refs[: sum(sizes)], refs[sum(sizes) :]
    one, two = sources[: sizes[0]], sources[sizes[0] :]
    branch_out, normed, active, slope, grad_down, out_w, up_w, sems = refs
    made = [copies(place[0], one, out_plan, out_w, sems, 0)]
    first = len(out_plan)
    for m, plan in enumerate(up_plans):
        made.append(copies(place[0], two, plan, up_w.at[m], sems, first))
        first += len(plan)

    @pl.when(pl.program_id(0) == 0)
    def _():
        for group in made:
            start_all(group)
        wait_all(made[0])

    branch = dot(mixed[...], out_w[...]) + vector(table, OUT_B)
    branch_out[...] = branch
    middle = rows[...].astype(F32) + vector(table, ATTN_S) * branch
    unit_rows, _ = centred_rows(middle)
    low = (unit_rows * vector(table, LN2_G) + vector(table, LN2_B)).astype(BF16)
    normed[...] = low
    live = live_rows(lengths, cotangent.shape)
    grad_out = jnp.where(live, cotangent[...].astype(F32), 0.0)
    grad_down[...] = (grad_out * vector(table, MLP_S)).astype(BF16)

    width = low.shape[1]
    for m in range(len(up_plans)):

        @pl.when(pl.program_id(0) == 0)
        def _(m=m):
            wait_all(made[m + 1])

        part = slice(m * width, (m + 1) * width)
        up = dot(low, up_w[m]) + vector(table, UP_B + m)
        value, rate = gelu_pair(up)
        active[:, part] = value.astype(BF16)
        slope[:, part] = rate.astype(BF16)


def hidden(place, lengths, rows, mixed, cotangent, table, group_one, group_two):
    count, width = rows.shape
    hidden_units = width * len(group_two[1])
    out_plan, up_plans = group_one[1][3], group_two[1]
    sizes = (len(group_one[0]), len(group_two[0]))
    return pl.pallas_call(
        functools.partial(hidden_kernel, out_plan, up_plans, sizes),
        grid=(count // TILE,),
        in_specs=[SMEM, SMEM]
        + [tile_of(width)] * 3
        + [whole(table.shape)]
        + [ANY] * sum(sizes),
        out_specs=[tile_of(width)] * 2 + [tile_of(hidden_units)] * 2 + [tile_of(width)],
        out_shape=[
            jax.ShapeDtypeStruct(rows.shape, F32),
            jax.ShapeDtypeStruct(rows.shape, BF16),
            jax.ShapeDtypeStruct((count, hidden_units), BF16),
            jax.ShapeDtypeStruct((count, hidden_units), BF16),
            jax.ShapeDtypeStruct(rows.shape, BF16),
        ],
        scratch_shapes=[
            pltpu.VMEM((width, width), BF16),
            pltpu.VMEM((len(up_plans), width, width), BF16),
            pltpu.SemaphoreType.DMA((len(out_plan) + sum(len(p) for p in up_plans),)),
        ],
        compiler_params=params(60),
        cost_estimate=cost(14 * count * width * hidden_units // 4, 26 * count * width, 2 * count * hidden_units),
        name="hidden",
    )(place, lengths, rows, mixed, cotangent, table, *group_one[0], *group_two[0])


STATS_TWO = 7


def back_kernel(
    out_plan, up_plans, down_plan, sizes, place, lengths, rows, branch_in, active, slope, grad_down, cotangent,
    table, *refs,
):
    sources, refs = refs[: sum(sizes)], refs[sum(sizes) :]
    one, two = sources[: sizes[0]], sources[sizes[0] : sizes[0] + sizes[1]]
    three = sources[sizes[0] + sizes[1] :]
    result, grad_hidden, grad_middle_out, grad_branch, grad_mixed, stats, hidden_stats = refs[:7]
    out_w, up_w, down_w, sems = refs[7:]
    made = [copies(place[0], three, down_plan, down_w, sems, 0)]
    first = len(down_plan)
    for m, plan in enumerate(up_plans):
        made.append(copies(place[0], two, plan, up_w.at[m], sems, first))
        first += len(plan)
    made.append(copies(place[0], one, out_plan, out_w, sems, first))

    @pl.when(pl.program_id(0) == 0)
    def _():
        for group in made:
            start_all(group)
        stats[...] = jnp.zeros_like(stats)
        hidden_stats[...] = jnp.zeros_like(hidden_stats)
        wait_all(made[0])

    live = live_rows(lengths, cotangent.shape)
    branch = branch_in[...]
    middle = rows[...].astype(F32) + vector(table, ATTN_S) * branch
    down_out = dot(active[...], down_w[...]) + vector(table, DOWN_B)
    result[...] = jnp.where(live, middle + vector(table, MLP_S) * down_out, 0.0).astype(BF16)
    grad_out = jnp.where(live, cotangent[...].astype(F32), 0.0)
    sums = [row_sum(grad_out * down_out), row_sum(grad_down[...].astype(F32))]

    @pl.when(pl.program_id(0) == 0)
    def _():
        for group in made[1:]:
            wait_all(group)

    width = middle.shape[1]
    grad_normed = jnp.zeros(middle.shape, F32)
    for m in range(len(up_plans)):
        part = slice(m * width, (m + 1) * width)
        grad_active = dot_nt(grad_down[...], down_w[part, :])
        low = (grad_active * slope[:, part].astype(F32)).astype(BF16)
        grad_hidden[:, part] = low
        hidden_stats[m : m + 1, :] += row_sum(low.astype(F32))
        grad_normed += dot_nt(low, up_w[m])
    unit_rows, inverse = centred_rows(middle)
    sums += [row_sum(grad_normed * unit_rows), row_sum(grad_normed)]
    grad_middle = grad_out + norm_back(grad_normed, unit_rows, inverse, vector(table, LN2_G))
    grad_middle_out[...] = grad_middle
    low = (grad_middle * vector(table, ATTN_S)).astype(BF16)
    grad_branch[...] = low
    sums += [row_sum(grad_middle * branch), row_sum(low.astype(F32))]
    grad_mixed[...] = dot_nt(low, out_w[...]).astype(BF16)
    for at, total in enumerate(sums):
        stats[at : at + 1, :] += total


def back(place, lengths, rows, branch, active, slope, grad_down, cotangent, table, one, two, three):
    count, width = rows.shape
    hidden_units = active.shape[1]
    plans = (one[1][3], two[1], three[1][0])
    sizes = (len(one[0]), len(two[0]), len(three[0]))
    return pl.pallas_call(
        functools.partial(back_kernel, *plans, sizes),
        grid=(count // TILE,),
        in_specs=[SMEM, SMEM]
        + [tile_of(width)] * 2
        + [tile_of(hidden_units)] * 2
        + [tile_of(width)] * 2
        + [whole(table.shape)]
        + [ANY] * sum(sizes),
        out_specs=[tile_of(width), tile_of(hidden_units)]
        + [tile_of(width)] * 3
        + [whole((8, width)), whole((8, width))],
        out_shape=[
            jax.ShapeDtypeStruct(rows.shape, BF16),
            jax.ShapeDtypeStruct(active.shape, BF16),
            jax.ShapeDtypeStruct(rows.shape, F32),
            jax.ShapeDtypeStruct(rows.shape, BF16),
            jax.ShapeDtypeStruct(rows.shape, BF16),
            jax.ShapeDtypeStruct((8, width), F32),
            jax.ShapeDtypeStruct((8, width), F32),
        ],
        scratch_shapes=[
            pltpu.VMEM((width, width), BF16),
            pltpu.VMEM((len(plans[1]), width, width), BF16),
            pltpu.VMEM((hidden_units, width), BF16),
            pltpu.SemaphoreType.DMA(
                (len(plans[0]) + sum(len(p) for p in plans[1]) + len(plans[2]),)
            ),
        ],
        compiler_params=params(60),
        cost_estimate=cost(26 * count * width * hidden_units // 4, 40 * count * width),
        name="back",
    )(place, lengths, rows, branch, active, slope, grad_down, cotangent, table, *one[0], *two[0], *three[0])


def outer_kernel(spread, steps, place, *refs):
    lefts, refs = refs[: len(steps)], refs[len(steps) :]
    count = sum(len(own) for own in steps)
    rights, refs = refs[:count], refs[count:]
    flat = refs[-1]
    step = pl.program_id(0)

    def put(right):
        value = dot(flat[...], right[...])
        if not spread:
            refs[0][...] = value.astype(BF16)
            return
        mine, theirs = refs[:2]
        unit = flat.shape[0] // 8
        value = value.astype(BF16)
        for at in range(4):
            mine[at, 0] = value[2 * at * unit : (2 * at + 1) * unit]
            theirs[at, 0] = value[(2 * at + 1) * unit : (2 * at + 2) * unit]

    first, at_right = 0, 0
    for left, own in zip(lefts, steps):

        @pl.when(step == first)
        def _(left=left):
            for at in range(0, flat.shape[0], 128):
                block = left[:, at : at + 128].astype(F32)
                turned = jnp.transpose(block).astype(BF16)
                if spread:
                    refs[2][at : at + 128, :] = turned
                else:
                    flat[at : at + 128, :] = turned
            if spread:
                unit = flat.shape[0] // 8
                for rel in range(8):
                    start = pl.multiple_of((place[0] ^ rel) * unit, 16)
                    flat[rel * unit : (rel + 1) * unit, :] = refs[2][pl.ds(start, unit), :]

        for count in own:

            @pl.when((step >= first) & (step < first + count))
            def _(right=rights[at_right]):
                put(right)

            first += count
            at_right += 1


def outer(place, pairs, width):
    count, height = pairs[0][0].shape
    steps = [[right.shape[1] // width for right in rights] for _, rights in pairs]
    total = sum(sum(own) for own in steps)
    right_specs, first = [], 0
    for own in sum(steps, []):
        right_specs.append(
            pl.BlockSpec(
                (count, width),
                lambda i, first=first, own=own: (0, jnp.clip(i - first, 0, own - 1)),
            )
        )
        first += own
    scratch = [pltpu.VMEM((height, count), BF16)]
    if direct():
        block = pl.BlockSpec((4, 1, height // 8, width), lambda i: (0, i, 0, 0))
        shape = jax.ShapeDtypeStruct((4, total, height // 8, width), BF16)
        specs, shapes = [block, block], [shape, shape]
        scratch = scratch * 2
    else:
        specs = pl.BlockSpec((height, width), lambda i: (0, i))
        shapes = jax.ShapeDtypeStruct((height, total * width), BF16)
    return pl.pallas_call(
        functools.partial(outer_kernel, direct(), steps),
        grid=(total,),
        in_specs=[SMEM] + [whole((count, height))] * len(pairs) + right_specs,
        out_specs=specs,
        out_shape=shapes,
        scratch_shapes=scratch,
        compiler_params=params(60),
        cost_estimate=cost(2 * count * height * total * width, 2 * (count + height) * total * width),
        name="outer",
    )(place, *(left for left, _ in pairs), *(right for _, rights in pairs for right in rights))


def wide_outer_kernel(place, left, right, out, flat):
    @pl.when(pl.program_id(0) == 0)
    def _():
        for at in range(0, flat.shape[0], 128):
            block = left[:, at : at + 128].astype(F32)
            flat[at : at + 128, :] = jnp.transpose(block).astype(BF16)

    value = dot(flat[...], right[...]).astype(BF16)
    half = value.shape[1] // 2
    out[0] = value[:, :half]
    out[1] = value[:, half:]


def wide_outer(place, left, right):
    count, height = left.shape
    columns = right.shape[1]
    steps = 8
    step = columns // steps
    return pl.pallas_call(
        wide_outer_kernel,
        grid=(steps // 2,),
        in_specs=[SMEM, whole(left.shape), pl.BlockSpec((count, 2 * step), lambda i: (0, i))],
        out_specs=pl.BlockSpec((2, height, step), lambda i: (i, 0, 0)),
        out_shape=jax.ShapeDtypeStruct((steps, height, step), BF16),
        scratch_shapes=[pltpu.VMEM((height, count), BF16)],
        compiler_params=params(60),
        cost_estimate=cost(2 * count * height * columns, 2 * (count + height) * (height + columns)),
        name="wide_outer",
    )(place, left, right)


def inputs_kernel(plans, place, rows, grad_middle, grad_q, grad_k, grad_v, table, *refs):
    count = len(refs) - 2 - 2
    sources, (grad_rows, stats, weights, sems) = refs[:count], refs[count:]
    made, first = [], 0
    for m in range(3):
        made.append(copies(place[0], sources, plans[m], weights.at[m], sems, first))
        first += len(plans[m])

    @pl.when(pl.program_id(0) == 0)
    def _():
        for group in made:
            start_all(group)
        stats[...] = jnp.zeros_like(stats)
        for group in made:
            wait_all(group)

    grad = dot_nt(grad_q[...], weights[0])
    grad += dot_nt(grad_k[...], weights[1])
    grad += dot_nt(grad_v[...], weights[2])
    unit_rows, inverse = centred_rows(rows[...].astype(F32))
    grad_rows[...] = grad_middle[...] + norm_back(grad, unit_rows, inverse, vector(table, LN1_G))
    sums = [row_sum(grad * unit_rows), row_sum(grad)]
    sums += [row_sum(grad_q[...].astype(F32)), row_sum(grad_v[...].astype(F32))]
    for at, total in enumerate(sums):
        stats[at : at + 1, :] += total


def inputs_back(place, rows, grad_middle, grad_q, grad_k, grad_v, table, group):
    arrays, plans = group
    count, width = rows.shape
    return pl.pallas_call(
        functools.partial(inputs_kernel, plans),
        grid=(count // TILE,),
        in_specs=[SMEM] + [tile_of(width)] * 5 + [whole(table.shape)] + [ANY] * len(arrays),
        out_specs=[tile_of(width), whole((8, width))],
        out_shape=[
            jax.ShapeDtypeStruct(rows.shape, F32),
            jax.ShapeDtypeStruct((8, width), F32),
        ],
        scratch_shapes=[
            pltpu.VMEM((3, width, width), BF16),
            pltpu.SemaphoreType.DMA((sum(len(p) for p in plans[:3]),)),
        ],
        compiler_params=params(60),
        cost_estimate=cost(6 * count * width * width, 20 * count * width),
        name="inputs_back",
    )(place, rows, grad_middle, grad_q, grad_k, grad_v, table, *arrays)


def add_low(left, right):
    return (left.astype(F32) + right.astype(F32)).astype(left.dtype)


def split_cores(stacked):
    stacked = flip_own(stacked)
    pieces = stacked.reshape((-1, 2) + stacked.shape[1:])
    return pieces[:, 0], pieces[:, 1]


def quarters(held):
    held = held.reshape((-1, 4) + held.shape[1:])
    return tuple(held[:, i] for i in range(4))


def add_kernel(mine, other, own, by_x, by_y, near, far):
    total = (mine[...].astype(F32) + other[...].astype(F32)).astype(BF16)
    own[0] = total[0]

    @pl.when(pl.program_id(0) == 0)
    def _():
        by_x[0] = total[3]
        by_x[1] = total[1]
        far[0] = total[2]

    @pl.when(pl.program_id(0) == 1)
    def _():
        by_y[0] = total[3]
        by_y[1] = total[2]
        near[0] = total[1]


def sums_of_cores(mine, other):
    rows, columns = mine.shape[1:]
    half = rows // 2
    if not direct():
        own, near, far, corner = quarters(add_low(mine, other))
        by_x = jnp.stack([corner[:, :half], near[:, :half]], axis=1)
        by_y = jnp.stack([corner[:, half:], far[:, half:]], axis=1)
        return own, by_x, by_y, near[:, half:], far[:, :half]
    sizes = [rows, 2 * half, 2 * half, half, half]
    whole_out = [(1, rows, columns), (2, half, columns), (2, half, columns), (1, half, columns), (1, half, columns)]
    own, by_x, by_y, near, far = pl.pallas_call(
        add_kernel,
        grid=(2,),
        in_specs=[pl.BlockSpec((4, half, columns), lambda i: (0, i, 0))] * 2,
        out_specs=[pl.BlockSpec((1, half, columns), lambda i: (0, i, 0))]
        + [whole(shape) for shape in whole_out[1:]],
        out_shape=[jax.ShapeDtypeStruct(shape, BF16) for shape in whole_out],
        compiler_params=params(60),
        cost_estimate=cost(4 * rows * columns, 24 * rows * columns),
        name="core_add",
    )(mine, other)
    return own, by_x[None], by_y[None], near, far


def second_sends(held, first):
    by_x, by_y = first
    return [add_low(held[3], by_y[:, 0]), add_low(held[4], by_x[:, 0])]


def own_sum(own, first, second):
    (by_x, by_y), (near, far) = first, second
    total = own.astype(F32) + jnp.concatenate([by_x[:, 1], near], axis=1).astype(F32)
    total = total + jnp.concatenate([far, by_y[:, 1]], axis=1).astype(F32)
    return total.astype(BF16)


def halve(total):
    for bit in reversed(range(3, wide_bits())):
        count = total.shape[0] // 2
        total = add_low(total[:count], cross(total[count:], bit))
    return total[0]


def spread_blocks(stacked):
    size = stacked.shape[0]
    here = lax.axis_index("narrow")
    steps = sorted(range(1, size), key=lambda step: min(step, size - step))
    blocks = [
        lax.dynamic_index_in_dim(stacked, lax.rem(here + step, size), keepdims=False)
        for step in steps
    ]
    return blocks, [lambda v, step=step: shift(v, step) for step in steps]


def add_blocks(stacked, moved):
    total = lax.dynamic_index_in_dim(stacked, lax.axis_index("narrow"), keepdims=False)
    total = total.astype(F32)
    for block in moved:
        total = total + block.astype(F32)
    return total


def column_starts(columns, part, layers):
    starts = [at * part // 128 * 128 for at in range(layers)]
    room = max(-(-(at + 1) * part // 128) * 128 - starts[at] for at in range(layers))
    return [min(start, columns - room) for start in starts], room


def columns_blocks(blocks, part, layers):
    here = lax.axis_index("narrow")
    starts, room = column_starts(blocks.shape[1], part, layers)
    choices = [blocks[:, start : start + room] for start in starts]

    def block_of(index):
        chosen = choices[-1]
        for at in reversed(range(layers - 1)):
            chosen = jnp.where(index == at, choices[at], chosen)
        return chosen

    own, *sends = [block_of(lax.rem(here + step, layers)) for step in range(layers)]
    return own, sends, shifts(layers)


def own_columns(own, moved, part, columns):
    layers = len(moved) + 1
    here = lax.axis_index("narrow")
    starts, _ = column_starts(columns, part, layers)
    total = own.astype(F32)
    for block in moved:
        total = total + block.astype(F32)
    cuts = [total[:, at * part - start : (at + 1) * part - start] for at, start in enumerate(starts)]
    result = cuts[-1]
    for at in reversed(range(layers - 1)):
        result = jnp.where(here == at, cuts[at], result)
    return result


def by_core(grad, parts):
    if direct():
        return tuple(piece.reshape(4, -1, piece.shape[3]) for piece in grad)
    places = lax.axis_size("wide")
    height, columns = grad.shape
    stacked = grad.reshape(places, height // places, parts, columns // parts).transpose(0, 2, 1, 3)
    return split_cores(stacked.reshape(places, -1, columns // parts))


def own_spot(places, layers, piece, width):
    start = (lax.axis_index("wide") * layers + lax.axis_index("narrow")) * piece
    return start // width, start % width


def shards(
    patches, lengths, w_qkv, w_out, w_up, w_down, ln1_gain, ln1_bias, q_bias, v_bias, out_bias, attn_scale,
    ln2_gain, ln2_bias, up_bias, down_bias, mlp_scale, cotangent,
):
    places, layers = lax.axis_size("wide"), lax.axis_size("narrow")
    place = lax.axis_index("wide").astype(jnp.int32).reshape(1)
    short, width = w_up.shape
    part = w_qkv.shape[1]
    quarter = w_out.shape[1]
    packs, pack_rows, _ = patches.shape
    rows = patches.reshape(-1, width)
    cotangent = cotangent.reshape(-1, width)

    small = [ln1_gain, ln1_bias, q_bias, v_bias, out_bias, attn_scale, ln2_gain, ln2_bias, down_bias, mlp_scale]
    piece, long = ln1_gain.shape[0], up_bias.shape[0]
    small_spot = own_spot(places, layers, piece, width)
    up_spot = own_spot(places, layers, long, width)
    extra = jnp.pad(jnp.stack(small), ((0, 0), (0, part - piece)))
    extra = jnp.concatenate([extra, jnp.pad(up_bias[None], ((0, 5), (0, part - long)))])
    extra = jnp.pad(extra, ((0, 0), (0, quarter)))
    early = jnp.concatenate([jnp.concatenate([w_qkv, w_out], axis=1), extra])

    moved = [move(early) for move in shifts(layers)]
    one = by_origin([early, *moved])
    extra = side_by_side(one[:, short : short + 10, :piece])
    extra = jnp.pad(extra, ((0, 6), (0, width - layers * piece)))
    long_row = side_by_side(one[:, short + 10 : short + 11, :long])
    long_row = jnp.pad(long_row, ((10, 5), (0, width - layers * long)))
    qkv, out = side_by_side(one[:, :short, :part]), side_by_side(one[:, :short, part:])
    one = jnp.concatenate([*jnp.split(qkv, 3, axis=1), out, extra + long_row])
    held = double(one)
    sends = [held, held] + [w_up] * (layers - 1)
    (near, far, *two) = [move(send) for move, send in zip(planes() + shifts(layers), sends)]
    near, far, two = lax.optimization_barrier((near, far, two))
    half = near.shape[1] // 32 * 16
    sends = [near[:, :half], far[:, half:], jnp.concatenate([held, near, far])]
    two = by_origin([w_up, *two]).reshape(-1, width)
    two, sends = lax.optimization_barrier((two, sends))
    two = in_order(lax.all_gather(two, "wide"), layers)
    moves = corners() + [lambda v: cross(v, 0)]
    moved = lax.optimization_barrier([move(send) for move, send in zip(moves, sends)])
    planes_one = held, near, far, jnp.concatenate(moved[:2], axis=1)
    side_down = jnp.concatenate(jnp.split(w_down, layers, axis=0), axis=1)
    side_down = after(side_down, moved)
    one, extras = matrices(planes_one, (moved[2], cross(planes_one[3], 0)), 4, layers * piece, layers * long)

    (normed, query, key, value, table), three = beside(
        lambda v: project(place, v, extras, one), rows, [side_down] * (layers - 1), shifts(layers)
    )
    three = by_origin([side_down, *three])
    three = jnp.concatenate(
        [side_by_side(three[:, :, i * quarter : (i + 1) * quarter]) for i in range(layers)]
    )
    query, three = lax.optimization_barrier((query, three))
    three = in_order(lax.all_gather(three, "wide"), 1)
    kept, mixed = [], ()
    for pack in range(packs):
        mixed, weights = attend(lengths, query, key, value, pack, mixed)
        mixed = (mixed,)
        kept.append(weights)
    (mixed,) = mixed
    branch, normed_two, active, slope, grad_down = hidden(
        place, lengths, rows, mixed, cotangent, table, one, two
    )
    grad_w_down = wide_outer(place, grad_down, active)
    active = after(active, grad_w_down)
    if places != 8:
        grad_w_down = grad_w_down.reshape(8, width, places // 8, -1).transpose(0, 2, 1, 3)
    total_down = lax.psum_scatter(grad_w_down.reshape(places, width, -1), "wide")

    result, grad_hidden, grad_middle, grad_branch, grad_mixed, stats_two, hidden_stats = back(
        place, lengths, rows, branch, active, slope, grad_down, cotangent, table, one, two, three
    )
    mine, theirs = by_core(
        outer(place, [(normed_two, [grad_hidden]), (mixed, [grad_branch])], width), layers + 1
    )
    grads, (other,) = beside(
        lambda v: attend_back(query, key, value, v, kept[0], 0),
        grad_mixed,
        [theirs],
        [lambda v: cross(v, 0)],
    )
    up_held = sums_of_cores(mine, other)
    total_down, grads = lax.optimization_barrier((total_down, grads))
    total_down = lax.psum_scatter(total_down.reshape(layers, quarter, -1), "narrow")
    for pack in range(1, packs):
        run = functools.partial(attend_back, query, key, value, grad_mixed, kept[pack], pack)
        if pack == packs - 1:
            grads, moved = beside(run, grads, up_held[1:3], planes())
        else:
            grads = run(grads)
    up_moved, sends = moved, second_sends(up_held, moved)
    grads, sends = lax.optimization_barrier((grads, sends))
    mine_theirs, moved = beside(
        lambda v: outer(place, [(normed, v)], width), grads, sends, planes()
    )
    mine_theirs, total_down = lax.optimization_barrier((mine_theirs, total_down))
    mine, theirs = by_core(mine_theirs, 3)
    total_up = halve(own_sum(up_held[0], up_moved, moved))
    total_out = total_up[layers * short :].reshape(short, layers, quarter).transpose(1, 0, 2)
    total_up = total_up[: layers * short].reshape(layers, short, width)
    total_up = jnp.concatenate([total_up, total_out], axis=2)
    up_sends, up_moves = spread_blocks(total_up)
    up_sends, (other,) = beside(lambda v: v, up_sends, [theirs], [lambda v: cross(v, 0)])
    held = sums_of_cores(mine, other)
    grad_q, grad_k, grad_v = grads
    (grad_rows, stats_one), moved = beside(
        lambda v: inputs_back(place, rows, grad_middle, v, grad_k, grad_v, table, one),
        grad_q,
        [*held[1:3], *up_sends],
        planes() + up_moves,
    )
    first, up_parts = moved[:2], moved[2:]
    sums = jnp.concatenate([stats_one, stats_two, hidden_stats])
    others = [sums] * (layers - 1)
    sums, moved = beside(
        lambda v: v, sums, [*second_sends(held, first), *others], planes() + shifts(layers)
    )
    second = moved[:2]
    for piece_sums in moved[2:]:
        sums = sums + piece_sums
    total_qkv = halve(own_sum(held[0], first, second))
    blocks = jnp.concatenate([total_qkv[i * short : (i + 1) * short] for i in range(3)], axis=1)
    own_block, sends, moves = columns_blocks(blocks, part, layers)
    both = [lambda v: exchange(v, "wide", lambda i: i ^ 6)]
    sums, moved = beside(lambda v: v, sums, [*sends, sums, sums, sums], moves + planes() + both)
    total_qkv = own_columns(own_block, moved[: layers - 1], part, blocks.shape[1])
    for piece_sums in moved[layers - 1 :]:
        sums = sums + piece_sums
    for bit in (0, *range(3, wide_bits())):
        sums = sums + cross(sums, bit)
    total_up = add_blocks(total_up, up_parts)
    total_down = total_down.astype(F32).T

    own = lax.dynamic_slice(sums, (0, small_spot[1]), (16, ln1_gain.shape[0]))
    own_up = lax.dynamic_slice(sums, (16 + up_spot[0], up_spot[1]), (1, up_bias.shape[0]))[0]
    return (
        result.reshape(patches.shape),
        grad_rows.reshape(patches.shape),
        total_qkv,
        total_up[:, width:],
        total_up[:, :width],
        total_down,
        own[0],
        own[1],
        own[2],
        own[3],
        own[13],
        own[12],
        own[10],
        own[11],
        own_up,
        own[9],
        own[8],
    )


def solution(mesh):
    return jax.shard_map(
        shards,
        mesh=mesh,
        in_specs=(
            P(("wide", "narrow"), None, None),
            P(("wide", "narrow"), None),
            P("wide", "narrow"),
            P("wide", "narrow"),
            P("wide", "narrow"),
            P("wide", "narrow"),
            P(("wide", "narrow")),
            P(("wide", "narrow")),
            P(("wide", "narrow")),
            P(("wide", "narrow")),
            P(("wide", "narrow")),
            P(("wide", "narrow")),
            P(("wide", "narrow")),
            P(("wide", "narrow")),
            P(("wide", "narrow")),
            P(("wide", "narrow")),
            P(("wide", "narrow")),
            P(("wide", "narrow"), None, None),
        ),
        out_specs=(
            P(("wide", "narrow"), None, None),
            P(("wide", "narrow"), None, None),
            P("wide", "narrow"),
            P("wide", "narrow"),
            P("wide", "narrow"),
            P("wide", "narrow"),
            P(("wide", "narrow")),
            P(("wide", "narrow")),
            P(("wide", "narrow")),
            P(("wide", "narrow")),
            P(("wide", "narrow")),
            P(("wide", "narrow")),
            P(("wide", "narrow")),
            P(("wide", "narrow")),
            P(("wide", "narrow")),
            P(("wide", "narrow")),
            P(("wide", "narrow")),
        ),
        check_vma=False,
    )
```

```python
import functools
import math

import jax
import jax.numpy as jnp
from jax import lax
from jax.experimental import pallas as pl
from jax.experimental.pallas import tpu as pltpu
from jax.sharding import PartitionSpec as P

HD = 64
HEADS = 4
LN_EPSILON = 1e-06
MASKED = -1e30
TILE = 256
F32 = jnp.float32
BF16 = jnp.bfloat16
MIB = 1 << 20


def exchange(value, axis_name, partner):
    size = lax.axis_size(axis_name)
    return lax.ppermute(value, axis_name, [(i, partner(i) % size) for i in range(size)])


def cross(value, bit):
    return exchange(value, "wide", lambda i: i ^ (1 << bit))


def shift(value, step):
    return exchange(value, "narrow", lambda i: i + step)


def wide_bits():
    return lax.axis_size("wide").bit_length() - 1


def by_origin(pieces):
    size = len(pieces)
    backward = jnp.stack(pieces[::-1])
    twice = jnp.concatenate([backward, backward])
    return lax.dynamic_slice_in_dim(twice, size - 1 - lax.axis_index("narrow"), size)


def flip_own(stacked):
    here = lax.axis_index("wide")
    size = stacked.shape[0]
    for bit in range(size.bit_length() - 1):
        halves = stacked.reshape((size >> (bit + 1), 2, 1 << bit) + stacked.shape[1:])
        halves = jnp.where((here >> bit) & 1, halves[:, ::-1], halves)
        stacked = halves.reshape(stacked.shape)
    return stacked


def after(value, *others):
    return lax.optimization_barrier((value, others))[0]


def beside(run, value, sends, moves):
    value, sends = lax.optimization_barrier((value, sends))
    moved = [move(send) for move, send in zip(moves, sends, strict=True)]
    return lax.optimization_barrier((run(value), moved))


def beside_loose(run, value, sends, moves):
    return beside(run, value, sends, moves)


def planes():
    return [lambda v: cross(v, 1), lambda v: cross(v, 2)]


def corners():
    return [lambda v: cross(v, 2), lambda v: cross(v, 1)]


def shifts(layers):
    return [lambda v, step=step: shift(v, step) for step in range(1, layers)]


def double(block):
    held = block[None]
    for bit in range(3, wide_bits()):
        held = jnp.concatenate([held, cross(held, bit)])
    return held


def side_by_side(stacked):
    return jnp.concatenate([stacked[i] for i in range(stacked.shape[0])], axis=1)


def direct():
    return lax.axis_size("wide") == 8


def in_order(stacked, parts):
    places, rows, columns = stacked.shape
    unit = rows // parts
    if parts == 1 or not direct():
        stacked = stacked.reshape(places, parts, unit, columns)
        arrays = [stacked[:, m].reshape(-1, columns) for m in range(parts)]
        return arrays, [[(m, 0, 0, None, unit)] for m in range(parts)]
    return [stacked], [[(0, at, m * unit, at, -unit) for at in range(places)] for m in range(parts)]


def matrices(planes, cores, parts, short, long):
    unit = (planes[0].shape[1] - 16) // parts
    behind = parts * unit
    if not direct():
        other = [*jnp.split(cores[0], 3), cores[1]]
        stacked = jnp.stack([jnp.stack(pair, axis=1) for pair in zip(planes, other)], axis=1)
        stacked = flip_own(stacked.reshape((-1,) + planes[0].shape[1:]))
        width = stacked.shape[2]
        rows = stacked[:, behind:].transpose(1, 0, 2)
        table = rows[:10, :, :short].reshape(10, width)
        up = rows[10, :, :long].reshape(-1, width)
        table = jnp.concatenate([table, up])
        table = jnp.pad(table, ((0, 16 - table.shape[0]), (0, 0)))
        stacked = stacked[:, :behind].reshape(stacked.shape[0], parts, unit, -1)
        arrays = [stacked[:, m].reshape(-1, stacked.shape[3]) for m in range(parts)]
        plans = [[(m, 0, 0, None, unit)] for m in range(parts)]
        return (arrays, plans), (table, None)
    spots = [(0, 0, 0), (1, 0, 2), (2, 0, 4), (3, 0, 6), (4, 0, 1), (4, 1, 3), (4, 2, 5), (5, 0, 7)]
    plans = [[(at, index, m * unit, rel, unit) for at, index, rel in spots] for m in range(parts)]
    return ([*planes, *cores], plans), (None, (spots, behind, short, long))


def copies(place, refs, plan, target, sems, first):
    made = []
    for at, index, row, rel, unit in plan:
        sem = sems.at[first + len(made)]
        if rel is None:
            made.append(pltpu.make_async_copy(refs[at], target, sem))
        else:
            start = -rel * unit if unit < 0 else pl.multiple_of((place ^ rel) * unit, 16)
            unit = abs(unit)
            source = refs[at].at[index, pl.ds(row, unit)]
            made.append(pltpu.make_async_copy(source, target.at[pl.ds(start, unit)], sem))
    return made


def start_all(made):
    for copy in made:
        copy.start()


def wait_all(made):
    for copy in made:
        copy.wait()


def dot(left, right):
    return lax.dot_general(left, right, (((1,), (0,)), ((), ())), preferred_element_type=F32)


def dot_nt(left, right):
    return lax.dot_general(left, right, (((1,), (1,)), ((), ())), preferred_element_type=F32)


def centred_rows(values):
    row_mean = jnp.mean(values, axis=-1, keepdims=True)
    centred = values - row_mean
    row_var = jnp.mean(centred * centred, axis=-1, keepdims=True)
    inverse = lax.rsqrt(row_var + LN_EPSILON)
    return centred * inverse, inverse


def norm_back(grad, unit_rows, inverse, gain):
    scaled = grad * gain
    mean_one = jnp.mean(scaled, axis=-1, keepdims=True)
    mean_two = jnp.mean(scaled * unit_rows, axis=-1, keepdims=True)
    return (scaled - mean_one - unit_rows * mean_two) * inverse


def row_sum(values):
    return jnp.sum(values, axis=0, keepdims=True)


def gelu_pair(values):
    bell = jnp.exp(values * values * -0.5)
    share = 0.5 + 0.5 * lax.erf(values * math.sqrt(0.5))
    return values * share, share + values * bell * (1.0 / math.sqrt(2.0 * math.pi))


ANY = pl.BlockSpec(memory_space=pl.ANY)
SMEM = pl.BlockSpec(memory_space=pltpu.SMEM)


def whole(shape):
    return pl.BlockSpec(shape, lambda *_: (0,) * len(shape))


def tile_of(columns):
    return pl.BlockSpec((TILE, columns), lambda i: (i, 0))


def cost(flops, moved, exps=0):
    return pl.CostEstimate(flops=flops, bytes_accessed=moved, transcendentals=exps)


def params(mib, dims=1):
    return pltpu.CompilerParams(
        vmem_limit_bytes=mib * MIB, dimension_semantics=("arbitrary",) * dims
    )


LN1_G, LN1_B, Q_B, V_B, OUT_B, ATTN_S, LN2_G, LN2_B, DOWN_B, MLP_S, UP_B = range(11)


def vector(table, row):
    return table[row : row + 1, :]


def make_table(place, pieces, layout):
    spots, _, short, long = layout
    shape = pieces.shape[1:]
    lane = lax.broadcasted_iota(jnp.int32, shape, 1)
    row = lax.broadcasted_iota(jnp.int32, shape, 0)
    table = jnp.zeros(shape, F32)
    for at, (_, _, rel) in enumerate(spots):
        spot = place ^ rel
        piece = pieces[at].astype(F32)
        table += pltpu.roll(jnp.where((row < UP_B) & (lane < short), piece, 0.0), spot * short, 1)
        start = spot * long
        up = jnp.where(lane[:1] < long, piece[UP_B : UP_B + 1], 0.0)
        up = pltpu.roll(jnp.broadcast_to(up, shape), lax.rem(start, shape[1]), 1)
        table += jnp.where(row == UP_B + start // shape[1], up, 0.0)
    return table


def project_kernel(plans, layout, place, rows, extras, *refs):
    count = len(refs) - 5 - 4
    sources, refs = refs[:count], refs[count:]
    normed, query, key, value, table, weights, pieces, sems, piece_sems = refs
    made, first = [], 0
    for m in range(3):
        made.append(copies(place[0], sources, plans[m], weights.at[m], sems, first))
        first += len(plans[m])

    @pl.when(pl.program_id(0) == 0)
    def _():
        for group in made:
            start_all(group)
        if layout is None:
            table[...] = extras[...].astype(F32)
            return
        brought = []
        for at, (source, index, _) in enumerate(layout[0]):
            piece = sources[source].at[index, pl.ds(layout[1], 16)]
            brought.append(pltpu.make_async_copy(piece, pieces.at[at], piece_sems.at[at]))
        start_all(brought)
        wait_all(brought)
        table[...] = make_table(place[0], pieces, layout)

    unit_rows, _ = centred_rows(rows[...].astype(F32))
    low = (unit_rows * vector(table, LN1_G) + vector(table, LN1_B)).astype(BF16)
    normed[...] = low

    @pl.when(pl.program_id(0) == 0)
    def _():
        for group in made:
            wait_all(group)

    query[...] = ((dot(low, weights[0]) + vector(table, Q_B)) * 0.125).astype(BF16)
    key[...] = dot(low, weights[1]).astype(BF16)
    value[...] = (dot(low, weights[2]) + vector(table, V_B)).astype(BF16)


def project(place, rows, extras, group):
    arrays, plans = group
    extras, layout = extras
    count, width = rows.shape
    if extras is None:
        extras = jnp.zeros((16, width), BF16)
    return pl.pallas_call(
        functools.partial(project_kernel, plans, layout),
        grid=(count // TILE,),
        in_specs=[SMEM, tile_of(width), whole(extras.shape)] + [ANY] * len(arrays),
        out_specs=[tile_of(width)] * 4 + [whole((16, width))],
        out_shape=[jax.ShapeDtypeStruct(rows.shape, BF16)] * 4
        + [jax.ShapeDtypeStruct((16, width), F32)],
        scratch_shapes=[
            pltpu.VMEM((3, width, width), BF16),
            pltpu.VMEM((8, 16, width), BF16),
            pltpu.SemaphoreType.DMA((sum(len(p) for p in plans[:3]),)),
            pltpu.SemaphoreType.DMA((8,)),
        ],
        compiler_params=params(60),
        cost_estimate=cost(6 * count * width * width, 14 * count * width),
        name="project",
    )(place, rows, extras, *arrays)


def segments(lengths, pack, position):
    end, segment = 0, jnp.zeros_like(position)
    for slot in range(lengths.shape[1] - 1):
        end = end + lengths[pack, slot]
        segment = segment + (position >= end).astype(jnp.int32)
    return jnp.where(position < end, segment, lengths.shape[1] + position)


def same_segment(lengths, pack, rows):
    down = lax.broadcasted_iota(jnp.int32, (rows, 128), 0)
    along = lax.broadcasted_iota(jnp.int32, (1, rows), 1)
    column = segments(lengths, pack, down)
    row = segments(lengths, pack, along)
    return jnp.concatenate([column] * (rows // 128), axis=1) == row


def head_lanes(shape, head):
    lane = lax.broadcasted_iota(jnp.int32, shape, 1)
    return (lane >= head * HD) & (lane < (head + 1) * HD)


def by_lanes(heads):
    chosen = heads[-1]
    for head in reversed(range(len(heads) - 1)):
        chosen = jnp.where(head_lanes(chosen.shape, head), heads[head], chosen)
    return chosen


def only(values, head):
    return jnp.where(head_lanes(values.shape, head), values, jnp.zeros_like(values))


def attend_kernel(pack, lengths, query, key, value, *refs):
    attended, kept = refs[-2:]
    rows = query.shape[0]
    same = same_segment(lengths, pack, rows)
    flat = jnp.transpose(value[...].astype(F32)).astype(BF16)
    mixed = []
    for head in range(HEADS):
        scores = dot_nt(key[...], only(query[...], head))
        scores = jnp.where(same, scores, MASKED)
        top = jnp.max(scores, axis=0, keepdims=True)
        powers = jnp.exp(scores - top)
        total = jnp.sum(powers, axis=0, keepdims=True)
        weights = (powers * (1.0 / total)).astype(BF16)
        mixed.append(dot(flat[head * HD : (head + 1) * HD], weights))
        kept[head] = weights
    attended[...] = jnp.transpose(jnp.concatenate(mixed, axis=0)).astype(BF16)


def pair_block(rows, pack, first=0):
    return pl.BlockSpec((rows, HEADS * HD), lambda h: (pack, h + first))


def kept_block(rows, first=0):
    return pl.BlockSpec((HEADS, rows, rows), lambda h: (h + first, 0, 0))


def attend(lengths, query, key, value, pack, earlier=()):
    packs = lengths.shape[0]
    count, width = query.shape
    rows, pairs = count // packs, width // (HEADS * HD)
    return pl.pallas_call(
        functools.partial(attend_kernel, pack),
        grid=(pairs,),
        in_specs=[SMEM] + [pair_block(rows, pack)] * 3 + [ANY] * len(earlier),
        out_specs=[pair_block(rows, pack), kept_block(rows)],
        out_shape=[
            jax.ShapeDtypeStruct(query.shape, BF16),
            jax.ShapeDtypeStruct((HEADS * pairs, rows, rows), BF16),
        ],
        input_output_aliases={4 + i: i for i in range(len(earlier))},
        compiler_params=params(60),
        cost_estimate=cost(16 * rows * rows * width, 8 * rows * width) if earlier else cost(0, 0),
        name="attend",
    )(lengths, query, key, value, *earlier)


def attend_back_kernel(query, key, value, grad, kept, *refs):
    grad_q, grad_k, grad_v = refs[-3:]
    flat_key = jnp.transpose(key[...].astype(F32)).astype(BF16)
    by_query, by_key, by_value = [], [], []
    for head in range(HEADS):
        weights = kept[head]
        probs = weights.astype(F32)
        by_value.append(dot(weights, grad[...]))
        grad_probs = dot_nt(value[...], only(grad[...], head))
        centre = jnp.sum(grad_probs * probs, axis=0, keepdims=True)
        grad_scores = (probs * (grad_probs - centre)).astype(BF16)
        by_key.append(dot(grad_scores, query[...]))
        by_query.append(dot(flat_key[head * HD : (head + 1) * HD], grad_scores))
    grad_k[...] = by_lanes(by_key).astype(BF16)
    grad_v[...] = by_lanes(by_value).astype(BF16)
    grad_q[...] = jnp.transpose(jnp.concatenate(by_query, axis=0)).astype(BF16) * 0.125


def attend_back(query, key, value, grad, kept, pack, first, last, earlier=()):
    rows = kept.shape[1]
    width = query.shape[1]
    part = last - first
    return pl.pallas_call(
        attend_back_kernel,
        grid=(part,),
        in_specs=[pair_block(rows, pack, first)] * 4
        + [kept_block(rows, first)]
        + [ANY] * len(earlier),
        out_specs=[pair_block(rows, pack, first)] * 3,
        out_shape=[jax.ShapeDtypeStruct(query.shape, BF16)] * 3,
        input_output_aliases={5 + i: i for i in range(len(earlier))},
        compiler_params=params(60),
        cost_estimate=cost(32 * rows * rows * HEADS * HD * part, 14 * rows * HEADS * HD * part, 0),
        name="attend_back",
    )(query, key, value, grad, kept, *earlier)


def live_rows(lengths, shape):
    tiles = pl.num_programs(0) // lengths.shape[0]
    step = pl.program_id(0)
    pack = step // tiles
    end = 0
    for slot in range(lengths.shape[1] - 1):
        end = end + lengths[pack, slot]
    position = lax.broadcasted_iota(jnp.int32, shape, 0) + (step - pack * tiles) * shape[0]
    return position < end


def hidden_kernel(out_plan, up_plans, sizes, place, lengths, rows, mixed, cotangent, table, *refs):
    sources, refs = refs[: sum(sizes)], refs[sum(sizes) :]
    one, two = sources[: sizes[0]], sources[sizes[0] :]
    branch_out, normed, active, slope, grad_down, out_w, up_w, sems = refs
    made = [copies(place[0], one, out_plan, out_w, sems, 0)]
    first = len(out_plan)
    for m, plan in enumerate(up_plans):
        made.append(copies(place[0], two, plan, up_w.at[m], sems, first))
        first += len(plan)

    @pl.when(pl.program_id(0) == 0)
    def _():
        for group in made:
            start_all(group)
        wait_all(made[0])

    branch = dot(mixed[...], out_w[...]) + vector(table, OUT_B)
    branch_out[...] = branch
    middle = rows[...].astype(F32) + vector(table, ATTN_S) * branch
    unit_rows, _ = centred_rows(middle)
    low = (unit_rows * vector(table, LN2_G) + vector(table, LN2_B)).astype(BF16)
    normed[...] = low
    live = live_rows(lengths, cotangent.shape)
    grad_out = jnp.where(live, cotangent[...].astype(F32), 0.0)
    grad_down[...] = (grad_out * vector(table, MLP_S)).astype(BF16)

    width = low.shape[1]
    for m in range(len(up_plans)):

        @pl.when(pl.program_id(0) == 0)
        def _(m=m):
            wait_all(made[m + 1])

        part = slice(m * width, (m + 1) * width)
        up = dot(low, up_w[m]) + vector(table, UP_B + m)
        value, rate = gelu_pair(up)
        active[:, part] = value.astype(BF16)
        slope[:, part] = rate.astype(BF16)


def hidden(place, lengths, rows, mixed, cotangent, table, group_one, group_two):
    count, width = rows.shape
    hidden_units = width * len(group_two[1])
    out_plan, up_plans = group_one[1][3], group_two[1]
    sizes = (len(group_one[0]), len(group_two[0]))
    return pl.pallas_call(
        functools.partial(hidden_kernel, out_plan, up_plans, sizes),
        grid=(count // TILE,),
        in_specs=[SMEM, SMEM]
        + [tile_of(width)] * 3
        + [whole(table.shape)]
        + [ANY] * sum(sizes),
        out_specs=[tile_of(width)] * 2 + [tile_of(hidden_units)] * 2 + [tile_of(width)],
        out_shape=[
            jax.ShapeDtypeStruct(rows.shape, F32),
            jax.ShapeDtypeStruct(rows.shape, BF16),
            jax.ShapeDtypeStruct((count, hidden_units), BF16),
            jax.ShapeDtypeStruct((count, hidden_units), BF16),
            jax.ShapeDtypeStruct(rows.shape, BF16),
        ],
        scratch_shapes=[
            pltpu.VMEM((width, width), BF16),
            pltpu.VMEM((len(up_plans), width, width), BF16),
            pltpu.SemaphoreType.DMA((len(out_plan) + sum(len(p) for p in up_plans),)),
        ],
        compiler_params=params(60),
        cost_estimate=cost(14 * count * width * hidden_units // 4, 26 * count * width, 2 * count * hidden_units),
        name="hidden",
    )(place, lengths, rows, mixed, cotangent, table, *group_one[0], *group_two[0])


STATS_UP, STATS_ONE = 6, 10


def back_kernel(
    out_plan, up_plans, down_plan, sizes, place, lengths, rows, branch_in, active, slope, grad_down, cotangent,
    table, *refs,
):
    sources, refs = refs[: sum(sizes)], refs[sum(sizes) :]
    one, two = sources[: sizes[0]], sources[sizes[0] : sizes[0] + sizes[1]]
    three = sources[sizes[0] + sizes[1] :]
    result, grad_hidden, grad_middle_out, grad_branch, grad_mixed, stats = refs[:6]
    out_w, up_w, down_w, sems = refs[6:]
    made = [copies(place[0], three, down_plan, down_w, sems, 0)]
    first = len(down_plan)
    for m, plan in enumerate(up_plans):
        made.append(copies(place[0], two, plan, up_w.at[m], sems, first))
        first += len(plan)
    made.append(copies(place[0], one, out_plan, out_w, sems, first))

    @pl.when(pl.program_id(0) == 0)
    def _():
        for group in made:
            start_all(group)
        stats[...] = jnp.zeros_like(stats)
        wait_all(made[0])

    live = live_rows(lengths, cotangent.shape)
    branch = branch_in[...]
    middle = rows[...].astype(F32) + vector(table, ATTN_S) * branch
    down_out = dot(active[...], down_w[...]) + vector(table, DOWN_B)
    result[...] = jnp.where(live, middle + vector(table, MLP_S) * down_out, 0.0).astype(BF16)
    grad_out = jnp.where(live, cotangent[...].astype(F32), 0.0)
    sums = [row_sum(grad_out * down_out), row_sum(grad_down[...].astype(F32))]

    @pl.when(pl.program_id(0) == 0)
    def _():
        for group in made[1:]:
            wait_all(group)

    width = middle.shape[1]
    grad_normed = jnp.zeros(middle.shape, F32)
    for m in range(len(up_plans)):
        part = slice(m * width, (m + 1) * width)
        grad_active = dot_nt(grad_down[...], down_w[part, :])
        low = (grad_active * slope[:, part].astype(F32)).astype(BF16)
        grad_hidden[:, part] = low
        stats[STATS_UP + m : STATS_UP + m + 1, :] += row_sum(low.astype(F32))
        grad_normed += dot_nt(low, up_w[m])
    unit_rows, inverse = centred_rows(middle)
    sums += [row_sum(grad_normed * unit_rows), row_sum(grad_normed)]
    grad_middle = grad_out + norm_back(grad_normed, unit_rows, inverse, vector(table, LN2_G))
    grad_middle_out[...] = grad_middle
    low = (grad_middle * vector(table, ATTN_S)).astype(BF16)
    grad_branch[...] = low
    sums += [row_sum(grad_middle * branch), row_sum(low.astype(F32))]
    grad_mixed[...] = dot_nt(low, out_w[...]).astype(BF16)
    for at, total in enumerate(sums):
        stats[at : at + 1, :] += total


def back(place, lengths, rows, branch, active, slope, grad_down, cotangent, table, one, two, three):
    count, width = rows.shape
    hidden_units = active.shape[1]
    plans = (one[1][3], two[1], three[1][0])
    sizes = (len(one[0]), len(two[0]), len(three[0]))
    return pl.pallas_call(
        functools.partial(back_kernel, *plans, sizes),
        grid=(count // TILE,),
        in_specs=[SMEM, SMEM]
        + [tile_of(width)] * 2
        + [tile_of(hidden_units)] * 2
        + [tile_of(width)] * 2
        + [whole(table.shape)]
        + [ANY] * sum(sizes),
        out_specs=[tile_of(width), tile_of(hidden_units)]
        + [tile_of(width)] * 3
        + [whole((16, width))],
        out_shape=[
            jax.ShapeDtypeStruct(rows.shape, BF16),
            jax.ShapeDtypeStruct(active.shape, BF16),
            jax.ShapeDtypeStruct(rows.shape, F32),
            jax.ShapeDtypeStruct(rows.shape, BF16),
            jax.ShapeDtypeStruct(rows.shape, BF16),
            jax.ShapeDtypeStruct((16, width), F32),
        ],
        scratch_shapes=[
            pltpu.VMEM((width, width), BF16),
            pltpu.VMEM((len(plans[1]), width, width), BF16),
            pltpu.VMEM((hidden_units, width), BF16),
            pltpu.SemaphoreType.DMA(
                (len(plans[0]) + sum(len(p) for p in plans[1]) + len(plans[2]),)
            ),
        ],
        compiler_params=params(60),
        cost_estimate=cost(26 * count * width * hidden_units // 4, 40 * count * width),
        name="back",
    )(place, lengths, rows, branch, active, slope, grad_down, cotangent, table, *one[0], *two[0], *three[0])


def outer_kernel(spread, steps, place, *refs):
    lefts, refs = refs[: len(steps)], refs[len(steps) :]
    count = sum(len(own) for own in steps)
    rights, refs = refs[:count], refs[count:]
    flat = refs[-1]
    step = pl.program_id(0)

    def put(right):
        value = dot(flat[...], right[...])
        if not spread:
            refs[0][...] = value.astype(BF16)
            return
        mine, theirs = refs[:2]
        unit = flat.shape[0] // 8
        value = value.astype(BF16)
        for at in range(4):
            mine[at, 0] = value[2 * at * unit : (2 * at + 1) * unit]
            theirs[at, 0] = value[(2 * at + 1) * unit : (2 * at + 2) * unit]

    first, at_right = 0, 0
    for left, own in zip(lefts, steps):

        @pl.when(step == first)
        def _(left=left):
            for at in range(0, flat.shape[0], 128):
                block = left[:, at : at + 128].astype(F32)
                turned = jnp.transpose(block).astype(BF16)
                if spread:
                    refs[2][at : at + 128, :] = turned
                else:
                    flat[at : at + 128, :] = turned
            if spread:
                unit = flat.shape[0] // 8
                for rel in range(8):
                    start = pl.multiple_of((place[0] ^ rel) * unit, 16)
                    flat[rel * unit : (rel + 1) * unit, :] = refs[2][pl.ds(start, unit), :]

        for count in own:

            @pl.when((step >= first) & (step < first + count))
            def _(right=rights[at_right]):
                put(right)

            first += count
            at_right += 1


def outer(place, pairs, width):
    count, height = pairs[0][0].shape
    steps = [[right.shape[1] // width for right in rights] for _, rights in pairs]
    total = sum(sum(own) for own in steps)
    right_specs, first = [], 0
    for own in sum(steps, []):
        right_specs.append(
            pl.BlockSpec(
                (count, width),
                lambda i, first=first, own=own: (0, jnp.clip(i - first, 0, own - 1)),
            )
        )
        first += own
    scratch = [pltpu.VMEM((height, count), BF16)]
    if direct():
        block = pl.BlockSpec((4, 1, height // 8, width), lambda i: (0, i, 0, 0))
        shape = jax.ShapeDtypeStruct((4, total, height // 8, width), BF16)
        specs, shapes = [block, block], [shape, shape]
        scratch = scratch * 2
    else:
        specs = pl.BlockSpec((height, width), lambda i: (0, i))
        shapes = jax.ShapeDtypeStruct((height, total * width), BF16)
    return pl.pallas_call(
        functools.partial(outer_kernel, direct(), steps),
        grid=(total,),
        in_specs=[SMEM] + [whole((count, height))] * len(pairs) + right_specs,
        out_specs=specs,
        out_shape=shapes,
        scratch_shapes=scratch,
        compiler_params=params(60),
        cost_estimate=cost(2 * count * height * total * width, 2 * (count + height) * total * width),
        name="outer",
    )(place, *(left for left, _ in pairs), *(right for _, rights in pairs for right in rights))


def wide_outer_kernel(place, left, right, out, flat):
    @pl.when(pl.program_id(0) == 0)
    def _():
        for at in range(0, flat.shape[0], 128):
            block = left[:, at : at + 128].astype(F32)
            flat[at : at + 128, :] = jnp.transpose(block).astype(BF16)

    value = dot(flat[...], right[...]).astype(BF16)
    half = value.shape[1] // 2
    out[0] = value[:, :half]
    out[1] = value[:, half:]


def wide_outer(place, left, right):
    count, height = left.shape
    columns = right.shape[1]
    steps = 8
    step = columns // steps
    return pl.pallas_call(
        wide_outer_kernel,
        grid=(steps // 2,),
        in_specs=[SMEM, whole(left.shape), pl.BlockSpec((count, 2 * step), lambda i: (0, i))],
        out_specs=pl.BlockSpec((2, height, step), lambda i: (i, 0, 0)),
        out_shape=jax.ShapeDtypeStruct((steps, height, step), BF16),
        scratch_shapes=[pltpu.VMEM((height, count), BF16)],
        compiler_params=params(60),
        cost_estimate=cost(2 * count * height * columns, 2 * (count + height) * (height + columns)),
        name="wide_outer",
    )(place, left, right)


def inputs_kernel(plans, place, rows, grad_middle, grad_q, grad_k, grad_v, table, earlier, *refs):
    count = len(refs) - 2 - 2
    sources, (grad_rows, stats, weights, sems) = refs[:count], refs[count:]
    made, first = [], 0
    for m in range(3):
        made.append(copies(place[0], sources, plans[m], weights.at[m], sems, first))
        first += len(plans[m])

    @pl.when(pl.program_id(0) == 0)
    def _():
        for group in made:
            start_all(group)
        stats[...] = earlier[...]
        for group in made:
            wait_all(group)

    grad = dot_nt(grad_q[...], weights[0])
    grad += dot_nt(grad_k[...], weights[1])
    grad += dot_nt(grad_v[...], weights[2])
    unit_rows, inverse = centred_rows(rows[...].astype(F32))
    grad_rows[...] = grad_middle[...] + norm_back(grad, unit_rows, inverse, vector(table, LN1_G))
    sums = [row_sum(grad * unit_rows), row_sum(grad)]
    sums += [row_sum(grad_q[...].astype(F32)), row_sum(grad_v[...].astype(F32))]
    for at, total in enumerate(sums):
        stats[STATS_ONE + at : STATS_ONE + at + 1, :] += total


def inputs_back(place, rows, grad_middle, grad_q, grad_k, grad_v, table, earlier, group):
    arrays, plans = group
    count, width = rows.shape
    return pl.pallas_call(
        functools.partial(inputs_kernel, plans),
        grid=(count // TILE,),
        in_specs=[SMEM] + [tile_of(width)] * 5 + [whole(table.shape)] * 2 + [ANY] * len(arrays),
        out_specs=[tile_of(width), whole((16, width))],
        out_shape=[
            jax.ShapeDtypeStruct(rows.shape, F32),
            jax.ShapeDtypeStruct((16, width), F32),
        ],
        scratch_shapes=[
            pltpu.VMEM((3, width, width), BF16),
            pltpu.SemaphoreType.DMA((sum(len(p) for p in plans[:3]),)),
        ],
        compiler_params=params(60),
        cost_estimate=cost(6 * count * width * width, 20 * count * width),
        name="inputs_back",
    )(place, rows, grad_middle, grad_q, grad_k, grad_v, table, earlier, *arrays)


def add_low(left, right):
    return (left.astype(F32) + right.astype(F32)).astype(left.dtype)


def split_cores(stacked):
    stacked = flip_own(stacked)
    pieces = stacked.reshape((-1, 2) + stacked.shape[1:])
    return pieces[:, 0], pieces[:, 1]


def quarters(held):
    held = held.reshape((-1, 4) + held.shape[1:])
    return tuple(held[:, i] for i in range(4))


def add_kernel(mine, other, own, by_x, by_y, near, far):
    total = (mine[...].astype(F32) + other[...].astype(F32)).astype(BF16)
    own[0] = total[0]
    early = pl.program_id(0) < pl.num_programs(0) // 2

    @pl.when(early)
    def _():
        by_x[0] = total[3]
        by_x[1] = total[1]
        far[0] = total[2]

    @pl.when(jnp.logical_not(early))
    def _():
        by_y[0] = total[3]
        by_y[1] = total[2]
        near[0] = total[1]


def sums_of_cores(mine, other):
    rows, columns = mine.shape[1:]
    half = rows // 2
    if not direct():
        own, near, far, corner = quarters(add_low(mine, other))
        by_x = jnp.stack([corner[:, :half], near[:, :half]], axis=1)
        by_y = jnp.stack([corner[:, half:], far[:, half:]], axis=1)
        return own, by_x, by_y, near[:, half:], far[:, :half]
    shapes = [(1, rows, columns), (2, half, columns), (2, half, columns), (1, half, columns), (1, half, columns)]
    steps = 2
    step = rows // steps
    spots = [
        lambda i: i,
        lambda i: jnp.minimum(i, steps // 2 - 1),
        lambda i: jnp.maximum(i - steps // 2, 0),
        lambda i: jnp.maximum(i - steps // 2, 0),
        lambda i: jnp.minimum(i, steps // 2 - 1),
    ]
    own, by_x, by_y, near, far = pl.pallas_call(
        add_kernel,
        grid=(steps,),
        in_specs=[pl.BlockSpec((4, step, columns), lambda i: (0, i, 0))] * 2,
        out_specs=[
            pl.BlockSpec((shape[0], step, columns), lambda i, spot=spot: (0, spot(i), 0))
            for shape, spot in zip(shapes, spots)
        ],
        out_shape=[jax.ShapeDtypeStruct(shape, BF16) for shape in shapes],
        compiler_params=params(24),
        cost_estimate=cost(4 * rows * columns, 24 * rows * columns),
        name="core_add",
    )(mine, other)
    return own, by_x[None], by_y[None], near, far


def second_sends(held, first):
    by_x, by_y = first
    return [add_low(held[3], by_y[:, 0]), add_low(held[4], by_x[:, 0])]


def own_sum(own, first, second):
    (by_x, by_y), (near, far) = first, second
    total = own.astype(F32) + jnp.concatenate([by_x[:, 1], near], axis=1).astype(F32)
    total = total + jnp.concatenate([far, by_y[:, 1]], axis=1).astype(F32)
    return total.astype(BF16)


def halve(total):
    for bit in reversed(range(3, wide_bits())):
        count = total.shape[0] // 2
        total = add_low(total[:count], cross(total[count:], bit))
    return total[0]


def spread_blocks(stacked):
    size = stacked.shape[0]
    here = lax.axis_index("narrow")
    steps = sorted(range(1, size), key=lambda step: min(step, size - step))
    blocks = [
        lax.dynamic_index_in_dim(stacked, lax.rem(here + step, size), keepdims=False)
        for step in steps
    ]
    return blocks, [lambda v, step=step: shift(v, step) for step in steps]


def add_blocks(stacked, moved):
    total = lax.dynamic_index_in_dim(stacked, lax.axis_index("narrow"), keepdims=False)
    total = total.astype(F32)
    for block in moved:
        total = total + block.astype(F32)
    return total


def column_starts(columns, part, layers):
    starts = [at * part // 128 * 128 for at in range(layers)]
    room = max(-(-(at + 1) * part // 128) * 128 - starts[at] for at in range(layers))
    return [min(start, columns - room) for start in starts], room


def columns_blocks(blocks, part, layers):
    here = lax.axis_index("narrow")
    starts, room = column_starts(blocks.shape[1], part, layers)
    choices = [blocks[:, start : start + room] for start in starts]

    def block_of(index):
        chosen = choices[-1]
        for at in reversed(range(layers - 1)):
            chosen = jnp.where(index == at, choices[at], chosen)
        return chosen

    own, *sends = [block_of(lax.rem(here + step, layers)) for step in range(layers)]
    return own, sends, shifts(layers)


def own_columns(own, moved, part, columns):
    layers = len(moved) + 1
    here = lax.axis_index("narrow")
    starts, _ = column_starts(columns, part, layers)
    total = own.astype(F32)
    for block in moved:
        total = total + block.astype(F32)
    cuts = [total[:, at * part - start : (at + 1) * part - start] for at, start in enumerate(starts)]
    result = cuts[-1]
    for at in reversed(range(layers - 1)):
        result = jnp.where(here == at, cuts[at], result)
    return result


def by_core(grad, parts):
    if direct():
        return tuple(piece.reshape(4, -1, piece.shape[3]) for piece in grad)
    places = lax.axis_size("wide")
    height, columns = grad.shape
    stacked = grad.reshape(places, height // places, parts, columns // parts).transpose(0, 2, 1, 3)
    return split_cores(stacked.reshape(places, -1, columns // parts))


def own_spot(places, layers, piece, width):
    start = (lax.axis_index("wide") * layers + lax.axis_index("narrow")) * piece
    return start // width, start % width


def shards(
    patches, lengths, w_qkv, w_out, w_up, w_down, ln1_gain, ln1_bias, q_bias, v_bias, out_bias, attn_scale,
    ln2_gain, ln2_bias, up_bias, down_bias, mlp_scale, cotangent,
):
    places, layers = lax.axis_size("wide"), lax.axis_size("narrow")
    place = lax.axis_index("wide").astype(jnp.int32).reshape(1)
    short, width = w_up.shape
    part = w_qkv.shape[1]
    quarter = w_out.shape[1]
    packs, pack_rows, _ = patches.shape
    rows = patches.reshape(-1, width)
    cotangent = cotangent.reshape(-1, width)

    small = [ln1_gain, ln1_bias, q_bias, v_bias, out_bias, attn_scale, ln2_gain, ln2_bias, down_bias, mlp_scale]
    piece, long = ln1_gain.shape[0], up_bias.shape[0]
    small_spot = own_spot(places, layers, piece, width)
    up_spot = own_spot(places, layers, long, width)
    extra = jnp.pad(jnp.stack(small), ((0, 0), (0, part - piece)))
    extra = jnp.concatenate([extra, jnp.pad(up_bias[None], ((0, 5), (0, part - long)))])
    extra = jnp.pad(extra, ((0, 0), (0, quarter)))
    early = jnp.concatenate([jnp.concatenate([w_qkv, w_out], axis=1), extra])

    moved = [move(early) for move in shifts(layers)]
    one = by_origin([early, *moved])
    extra = side_by_side(one[:, short : short + 10, :piece])
    extra = jnp.pad(extra, ((0, 6), (0, width - layers * piece)))
    long_row = side_by_side(one[:, short + 10 : short + 11, :long])
    long_row = jnp.pad(long_row, ((10, 5), (0, width - layers * long)))
    qkv, out = side_by_side(one[:, :short, :part]), side_by_side(one[:, :short, part:])
    one = jnp.concatenate([*jnp.split(qkv, 3, axis=1), out, extra + long_row])
    held = double(one)
    sends = [held, held] + [w_up] * (layers - 1)
    (near, far, *two) = [move(send) for move, send in zip(planes() + shifts(layers), sends)]
    near, far, two = lax.optimization_barrier((near, far, two))
    half = near.shape[1] // 32 * 16
    sends = [near[:, :half], far[:, half:], jnp.concatenate([held, near, far])]
    two = by_origin([w_up, *two]).reshape(-1, width)
    two, sends = lax.optimization_barrier((two, sends))
    two = in_order(lax.all_gather(two, "wide"), layers)
    moves = corners() + [lambda v: cross(v, 0)]
    moved = lax.optimization_barrier([move(send) for move, send in zip(moves, sends)])
    planes_one = held, near, far, jnp.concatenate(moved[:2], axis=1)
    side_down = jnp.concatenate(jnp.split(w_down, layers, axis=0), axis=1)
    side_down = after(side_down, moved)
    one, extras = matrices(planes_one, (moved[2], cross(planes_one[3], 0)), 4, layers * piece, layers * long)

    (normed, query, key, value, table), three = beside(
        lambda v: project(place, v, extras, one), rows, [side_down] * (layers - 1), shifts(layers)
    )
    three = by_origin([side_down, *three])
    three = jnp.concatenate(
        [side_by_side(three[:, :, i * quarter : (i + 1) * quarter]) for i in range(layers)]
    )
    query, three = lax.optimization_barrier((query, three))
    three = in_order(lax.all_gather(three, "wide"), 1)
    kept, mixed = [], ()
    for pack in range(packs):
        mixed, weights = attend(lengths, query, key, value, pack, mixed)
        mixed = (mixed,)
        kept.append(weights)
    (mixed,) = mixed
    branch, normed_two, active, slope, grad_down = hidden(
        place, lengths, rows, mixed, cotangent, table, one, two
    )
    grad_w_down = wide_outer(place, grad_down, active)
    active = after(active, grad_w_down)
    if places != 8:
        grad_w_down = grad_w_down.reshape(8, width, places // 8, -1).transpose(0, 2, 1, 3)
    total_down = lax.psum_scatter(grad_w_down.reshape(places, width, -1), "wide")

    result, grad_hidden, grad_middle, grad_branch, grad_mixed, stats = back(
        place, lengths, rows, branch, active, slope, grad_down, cotangent, table, one, two, three
    )
    mine, theirs = by_core(
        outer(place, [(normed_two, [grad_hidden]), (mixed, [grad_branch])], width), layers + 1
    )
    def heads_back(grads, value, spans):
        for pack, first, last in spans:
            grads = attend_back(query, key, value_rows, value, kept[pack], pack, first, last, grads)
        return grads

    groups = width // (HEADS * HD)
    spans = [(0, 0, 1), (0, 1, groups)] + [(pack, 0, groups) for pack in range(1, packs)]
    value_rows = value
    grads, (other,) = beside(
        lambda v: heads_back((), v, spans[:1]), grad_mixed, [theirs], [lambda v: cross(v, 0)]
    )
    up_held = sums_of_cores(mine, other)
    total_down, grads = lax.optimization_barrier((total_down, grads))
    total_down = lax.psum_scatter(total_down.reshape(layers, quarter, -1), "narrow")
    grads, up_moved = beside(
        lambda v: heads_back(v, grad_mixed, spans[1:]), grads, up_held[1:3], planes()
    )
    sends = second_sends(up_held, up_moved)
    grads, sends = lax.optimization_barrier((grads, sends))
    mine_theirs, moved = beside(
        lambda v: outer(place, [(normed, v)], width), grads, sends, planes()
    )
    mine_theirs, total_down = lax.optimization_barrier((mine_theirs, total_down))
    mine, theirs = by_core(mine_theirs, 3)
    total_up = halve(own_sum(up_held[0], up_moved, moved))
    total_out = total_up[layers * short :].reshape(short, layers, quarter).transpose(1, 0, 2)
    total_up = total_up[: layers * short].reshape(layers, short, width)
    total_up = jnp.concatenate([total_up, total_out], axis=2)
    total_up, theirs = lax.optimization_barrier((total_up, theirs))
    total_up = lax.psum_scatter(total_up, "narrow")
    held = sums_of_cores(mine, cross(theirs, 0))
    grad_q, grad_k, grad_v = grads
    (grad_rows, sums), first = beside(
        lambda v: inputs_back(place, rows, grad_middle, v, grad_k, grad_v, table, stats, one),
        grad_q,
        held[1:3],
        planes(),
    )
    others = [sums] * (layers - 1)
    sums, moved = beside(
        lambda v: v, sums, [*second_sends(held, first), *others], planes() + shifts(layers)
    )
    second = moved[:2]
    for piece_sums in moved[2:]:
        sums = sums + piece_sums
    total_qkv = halve(own_sum(held[0], first, second))
    blocks = jnp.concatenate([total_qkv[i * short : (i + 1) * short] for i in range(3)], axis=1)
    own_block, sends, moves = columns_blocks(blocks, part, layers)
    both = [lambda v: exchange(v, "wide", lambda i: i ^ 6)]

    def last_part(value):
        sums, total_up, total_down = value
        return sums, total_up.astype(F32), total_down.astype(F32).T

    (sums, total_up, total_down), moved = beside(
        last_part, (sums, total_up, total_down), [*sends, sums, sums, sums], moves + planes() + both
    )
    total_qkv = own_columns(own_block, moved[: layers - 1], part, blocks.shape[1])
    for piece_sums in moved[layers - 1 :]:
        sums = sums + piece_sums
    for bit in (0, *range(3, wide_bits())):
        sums = sums + cross(sums, bit)

    own = lax.dynamic_slice(sums, (0, small_spot[1]), (16, piece))
    own_up = lax.dynamic_slice(sums, (STATS_UP + up_spot[0], up_spot[1]), (1, long))[0]
    return (
        result.reshape(patches.shape),
        grad_rows.reshape(patches.shape),
        total_qkv,
        total_up[:, width:],
        total_up[:, :width],
        total_down,
        own[STATS_ONE],
        own[STATS_ONE + 1],
        own[STATS_ONE + 2],
        own[STATS_ONE + 3],
        own[5],
        own[4],
        own[2],
        own[3],
        own_up,
        own[1],
        own[0],
    )


def solution(mesh):
    return jax.shard_map(
        shards,
        mesh=mesh,
        in_specs=(
            P(("wide", "narrow"), None, None),
            P(("wide", "narrow"), None),
            P("wide", "narrow"),
            P("wide", "narrow"),
            P("wide", "narrow"),
            P("wide", "narrow"),
            P(("wide", "narrow")),
            P(("wide", "narrow")),
            P(("wide", "narrow")),
            P(("wide", "narrow")),
            P(("wide", "narrow")),
            P(("wide", "narrow")),
            P(("wide", "narrow")),
            P(("wide", "narrow")),
            P(("wide", "narrow")),
            P(("wide", "narrow")),
            P(("wide", "narrow")),
            P(("wide", "narrow"), None, None),
        ),
        out_specs=(
            P(("wide", "narrow"), None, None),
            P(("wide", "narrow"), None, None),
            P("wide", "narrow"),
            P("wide", "narrow"),
            P("wide", "narrow"),
            P("wide", "narrow"),
            P(("wide", "narrow")),
            P(("wide", "narrow")),
            P(("wide", "narrow")),
            P(("wide", "narrow")),
            P(("wide", "narrow")),
            P(("wide", "narrow")),
            P(("wide", "narrow")),
            P(("wide", "narrow")),
            P(("wide", "narrow")),
            P(("wide", "narrow")),
            P(("wide", "narrow")),
        ),
        check_vma=False,
    )
```

```python
import functools
import math

import jax
import jax.numpy as jnp
from jax import lax
from jax.experimental import pallas as pl
from jax.experimental.pallas import tpu as pltpu
from jax.sharding import PartitionSpec as P

HD = 64
HEADS = 4
LN_EPSILON = 1e-06
MASKED = -1e30
TILE = 256
F32 = jnp.float32
BF16 = jnp.bfloat16
MIB = 1 << 20


def exchange(value, axis_name, partner):
    size = lax.axis_size(axis_name)
    return lax.ppermute(value, axis_name, [(i, partner(i) % size) for i in range(size)])


def cross(value, bit):
    return exchange(value, "wide", lambda i: i ^ (1 << bit))


def shift(value, step):
    return exchange(value, "narrow", lambda i: i + step)


def wide_bits():
    return lax.axis_size("wide").bit_length() - 1


def by_origin(pieces):
    size = len(pieces)
    backward = jnp.stack(pieces[::-1])
    twice = jnp.concatenate([backward, backward])
    return lax.dynamic_slice_in_dim(twice, size - 1 - lax.axis_index("narrow"), size)


def flip_own(stacked):
    here = lax.axis_index("wide")
    size = stacked.shape[0]
    for bit in range(size.bit_length() - 1):
        halves = stacked.reshape((size >> (bit + 1), 2, 1 << bit) + stacked.shape[1:])
        halves = jnp.where((here >> bit) & 1, halves[:, ::-1], halves)
        stacked = halves.reshape(stacked.shape)
    return stacked


def after(value, *others):
    return lax.optimization_barrier((value, others))[0]


def beside(run, value, sends, moves):
    value, sends = lax.optimization_barrier((value, sends))
    moved = [move(send) for move, send in zip(moves, sends, strict=True)]
    return lax.optimization_barrier((run(value), moved))


def beside_loose(run, value, sends, moves):
    return beside(run, value, sends, moves)


def planes():
    return [lambda v: cross(v, 1), lambda v: cross(v, 2)]


def corners():
    return [lambda v: cross(v, 2), lambda v: cross(v, 1)]


def shifts(layers):
    return [lambda v, step=step: shift(v, step) for step in range(1, layers)]


def double(block):
    held = block[None]
    for bit in range(3, wide_bits()):
        held = jnp.concatenate([held, cross(held, bit)])
    return held


def side_by_side(stacked):
    return jnp.concatenate([stacked[i] for i in range(stacked.shape[0])], axis=1)


def direct():
    return lax.axis_size("wide") == 8


def in_order(stacked, parts):
    places, rows, columns = stacked.shape
    unit = rows // parts
    if parts == 1 or not direct():
        stacked = stacked.reshape(places, parts, unit, columns)
        arrays = [stacked[:, m].reshape(-1, columns) for m in range(parts)]
        return arrays, [[(m, 0, 0, None, unit)] for m in range(parts)]
    return [stacked], [[(0, at, m * unit, at, -unit) for at in range(places)] for m in range(parts)]


def matrices(planes, cores, parts, short, long):
    unit = (planes[0].shape[1] - 16) // parts
    behind = parts * unit
    if not direct():
        other = [*jnp.split(cores[0], 3), cores[1]]
        stacked = jnp.stack([jnp.stack(pair, axis=1) for pair in zip(planes, other)], axis=1)
        stacked = flip_own(stacked.reshape((-1,) + planes[0].shape[1:]))
        width = stacked.shape[2]
        rows = stacked[:, behind:].transpose(1, 0, 2)
        table = rows[:10, :, :short].reshape(10, width)
        up = rows[10, :, :long].reshape(-1, width)
        table = jnp.concatenate([table, up])
        table = jnp.pad(table, ((0, 16 - table.shape[0]), (0, 0)))
        stacked = stacked[:, :behind].reshape(stacked.shape[0], parts, unit, -1)
        arrays = [stacked[:, m].reshape(-1, stacked.shape[3]) for m in range(parts)]
        plans = [[(m, 0, 0, None, unit)] for m in range(parts)]
        return (arrays, plans), (table, None)
    spots = [(0, 0, 0), (1, 0, 2), (2, 0, 4), (3, 0, 6), (4, 0, 1), (4, 1, 3), (4, 2, 5), (5, 0, 7)]
    plans = [[(at, index, m * unit, rel, unit) for at, index, rel in spots] for m in range(parts)]
    return ([*planes, *cores], plans), (None, (spots, behind, short, long))


def copies(place, refs, plan, target, sems, first):
    made = []
    for at, index, row, rel, unit in plan:
        sem = sems.at[first + len(made)]
        if rel is None:
            made.append(pltpu.make_async_copy(refs[at], target, sem))
        else:
            start = -rel * unit if unit < 0 else pl.multiple_of((place ^ rel) * unit, 16)
            unit = abs(unit)
            source = refs[at].at[index, pl.ds(row, unit)]
            made.append(pltpu.make_async_copy(source, target.at[pl.ds(start, unit)], sem))
    return made


def start_all(made):
    for copy in made:
        copy.start()


def wait_all(made):
    for copy in made:
        copy.wait()


def dot(left, right):
    return lax.dot_general(left, right, (((1,), (0,)), ((), ())), preferred_element_type=F32)


def dot_tn(left, right):
    return lax.dot_general(left, right, (((0,), (0,)), ((), ())), preferred_element_type=F32)


def dot_nt(left, right):
    return lax.dot_general(left, right, (((1,), (1,)), ((), ())), preferred_element_type=F32)


def centred_rows(values):
    row_mean = jnp.mean(values, axis=-1, keepdims=True)
    centred = values - row_mean
    row_var = jnp.mean(centred * centred, axis=-1, keepdims=True)
    inverse = lax.rsqrt(row_var + LN_EPSILON)
    return centred * inverse, inverse


def norm_back(grad, unit_rows, inverse, gain):
    scaled = grad * gain
    mean_one = jnp.mean(scaled, axis=-1, keepdims=True)
    mean_two = jnp.mean(scaled * unit_rows, axis=-1, keepdims=True)
    return (scaled - mean_one - unit_rows * mean_two) * inverse


def row_sum(values):
    return jnp.sum(values, axis=0, keepdims=True)


def gelu_pair(values):
    bell = jnp.exp(values * values * -0.5)
    share = 0.5 + 0.5 * lax.erf(values * math.sqrt(0.5))
    return values * share, share + values * bell * (1.0 / math.sqrt(2.0 * math.pi))


ANY = pl.BlockSpec(memory_space=pl.ANY)
SMEM = pl.BlockSpec(memory_space=pltpu.SMEM)


def whole(shape):
    return pl.BlockSpec(shape, lambda *_: (0,) * len(shape))


def tile_of(columns):
    return pl.BlockSpec((TILE, columns), lambda i: (i, 0))


def cost(flops, moved, exps=0):
    return pl.CostEstimate(flops=flops, bytes_accessed=moved, transcendentals=exps)


def params(mib, dims=1):
    return pltpu.CompilerParams(
        vmem_limit_bytes=mib * MIB, dimension_semantics=("arbitrary",) * dims
    )


LN1_G, LN1_B, Q_B, V_B, OUT_B, ATTN_S, LN2_G, LN2_B, DOWN_B, MLP_S, UP_B = range(11)


def vector(table, row):
    return table[row : row + 1, :]


def make_table(place, pieces, layout):
    spots, _, short, long = layout
    shape = pieces.shape[1:]
    lane = lax.broadcasted_iota(jnp.int32, shape, 1)
    row = lax.broadcasted_iota(jnp.int32, shape, 0)
    table = jnp.zeros(shape, F32)
    for at, (_, _, rel) in enumerate(spots):
        spot = place ^ rel
        piece = pieces[at].astype(F32)
        table += pltpu.roll(jnp.where((row < UP_B) & (lane < short), piece, 0.0), spot * short, 1)
        start = spot * long
        up = jnp.where(lane[:1] < long, piece[UP_B : UP_B + 1], 0.0)
        up = pltpu.roll(jnp.broadcast_to(up, shape), lax.rem(start, shape[1]), 1)
        table += jnp.where(row == UP_B + start // shape[1], up, 0.0)
    return table


def project_kernel(plans, layout, place, rows, extras, *refs):
    count = len(refs) - 5 - 4
    sources, refs = refs[:count], refs[count:]
    normed, query, key, value, table, weights, pieces, sems, piece_sems = refs
    made, first = [], 0
    for m in range(3):
        made.append(copies(place[0], sources, plans[m], weights.at[m], sems, first))
        first += len(plans[m])

    @pl.when(pl.program_id(0) == 0)
    def _():
        for group in made:
            start_all(group)
        if layout is None:
            table[...] = extras[...].astype(F32)
            return
        brought = []
        for at, (source, index, _) in enumerate(layout[0]):
            piece = sources[source].at[index, pl.ds(layout[1], 16)]
            brought.append(pltpu.make_async_copy(piece, pieces.at[at], piece_sems.at[at]))
        start_all(brought)
        wait_all(brought)
        table[...] = make_table(place[0], pieces, layout)

    unit_rows, _ = centred_rows(rows[...].astype(F32))
    low = (unit_rows * vector(table, LN1_G) + vector(table, LN1_B)).astype(BF16)
    normed[...] = low

    @pl.when(pl.program_id(0) == 0)
    def _():
        for group in made:
            wait_all(group)

    query[...] = ((dot(low, weights[0]) + vector(table, Q_B)) * 0.125).astype(BF16)
    key[...] = dot(low, weights[1]).astype(BF16)
    value[...] = (dot(low, weights[2]) + vector(table, V_B)).astype(BF16)


def project(place, rows, extras, group):
    arrays, plans = group
    extras, layout = extras
    count, width = rows.shape
    if extras is None:
        extras = jnp.zeros((16, width), BF16)
    return pl.pallas_call(
        functools.partial(project_kernel, plans, layout),
        grid=(count // TILE,),
        in_specs=[SMEM, tile_of(width), whole(extras.shape)] + [ANY] * len(arrays),
        out_specs=[tile_of(width)] * 4 + [whole((16, width))],
        out_shape=[jax.ShapeDtypeStruct(rows.shape, BF16)] * 4
        + [jax.ShapeDtypeStruct((16, width), F32)],
        scratch_shapes=[
            pltpu.VMEM((3, width, width), BF16),
            pltpu.VMEM((8, 16, width), BF16),
            pltpu.SemaphoreType.DMA((sum(len(p) for p in plans[:3]),)),
            pltpu.SemaphoreType.DMA((8,)),
        ],
        compiler_params=params(60),
        cost_estimate=cost(6 * count * width * width, 14 * count * width),
        name="project",
    )(place, rows, extras, *arrays)


def segments(lengths, pack, position):
    end, segment = 0, jnp.zeros_like(position)
    for slot in range(lengths.shape[1] - 1):
        end = end + lengths[pack, slot]
        segment = segment + (position >= end).astype(jnp.int32)
    return jnp.where(position < end, segment, lengths.shape[1] + position)


def same_segment(lengths, pack, rows):
    down = lax.broadcasted_iota(jnp.int32, (rows, 128), 0)
    along = lax.broadcasted_iota(jnp.int32, (1, rows), 1)
    column = segments(lengths, pack, down)
    row = segments(lengths, pack, along)
    return jnp.concatenate([column] * (rows // 128), axis=1) == row


def head_lanes(shape, head):
    lane = lax.broadcasted_iota(jnp.int32, shape, 1)
    return (lane >= head * HD) & (lane < (head + 1) * HD)


def by_lanes(heads):
    chosen = heads[-1]
    for head in reversed(range(len(heads) - 1)):
        chosen = jnp.where(head_lanes(chosen.shape, head), heads[head], chosen)
    return chosen


def only(values, head):
    return jnp.where(head_lanes(values.shape, head), values, jnp.zeros_like(values))


def attend_kernel(pack, lengths, query, key, value, *refs):
    attended, kept = refs[-2:]
    rows = query.shape[0]
    same = same_segment(lengths, pack, rows)
    flat = jnp.transpose(value[...].astype(F32)).astype(BF16)
    mixed = []
    for head in range(HEADS):
        scores = dot_nt(key[...], only(query[...], head))
        scores = jnp.where(same, scores, MASKED)
        top = jnp.max(scores, axis=0, keepdims=True)
        powers = jnp.exp(scores - top)
        total = jnp.sum(powers, axis=0, keepdims=True)
        weights = (powers * (1.0 / total)).astype(BF16)
        mixed.append(dot(flat[head * HD : (head + 1) * HD], weights))
        kept[head] = weights
    attended[...] = jnp.transpose(jnp.concatenate(mixed, axis=0)).astype(BF16)


def pair_block(rows, pack, first=0):
    return pl.BlockSpec((rows, HEADS * HD), lambda h: (pack, h + first))


def kept_block(rows, first=0):
    return pl.BlockSpec((HEADS, rows, rows), lambda h: (h + first, 0, 0))


def attend(lengths, query, key, value, pack, earlier=()):
    packs = lengths.shape[0]
    count, width = query.shape
    rows, pairs = count // packs, width // (HEADS * HD)
    return pl.pallas_call(
        functools.partial(attend_kernel, pack),
        grid=(pairs,),
        in_specs=[SMEM] + [pair_block(rows, pack)] * 3 + [ANY] * len(earlier),
        out_specs=[pair_block(rows, pack), kept_block(rows)],
        out_shape=[
            jax.ShapeDtypeStruct(query.shape, BF16),
            jax.ShapeDtypeStruct((HEADS * pairs, rows, rows), BF16),
        ],
        input_output_aliases={4 + i: i for i in range(len(earlier))},
        compiler_params=params(60),
        cost_estimate=cost(16 * rows * rows * width, 8 * rows * width) if earlier else cost(0, 0),
        name="attend",
    )(lengths, query, key, value, *earlier)


def attend_back_kernel(query, key, value, grad, kept, *refs):
    grad_q, grad_k, grad_v = refs[-3:]
    flat_key = jnp.transpose(key[...].astype(F32)).astype(BF16)
    by_query, by_key, by_value = [], [], []
    for head in range(HEADS):
        weights = kept[head]
        probs = weights.astype(F32)
        by_value.append(dot(weights, grad[...]))
        grad_probs = dot_nt(value[...], only(grad[...], head))
        centre = jnp.sum(grad_probs * probs, axis=0, keepdims=True)
        grad_scores = (probs * (grad_probs - centre)).astype(BF16)
        by_key.append(dot(grad_scores, query[...]))
        by_query.append(dot(flat_key[head * HD : (head + 1) * HD], grad_scores))
    grad_k[...] = by_lanes(by_key).astype(BF16)
    grad_v[...] = by_lanes(by_value).astype(BF16)
    grad_q[...] = jnp.transpose(jnp.concatenate(by_query, axis=0)).astype(BF16) * 0.125


def attend_back(query, key, value, grad, kept, pack, first, last, earlier=()):
    rows = kept.shape[1]
    width = query.shape[1]
    part = last - first
    return pl.pallas_call(
        attend_back_kernel,
        grid=(part,),
        in_specs=[pair_block(rows, pack, first)] * 4
        + [kept_block(rows, first)]
        + [ANY] * len(earlier),
        out_specs=[pair_block(rows, pack, first)] * 3,
        out_shape=[jax.ShapeDtypeStruct(query.shape, BF16)] * 3,
        input_output_aliases={5 + i: i for i in range(len(earlier))},
        compiler_params=params(60),
        cost_estimate=cost(32 * rows * rows * HEADS * HD * part, 14 * rows * HEADS * HD * part, 0),
        name="attend_back",
    )(query, key, value, grad, kept, *earlier)


def live_rows(lengths, shape):
    tiles = pl.num_programs(0) // lengths.shape[0]
    step = pl.program_id(0)
    pack = step // tiles
    end = 0
    for slot in range(lengths.shape[1] - 1):
        end = end + lengths[pack, slot]
    position = lax.broadcasted_iota(jnp.int32, shape, 0) + (step - pack * tiles) * shape[0]
    return position < end


def hidden_kernel(out_plan, up_plans, sizes, place, lengths, rows, mixed, cotangent, table, *refs):
    sources, refs = refs[: sum(sizes)], refs[sum(sizes) :]
    one, two = sources[: sizes[0]], sources[sizes[0] :]
    branch_out, normed, active, slope, grad_down, out_w, up_w, sems = refs
    made = [copies(place[0], one, out_plan, out_w, sems, 0)]
    first = len(out_plan)
    for m, plan in enumerate(up_plans):
        made.append(copies(place[0], two, plan, up_w.at[m], sems, first))
        first += len(plan)

    @pl.when(pl.program_id(0) == 0)
    def _():
        for group in made:
            start_all(group)
        wait_all(made[0])

    branch = dot(mixed[...], out_w[...]) + vector(table, OUT_B)
    branch_out[...] = branch
    middle = rows[...].astype(F32) + vector(table, ATTN_S) * branch
    unit_rows, _ = centred_rows(middle)
    low = (unit_rows * vector(table, LN2_G) + vector(table, LN2_B)).astype(BF16)
    normed[...] = low
    live = live_rows(lengths, cotangent.shape)
    grad_out = jnp.where(live, cotangent[...].astype(F32), 0.0)
    grad_down[...] = (grad_out * vector(table, MLP_S)).astype(BF16)

    width = low.shape[1]
    for m in range(len(up_plans)):

        @pl.when(pl.program_id(0) == 0)
        def _(m=m):
            wait_all(made[m + 1])

        part = slice(m * width, (m + 1) * width)
        up = dot(low, up_w[m]) + vector(table, UP_B + m)
        value, rate = gelu_pair(up)
        active[:, part] = value.astype(BF16)
        slope[:, part] = rate.astype(BF16)


def hidden(place, lengths, rows, mixed, cotangent, table, group_one, group_two):
    count, width = rows.shape
    hidden_units = width * len(group_two[1])
    out_plan, up_plans = group_one[1][3], group_two[1]
    sizes = (len(group_one[0]), len(group_two[0]))
    return pl.pallas_call(
        functools.partial(hidden_kernel, out_plan, up_plans, sizes),
        grid=(count // TILE,),
        in_specs=[SMEM, SMEM]
        + [tile_of(width)] * 3
        + [whole(table.shape)]
        + [ANY] * sum(sizes),
        out_specs=[tile_of(width)] * 2 + [tile_of(hidden_units)] * 2 + [tile_of(width)],
        out_shape=[
            jax.ShapeDtypeStruct(rows.shape, F32),
            jax.ShapeDtypeStruct(rows.shape, BF16),
            jax.ShapeDtypeStruct((count, hidden_units), BF16),
            jax.ShapeDtypeStruct((count, hidden_units), BF16),
            jax.ShapeDtypeStruct(rows.shape, BF16),
        ],
        scratch_shapes=[
            pltpu.VMEM((width, width), BF16),
            pltpu.VMEM((len(up_plans), width, width), BF16),
            pltpu.SemaphoreType.DMA((len(out_plan) + sum(len(p) for p in up_plans),)),
        ],
        compiler_params=params(60),
        cost_estimate=cost(14 * count * width * hidden_units // 4, 26 * count * width, 2 * count * hidden_units),
        name="hidden",
    )(place, lengths, rows, mixed, cotangent, table, *group_one[0], *group_two[0])


STATS_UP, STATS_ONE = 6, 10


def back_kernel(
    out_plan, up_plans, down_plan, sizes, place, lengths, rows, branch_in, active, slope, grad_down, cotangent,
    table, *refs,
):
    sources, refs = refs[: sum(sizes)], refs[sum(sizes) :]
    one, two = sources[: sizes[0]], sources[sizes[0] : sizes[0] + sizes[1]]
    three = sources[sizes[0] + sizes[1] :]
    result, grad_hidden, grad_middle_out, grad_branch, grad_mixed, stats = refs[:6]
    out_w, up_w, down_w, sems = refs[6:]
    made = [copies(place[0], three, down_plan, down_w, sems, 0)]
    first = len(down_plan)
    for m, plan in enumerate(up_plans):
        made.append(copies(place[0], two, plan, up_w.at[m], sems, first))
        first += len(plan)
    made.append(copies(place[0], one, out_plan, out_w, sems, first))

    @pl.when(pl.program_id(0) == 0)
    def _():
        for group in made:
            start_all(group)
        stats[...] = jnp.zeros_like(stats)
        wait_all(made[0])

    live = live_rows(lengths, cotangent.shape)
    branch = branch_in[...]
    middle = rows[...].astype(F32) + vector(table, ATTN_S) * branch
    down_out = dot(active[...], down_w[...]) + vector(table, DOWN_B)
    result[...] = jnp.where(live, middle + vector(table, MLP_S) * down_out, 0.0).astype(BF16)
    grad_out = jnp.where(live, cotangent[...].astype(F32), 0.0)
    sums = [row_sum(grad_out * down_out), row_sum(grad_down[...].astype(F32))]

    @pl.when(pl.program_id(0) == 0)
    def _():
        for group in made[1:]:
            wait_all(group)

    width = middle.shape[1]
    grad_normed = jnp.zeros(middle.shape, F32)
    for m in range(len(up_plans)):
        part = slice(m * width, (m + 1) * width)
        grad_active = dot_nt(grad_down[...], down_w[part, :])
        low = (grad_active * slope[:, part].astype(F32)).astype(BF16)
        grad_hidden[:, part] = low
        stats[STATS_UP + m : STATS_UP + m + 1, :] += row_sum(low.astype(F32))
        grad_normed += dot_nt(low, up_w[m])
    unit_rows, inverse = centred_rows(middle)
    sums += [row_sum(grad_normed * unit_rows), row_sum(grad_normed)]
    grad_middle = grad_out + norm_back(grad_normed, unit_rows, inverse, vector(table, LN2_G))
    grad_middle_out[...] = grad_middle
    low = (grad_middle * vector(table, ATTN_S)).astype(BF16)
    grad_branch[...] = low
    sums += [row_sum(grad_middle * branch), row_sum(low.astype(F32))]
    grad_mixed[...] = dot_nt(low, out_w[...]).astype(BF16)
    for at, total in enumerate(sums):
        stats[at : at + 1, :] += total


def back(place, lengths, rows, branch, active, slope, grad_down, cotangent, table, one, two, three):
    count, width = rows.shape
    hidden_units = active.shape[1]
    plans = (one[1][3], two[1], three[1][0])
    sizes = (len(one[0]), len(two[0]), len(three[0]))
    return pl.pallas_call(
        functools.partial(back_kernel, *plans, sizes),
        grid=(count // TILE,),
        in_specs=[SMEM, SMEM]
        + [tile_of(width)] * 2
        + [tile_of(hidden_units)] * 2
        + [tile_of(width)] * 2
        + [whole(table.shape)]
        + [ANY] * sum(sizes),
        out_specs=[tile_of(width), tile_of(hidden_units)]
        + [tile_of(width)] * 3
        + [whole((16, width))],
        out_shape=[
            jax.ShapeDtypeStruct(rows.shape, BF16),
            jax.ShapeDtypeStruct(active.shape, BF16),
            jax.ShapeDtypeStruct(rows.shape, F32),
            jax.ShapeDtypeStruct(rows.shape, BF16),
            jax.ShapeDtypeStruct(rows.shape, BF16),
            jax.ShapeDtypeStruct((16, width), F32),
        ],
        scratch_shapes=[
            pltpu.VMEM((width, width), BF16),
            pltpu.VMEM((len(plans[1]), width, width), BF16),
            pltpu.VMEM((hidden_units, width), BF16),
            pltpu.SemaphoreType.DMA(
                (len(plans[0]) + sum(len(p) for p in plans[1]) + len(plans[2]),)
            ),
        ],
        compiler_params=params(60),
        cost_estimate=cost(26 * count * width * hidden_units // 4, 40 * count * width),
        name="back",
    )(place, lengths, rows, branch, active, slope, grad_down, cotangent, table, *one[0], *two[0], *three[0])


def outer_kernel(spread, steps, place, *refs):
    lefts, refs = refs[: len(steps)], refs[len(steps) :]
    count = sum(len(own) for own in steps)
    rights, outs = refs[:count], refs[count:]
    step = pl.program_id(0)

    def put(left, right):
        value = dot_tn(left[...], right[...]).astype(BF16)
        if not spread:
            outs[0][...] = value
            return
        plane, core = place[0] // 2, place[0] % 2
        unit = value.shape[0] // 8
        for own in range(2):

            @pl.when(core == own)
            def _(own=own):
                for at in range(4):
                    for out, part in zip(outs, (own, 1 - own)):
                        first = (2 * at + part) * unit
                        out[at ^ plane, 0] = value[first : first + unit]

    first, at_right = 0, 0
    for left, own in zip(lefts, steps):
        for count in own:

            @pl.when((step >= first) & (step < first + count))
            def _(left=left, right=rights[at_right]):
                put(left, right)

            first += count
            at_right += 1


def outer(place, pairs, width):
    count, height = pairs[0][0].shape
    steps = [[right.shape[1] // width for right in rights] for _, rights in pairs]
    total = sum(sum(own) for own in steps)
    right_specs, first = [], 0
    for own in sum(steps, []):
        right_specs.append(
            pl.BlockSpec(
                (count, width),
                lambda i, first=first, own=own: (0, jnp.clip(i - first, 0, own - 1)),
            )
        )
        first += own
    if direct():
        block = pl.BlockSpec((4, 1, height // 8, width), lambda i: (0, i, 0, 0))
        shape = jax.ShapeDtypeStruct((4, total, height // 8, width), BF16)
        specs, shapes = [block, block], [shape, shape]
    else:
        specs = pl.BlockSpec((height, width), lambda i: (0, i))
        shapes = jax.ShapeDtypeStruct((height, total * width), BF16)
    return pl.pallas_call(
        functools.partial(outer_kernel, direct(), steps),
        grid=(total,),
        in_specs=[SMEM] + [whole((count, height))] * len(pairs) + right_specs,
        out_specs=specs,
        out_shape=shapes,
        compiler_params=params(54),
        cost_estimate=cost(2 * count * height * total * width, 2 * (count + height) * total * width),
        name="outer",
    )(place, *(left for left, _ in pairs), *(right for _, rights in pairs for right in rights))


def wide_outer_kernel(left, right, out):
    value = dot_tn(left[...], right[...]).astype(BF16)
    half = value.shape[1] // 2
    out[0] = value[:, :half]
    out[1] = value[:, half:]


def wide_outer(place, left, right):
    count, height = left.shape
    columns = right.shape[1]
    steps = 8
    step = columns // steps
    return pl.pallas_call(
        wide_outer_kernel,
        grid=(steps // 2,),
        in_specs=[whole(left.shape), pl.BlockSpec((count, 2 * step), lambda i: (0, i))],
        out_specs=pl.BlockSpec((2, height, step), lambda i: (i, 0, 0)),
        out_shape=jax.ShapeDtypeStruct((steps, height, step), BF16),
        compiler_params=params(60),
        cost_estimate=cost(2 * count * height * columns, 2 * (count + height) * (height + columns)),
        name="wide_outer",
    )(left, right)


def inputs_kernel(plans, place, rows, grad_middle, grad_q, grad_k, grad_v, table, earlier, *refs):
    count = len(refs) - 2 - 2
    sources, (grad_rows, stats, weights, sems) = refs[:count], refs[count:]
    made, first = [], 0
    for m in range(3):
        made.append(copies(place[0], sources, plans[m], weights.at[m], sems, first))
        first += len(plans[m])

    @pl.when(pl.program_id(0) == 0)
    def _():
        for group in made:
            start_all(group)
        stats[...] = earlier[...]
        for group in made:
            wait_all(group)

    grad = dot_nt(grad_q[...], weights[0])
    grad += dot_nt(grad_k[...], weights[1])
    grad += dot_nt(grad_v[...], weights[2])
    unit_rows, inverse = centred_rows(rows[...].astype(F32))
    grad_rows[...] = grad_middle[...] + norm_back(grad, unit_rows, inverse, vector(table, LN1_G))
    sums = [row_sum(grad * unit_rows), row_sum(grad)]
    sums += [row_sum(grad_q[...].astype(F32)), row_sum(grad_v[...].astype(F32))]
    for at, total in enumerate(sums):
        stats[STATS_ONE + at : STATS_ONE + at + 1, :] += total


def inputs_back(place, rows, grad_middle, grad_q, grad_k, grad_v, table, earlier, group):
    arrays, plans = group
    count, width = rows.shape
    return pl.pallas_call(
        functools.partial(inputs_kernel, plans),
        grid=(count // TILE,),
        in_specs=[SMEM] + [tile_of(width)] * 5 + [whole(table.shape)] * 2 + [ANY] * len(arrays),
        out_specs=[tile_of(width), whole((16, width))],
        out_shape=[
            jax.ShapeDtypeStruct(rows.shape, F32),
            jax.ShapeDtypeStruct((16, width), F32),
        ],
        scratch_shapes=[
            pltpu.VMEM((3, width, width), BF16),
            pltpu.SemaphoreType.DMA((sum(len(p) for p in plans[:3]),)),
        ],
        compiler_params=params(60),
        cost_estimate=cost(6 * count * width * width, 20 * count * width),
        name="inputs_back",
    )(place, rows, grad_middle, grad_q, grad_k, grad_v, table, earlier, *arrays)


def add_low(left, right):
    return (left.astype(F32) + right.astype(F32)).astype(left.dtype)


def split_cores(stacked):
    stacked = flip_own(stacked)
    pieces = stacked.reshape((-1, 2) + stacked.shape[1:])
    return pieces[:, 0], pieces[:, 1]


def quarters(held):
    held = held.reshape((-1, 4) + held.shape[1:])
    return tuple(held[:, i] for i in range(4))


def add_kernel(mine, other, own, by_x, by_y, near, far):
    total = (mine[...].astype(F32) + other[...].astype(F32)).astype(BF16)
    own[0] = total[0]
    early = pl.program_id(0) < pl.num_programs(0) // 2

    @pl.when(early)
    def _():
        by_x[0] = total[3]
        by_x[1] = total[1]
        far[0] = total[2]

    @pl.when(jnp.logical_not(early))
    def _():
        by_y[0] = total[3]
        by_y[1] = total[2]
        near[0] = total[1]


def sums_of_cores(mine, other):
    rows, columns = mine.shape[1:]
    half = rows // 2
    if not direct():
        own, near, far, corner = quarters(add_low(mine, other))
        by_x = jnp.stack([corner[:, :half], near[:, :half]], axis=1)
        by_y = jnp.stack([corner[:, half:], far[:, half:]], axis=1)
        return own, by_x, by_y, near[:, half:], far[:, :half]
    shapes = [(1, rows, columns), (2, half, columns), (2, half, columns), (1, half, columns), (1, half, columns)]
    steps = 2
    step = rows // steps
    spots = [
        lambda i: i,
        lambda i: jnp.minimum(i, steps // 2 - 1),
        lambda i: jnp.maximum(i - steps // 2, 0),
        lambda i: jnp.maximum(i - steps // 2, 0),
        lambda i: jnp.minimum(i, steps // 2 - 1),
    ]
    own, by_x, by_y, near, far = pl.pallas_call(
        add_kernel,
        grid=(steps,),
        in_specs=[pl.BlockSpec((4, step, columns), lambda i: (0, i, 0))] * 2,
        out_specs=[
            pl.BlockSpec((shape[0], step, columns), lambda i, spot=spot: (0, spot(i), 0))
            for shape, spot in zip(shapes, spots)
        ],
        out_shape=[jax.ShapeDtypeStruct(shape, BF16) for shape in shapes],
        compiler_params=params(24),
        cost_estimate=cost(4 * rows * columns, 24 * rows * columns),
        name="core_add",
    )(mine, other)
    return own, by_x[None], by_y[None], near, far


def second_sends(held, first):
    by_x, by_y = first
    return [add_low(held[3], by_y[:, 0]), add_low(held[4], by_x[:, 0])]


def own_sum(own, first, second):
    (by_x, by_y), (near, far) = first, second
    total = own.astype(F32) + jnp.concatenate([by_x[:, 1], near], axis=1).astype(F32)
    total = total + jnp.concatenate([far, by_y[:, 1]], axis=1).astype(F32)
    return total.astype(BF16)


def halve(total):
    for bit in reversed(range(3, wide_bits())):
        count = total.shape[0] // 2
        total = add_low(total[:count], cross(total[count:], bit))
    return total[0]


def spread_blocks(stacked):
    size = stacked.shape[0]
    here = lax.axis_index("narrow")
    steps = sorted(range(1, size), key=lambda step: min(step, size - step))
    blocks = [
        lax.dynamic_index_in_dim(stacked, lax.rem(here + step, size), keepdims=False)
        for step in steps
    ]
    return blocks, [lambda v, step=step: shift(v, step) for step in steps]


def add_blocks(stacked, moved):
    total = lax.dynamic_index_in_dim(stacked, lax.axis_index("narrow"), keepdims=False)
    total = total.astype(F32)
    for block in moved:
        total = total + block.astype(F32)
    return total


def column_starts(columns, part, layers):
    starts = [at * part // 128 * 128 for at in range(layers)]
    room = max(-(-(at + 1) * part // 128) * 128 - starts[at] for at in range(layers))
    return [min(start, columns - room) for start in starts], room


def columns_blocks(blocks, part, layers):
    here = lax.axis_index("narrow")
    starts, room = column_starts(blocks.shape[1], part, layers)
    choices = [blocks[:, start : start + room] for start in starts]

    def block_of(index):
        chosen = choices[-1]
        for at in reversed(range(layers - 1)):
            chosen = jnp.where(index == at, choices[at], chosen)
        return chosen

    own, *sends = [block_of(lax.rem(here + step, layers)) for step in range(layers)]
    return own, sends, shifts(layers)


def own_columns(own, moved, part, columns):
    layers = len(moved) + 1
    here = lax.axis_index("narrow")
    starts, _ = column_starts(columns, part, layers)
    total = own.astype(F32)
    for block in moved:
        total = total + block.astype(F32)
    cuts = [total[:, at * part - start : (at + 1) * part - start] for at, start in enumerate(starts)]
    result = cuts[-1]
    for at in reversed(range(layers - 1)):
        result = jnp.where(here == at, cuts[at], result)
    return result


def by_core(grad, parts):
    if direct():
        return tuple(piece.reshape(4, -1, piece.shape[3]) for piece in grad)
    places = lax.axis_size("wide")
    height, columns = grad.shape
    stacked = grad.reshape(places, height // places, parts, columns // parts).transpose(0, 2, 1, 3)
    return split_cores(stacked.reshape(places, -1, columns // parts))


def own_spot(places, layers, piece, width):
    start = (lax.axis_index("wide") * layers + lax.axis_index("narrow")) * piece
    return start // width, start % width


def shards(
    patches, lengths, w_qkv, w_out, w_up, w_down, ln1_gain, ln1_bias, q_bias, v_bias, out_bias, attn_scale,
    ln2_gain, ln2_bias, up_bias, down_bias, mlp_scale, cotangent,
):
    places, layers = lax.axis_size("wide"), lax.axis_size("narrow")
    place = lax.axis_index("wide").astype(jnp.int32).reshape(1)
    short, width = w_up.shape
    part = w_qkv.shape[1]
    quarter = w_out.shape[1]
    packs, pack_rows, _ = patches.shape
    rows = patches.reshape(-1, width)
    cotangent = cotangent.reshape(-1, width)

    small = [ln1_gain, ln1_bias, q_bias, v_bias, out_bias, attn_scale, ln2_gain, ln2_bias, down_bias, mlp_scale]
    piece, long = ln1_gain.shape[0], up_bias.shape[0]
    small_spot = own_spot(places, layers, piece, width)
    up_spot = own_spot(places, layers, long, width)
    extra = jnp.pad(jnp.stack(small), ((0, 0), (0, part - piece)))
    extra = jnp.concatenate([extra, jnp.pad(up_bias[None], ((0, 5), (0, part - long)))])
    extra = jnp.pad(extra, ((0, 0), (0, quarter)))
    early = jnp.concatenate([jnp.concatenate([w_qkv, w_out], axis=1), extra])

    moved = [move(early) for move in shifts(layers)]
    one = by_origin([early, *moved])
    extra = side_by_side(one[:, short : short + 10, :piece])
    extra = jnp.pad(extra, ((0, 6), (0, width - layers * piece)))
    long_row = side_by_side(one[:, short + 10 : short + 11, :long])
    long_row = jnp.pad(long_row, ((10, 5), (0, width - layers * long)))
    qkv, out = side_by_side(one[:, :short, :part]), side_by_side(one[:, :short, part:])
    one = jnp.concatenate([*jnp.split(qkv, 3, axis=1), out, extra + long_row])
    held = double(one)
    sends = [held, held] + [w_up] * (layers - 1)
    (near, far, *two) = [move(send) for move, send in zip(planes() + shifts(layers), sends)]
    near, far, two = lax.optimization_barrier((near, far, two))
    half = near.shape[1] // 32 * 16
    sends = [near[:, :half], far[:, half:], jnp.concatenate([held, near, far])]
    two = by_origin([w_up, *two]).reshape(-1, width)
    two, sends = lax.optimization_barrier((two, sends))
    two = in_order(lax.all_gather(two, "wide"), layers)
    moves = corners() + [lambda v: cross(v, 0)]
    moved = lax.optimization_barrier([move(send) for move, send in zip(moves, sends)])
    planes_one = held, near, far, jnp.concatenate(moved[:2], axis=1)
    side_down = jnp.concatenate(jnp.split(w_down, layers, axis=0), axis=1)
    side_down = after(side_down, moved)
    one, extras = matrices(planes_one, (moved[2], cross(planes_one[3], 0)), 4, layers * piece, layers * long)

    (normed, query, key, value, table), three = beside(
        lambda v: project(place, v, extras, one), rows, [side_down] * (layers - 1), shifts(layers)
    )
    three = by_origin([side_down, *three])
    three = jnp.concatenate(
        [side_by_side(three[:, :, i * quarter : (i + 1) * quarter]) for i in range(layers)]
    )
    query, three = lax.optimization_barrier((query, three))
    three = in_order(lax.all_gather(three, "wide"), 1)
    kept, mixed = [], ()
    for pack in range(packs):
        mixed, weights = attend(lengths, query, key, value, pack, mixed)
        mixed = (mixed,)
        kept.append(weights)
    (mixed,) = mixed
    branch, normed_two, active, slope, grad_down = hidden(
        place, lengths, rows, mixed, cotangent, table, one, two
    )
    grad_w_down = wide_outer(place, grad_down, active)
    active = after(active, grad_w_down)
    if places != 8:
        grad_w_down = grad_w_down.reshape(8, width, places // 8, -1).transpose(0, 2, 1, 3)
    total_down = lax.psum_scatter(grad_w_down.reshape(places, width, -1), "wide")

    result, grad_hidden, grad_middle, grad_branch, grad_mixed, stats = back(
        place, lengths, rows, branch, active, slope, grad_down, cotangent, table, one, two, three
    )
    mine, theirs = by_core(
        outer(place, [(normed_two, [grad_hidden]), (mixed, [grad_branch])], width), layers + 1
    )
    def heads_back(grads, value, spans):
        for pack, first, last in spans:
            grads = attend_back(query, key, value_rows, value, kept[pack], pack, first, last, grads)
        return grads

    groups = width // (HEADS * HD)
    spans = [(0, 0, groups - 1), (0, groups - 1, groups)] + [(pack, 0, groups) for pack in range(1, packs)]
    value_rows = value
    grads, (other,) = beside(
        lambda v: heads_back((), v, spans[:1]), grad_mixed, [theirs], [lambda v: cross(v, 0)]
    )
    up_held = sums_of_cores(mine, other)
    total_down, grads = lax.optimization_barrier((total_down, grads))
    total_down = lax.psum_scatter(total_down.reshape(layers, quarter, -1), "narrow")
    grads, up_moved = beside(
        lambda v: heads_back(v, grad_mixed, spans[1:]), grads, up_held[1:3], planes()
    )
    sends = second_sends(up_held, up_moved)
    grads, sends = lax.optimization_barrier((grads, sends))
    mine_theirs, moved = beside(
        lambda v: outer(place, [(normed, v)], width), grads, sends, planes()
    )
    mine_theirs, total_down = lax.optimization_barrier((mine_theirs, total_down))
    mine, theirs = by_core(mine_theirs, 3)
    total_up = halve(own_sum(up_held[0], up_moved, moved))
    total_out = total_up[layers * short :].reshape(short, layers, quarter).transpose(1, 0, 2)
    total_up = total_up[: layers * short].reshape(layers, short, width)
    total_up = jnp.concatenate([total_up, total_out], axis=2)
    total_up, theirs = lax.optimization_barrier((total_up, theirs))
    total_up = lax.psum_scatter(total_up, "narrow")
    held = sums_of_cores(mine, cross(theirs, 0))
    grad_q, grad_k, grad_v = grads
    (grad_rows, sums), first = beside(
        lambda v: inputs_back(place, rows, grad_middle, v, grad_k, grad_v, table, stats, one),
        grad_q,
        held[1:3],
        planes(),
    )
    others = [sums] * (layers - 1)
    sums, moved = beside(
        lambda v: v, sums, [*second_sends(held, first), *others], planes() + shifts(layers)
    )
    second = moved[:2]
    for piece_sums in moved[2:]:
        sums = sums + piece_sums
    total_qkv = halve(own_sum(held[0], first, second))
    blocks = jnp.concatenate([total_qkv[i * short : (i + 1) * short] for i in range(3)], axis=1)
    own_block, sends, moves = columns_blocks(blocks, part, layers)
    both = [lambda v: exchange(v, "wide", lambda i: i ^ 6)]

    def last_part(value):
        sums, total_up, total_down = value
        return sums, total_up.astype(F32), total_down.astype(F32).T

    (sums, total_up, total_down), moved = beside(
        last_part, (sums, total_up, total_down), [*sends, sums, sums, sums], moves + planes() + both
    )
    total_qkv = own_columns(own_block, moved[: layers - 1], part, blocks.shape[1])
    for piece_sums in moved[layers - 1 :]:
        sums = sums + piece_sums
    for bit in (0, *range(3, wide_bits())):
        sums = sums + cross(sums, bit)

    own = lax.dynamic_slice(sums, (0, small_spot[1]), (16, piece))
    own_up = lax.dynamic_slice(sums, (STATS_UP + up_spot[0], up_spot[1]), (1, long))[0]
    return (
        result.reshape(patches.shape),
        grad_rows.reshape(patches.shape),
        total_qkv,
        total_up[:, width:],
        total_up[:, :width],
        total_down,
        own[STATS_ONE],
        own[STATS_ONE + 1],
        own[STATS_ONE + 2],
        own[STATS_ONE + 3],
        own[5],
        own[4],
        own[2],
        own[3],
        own_up,
        own[1],
        own[0],
    )


def solution(mesh):
    return jax.shard_map(
        shards,
        mesh=mesh,
        in_specs=(
            P(("wide", "narrow"), None, None),
            P(("wide", "narrow"), None),
            P("wide", "narrow"),
            P("wide", "narrow"),
            P("wide", "narrow"),
            P("wide", "narrow"),
            P(("wide", "narrow")),
            P(("wide", "narrow")),
            P(("wide", "narrow")),
            P(("wide", "narrow")),
            P(("wide", "narrow")),
            P(("wide", "narrow")),
            P(("wide", "narrow")),
            P(("wide", "narrow")),
            P(("wide", "narrow")),
            P(("wide", "narrow")),
            P(("wide", "narrow")),
            P(("wide", "narrow"), None, None),
        ),
        out_specs=(
            P(("wide", "narrow"), None, None),
            P(("wide", "narrow"), None, None),
            P("wide", "narrow"),
            P("wide", "narrow"),
            P("wide", "narrow"),
            P("wide", "narrow"),
            P(("wide", "narrow")),
            P(("wide", "narrow")),
            P(("wide", "narrow")),
            P(("wide", "narrow")),
            P(("wide", "narrow")),
            P(("wide", "narrow")),
            P(("wide", "narrow")),
            P(("wide", "narrow")),
            P(("wide", "narrow")),
            P(("wide", "narrow")),
            P(("wide", "narrow")),
        ),
        check_vma=False,
    )
```

```python
import functools
import math

import jax
import jax.numpy as jnp
from jax import lax
from jax.experimental import pallas as pl
from jax.experimental.pallas import tpu as pltpu
from jax.sharding import PartitionSpec as P

HD = 64
HEADS = 4
LN_EPSILON = 1e-06
MASKED = -1e30
TILE = 256
F32 = jnp.float32
BF16 = jnp.bfloat16
MIB = 1 << 20


def exchange(value, axis_name, partner):
    size = lax.axis_size(axis_name)
    return lax.ppermute(value, axis_name, [(i, partner(i) % size) for i in range(size)])


def cross(value, bit):
    return exchange(value, "wide", lambda i: i ^ (1 << bit))


def shift(value, step):
    return exchange(value, "narrow", lambda i: i + step)


def wide_bits():
    return lax.axis_size("wide").bit_length() - 1


def by_origin(pieces):
    size = len(pieces)
    backward = jnp.stack(pieces[::-1])
    twice = jnp.concatenate([backward, backward])
    return lax.dynamic_slice_in_dim(twice, size - 1 - lax.axis_index("narrow"), size)


def flip_own(stacked):
    here = lax.axis_index("wide")
    size = stacked.shape[0]
    for bit in range(size.bit_length() - 1):
        halves = stacked.reshape((size >> (bit + 1), 2, 1 << bit) + stacked.shape[1:])
        halves = jnp.where((here >> bit) & 1, halves[:, ::-1], halves)
        stacked = halves.reshape(stacked.shape)
    return stacked


def after(value, *others):
    return lax.optimization_barrier((value, others))[0]


def beside(run, value, sends, moves):
    value, sends = lax.optimization_barrier((value, sends))
    moved = [move(send) for move, send in zip(moves, sends, strict=True)]
    return lax.optimization_barrier((run(value), moved))


def beside_loose(run, value, sends, moves):
    return beside(run, value, sends, moves)


def planes():
    return [lambda v: cross(v, 1), lambda v: cross(v, 2)]


def corners():
    return [lambda v: cross(v, 2), lambda v: cross(v, 1)]


def shifts(layers):
    return [lambda v, step=step: shift(v, step) for step in range(1, layers)]


def double(block):
    held = block[None]
    for bit in range(3, wide_bits()):
        held = jnp.concatenate([held, cross(held, bit)])
    return held


def side_by_side(stacked):
    return jnp.concatenate([stacked[i] for i in range(stacked.shape[0])], axis=1)


def direct():
    return lax.axis_size("wide") == 8


def in_order(stacked, parts):
    places, rows, columns = stacked.shape
    unit = rows // parts
    if parts == 1 or not direct():
        stacked = stacked.reshape(places, parts, unit, columns)
        arrays = [stacked[:, m].reshape(-1, columns) for m in range(parts)]
        return arrays, [[(m, 0, 0, None, unit)] for m in range(parts)]
    return [stacked], [[(0, at, m * unit, at, -unit) for at in range(places)] for m in range(parts)]


def matrices(planes, cores, parts, short, long):
    unit = (planes[0].shape[1] - 16) // parts
    behind = parts * unit
    if not direct():
        other = [*jnp.split(cores[0], 3), cores[1]]
        stacked = jnp.stack([jnp.stack(pair, axis=1) for pair in zip(planes, other)], axis=1)
        stacked = flip_own(stacked.reshape((-1,) + planes[0].shape[1:]))
        width = stacked.shape[2]
        rows = stacked[:, behind:].transpose(1, 0, 2)
        table = rows[:10, :, :short].reshape(10, width)
        up = rows[10, :, :long].reshape(-1, width)
        table = jnp.concatenate([table, up])
        table = jnp.pad(table, ((0, 16 - table.shape[0]), (0, 0)))
        stacked = stacked[:, :behind].reshape(stacked.shape[0], parts, unit, -1)
        arrays = [stacked[:, m].reshape(-1, stacked.shape[3]) for m in range(parts)]
        plans = [[(m, 0, 0, None, unit)] for m in range(parts)]
        return (arrays, plans), (table, None)
    spots = [(0, 0, 0), (1, 0, 2), (2, 0, 4), (3, 0, 6), (4, 0, 1), (4, 1, 3), (4, 2, 5), (5, 0, 7)]
    plans = [[(at, index, m * unit, rel, unit) for at, index, rel in spots] for m in range(parts)]
    return ([*planes, *cores], plans), (None, (spots, behind, short, long))


def copies(place, refs, plan, target, sems, first):
    made = []
    for at, index, row, rel, unit in plan:
        sem = sems.at[first + len(made)]
        if rel is None:
            made.append(pltpu.make_async_copy(refs[at], target, sem))
        else:
            start = -rel * unit if unit < 0 else pl.multiple_of((place ^ rel) * unit, 16)
            unit = abs(unit)
            source = refs[at].at[index, pl.ds(row, unit)]
            made.append(pltpu.make_async_copy(source, target.at[pl.ds(start, unit)], sem))
    return made


def start_all(made):
    for copy in made:
        copy.start()


def wait_all(made):
    for copy in made:
        copy.wait()


def dot(left, right):
    return lax.dot_general(left, right, (((1,), (0,)), ((), ())), preferred_element_type=F32)


def dot_tn(left, right):
    return lax.dot_general(left, right, (((0,), (0,)), ((), ())), preferred_element_type=F32)


def dot_nt(left, right):
    return lax.dot_general(left, right, (((1,), (1,)), ((), ())), preferred_element_type=F32)


def centred_rows(values):
    row_mean = jnp.mean(values, axis=-1, keepdims=True)
    centred = values - row_mean
    row_var = jnp.mean(centred * centred, axis=-1, keepdims=True)
    inverse = lax.rsqrt(row_var + LN_EPSILON)
    return centred * inverse, inverse


def norm_back(grad, unit_rows, inverse, gain):
    scaled = grad * gain
    mean_one = jnp.mean(scaled, axis=-1, keepdims=True)
    mean_two = jnp.mean(scaled * unit_rows, axis=-1, keepdims=True)
    return (scaled - mean_one - unit_rows * mean_two) * inverse


def row_sum(values):
    return jnp.sum(values, axis=0, keepdims=True)


def gelu_pair(values):
    bell = jnp.exp(values * values * -0.5)
    share = 0.5 + 0.5 * lax.erf(values * math.sqrt(0.5))
    return values * share, share + values * bell * (1.0 / math.sqrt(2.0 * math.pi))


ANY = pl.BlockSpec(memory_space=pl.ANY)
SMEM = pl.BlockSpec(memory_space=pltpu.SMEM)


def whole(shape):
    return pl.BlockSpec(shape, lambda *_: (0,) * len(shape))


def tile_of(columns):
    return pl.BlockSpec((TILE, columns), lambda i: (i, 0))


def cost(flops, moved, exps=0):
    return pl.CostEstimate(flops=flops, bytes_accessed=moved, transcendentals=exps)


def params(mib, dims=1):
    return pltpu.CompilerParams(
        vmem_limit_bytes=mib * MIB, dimension_semantics=("arbitrary",) * dims
    )


LN1_G, LN1_B, Q_B, V_B, OUT_B, ATTN_S, LN2_G, LN2_B, DOWN_B, MLP_S, UP_B = range(11)


def vector(table, row):
    return table[row : row + 1, :]


def make_table(place, pieces, layout):
    spots, _, short, long = layout
    shape = pieces.shape[1:]
    lane = lax.broadcasted_iota(jnp.int32, shape, 1)
    row = lax.broadcasted_iota(jnp.int32, shape, 0)
    table = jnp.zeros(shape, F32)
    for at, (_, _, rel) in enumerate(spots):
        spot = place ^ rel
        piece = pieces[at].astype(F32)
        table += pltpu.roll(jnp.where((row < UP_B) & (lane < short), piece, 0.0), spot * short, 1)
        start = spot * long
        up = jnp.where(lane[:1] < long, piece[UP_B : UP_B + 1], 0.0)
        up = pltpu.roll(jnp.broadcast_to(up, shape), lax.rem(start, shape[1]), 1)
        table += jnp.where(row == UP_B + start // shape[1], up, 0.0)
    return table


def project_kernel(plans, layout, place, rows, extras, *refs):
    count = len(refs) - 5 - 4
    sources, refs = refs[:count], refs[count:]
    normed, query, key, value, table, weights, pieces, sems, piece_sems = refs
    made, first = [], 0
    for m in range(3):
        made.append(copies(place[0], sources, plans[m], weights.at[m], sems, first))
        first += len(plans[m])

    @pl.when(pl.program_id(0) == 0)
    def _():
        for group in made:
            start_all(group)
        if layout is None:
            table[...] = extras[...].astype(F32)
            return
        brought = []
        for at, (source, index, _) in enumerate(layout[0]):
            piece = sources[source].at[index, pl.ds(layout[1], 16)]
            brought.append(pltpu.make_async_copy(piece, pieces.at[at], piece_sems.at[at]))
        start_all(brought)
        wait_all(brought)
        table[...] = make_table(place[0], pieces, layout)

    unit_rows, _ = centred_rows(rows[...].astype(F32))
    low = (unit_rows * vector(table, LN1_G) + vector(table, LN1_B)).astype(BF16)
    normed[...] = low

    @pl.when(pl.program_id(0) == 0)
    def _():
        for group in made:
            wait_all(group)

    query[...] = ((dot(low, weights[0]) + vector(table, Q_B)) * 0.125).astype(BF16)
    key[...] = dot(low, weights[1]).astype(BF16)
    value[...] = (dot(low, weights[2]) + vector(table, V_B)).astype(BF16)


def project(place, rows, extras, group):
    arrays, plans = group
    extras, layout = extras
    count, width = rows.shape
    if extras is None:
        extras = jnp.zeros((16, width), BF16)
    return pl.pallas_call(
        functools.partial(project_kernel, plans, layout),
        grid=(count // TILE,),
        in_specs=[SMEM, tile_of(width), whole(extras.shape)] + [ANY] * len(arrays),
        out_specs=[tile_of(width)] * 4 + [whole((16, width))],
        out_shape=[jax.ShapeDtypeStruct(rows.shape, BF16)] * 4
        + [jax.ShapeDtypeStruct((16, width), F32)],
        scratch_shapes=[
            pltpu.VMEM((3, width, width), BF16),
            pltpu.VMEM((8, 16, width), BF16),
            pltpu.SemaphoreType.DMA((sum(len(p) for p in plans[:3]),)),
            pltpu.SemaphoreType.DMA((8,)),
        ],
        compiler_params=params(60),
        cost_estimate=cost(6 * count * width * width, 14 * count * width),
        name="project",
    )(place, rows, extras, *arrays)


def segments(lengths, pack, position):
    end, segment = 0, jnp.zeros_like(position)
    for slot in range(lengths.shape[1] - 1):
        end = end + lengths[pack, slot]
        segment = segment + (position >= end).astype(jnp.int32)
    return jnp.where(position < end, segment, lengths.shape[1] + position)


def same_segment(lengths, pack, rows):
    down = lax.broadcasted_iota(jnp.int32, (rows, 128), 0)
    along = lax.broadcasted_iota(jnp.int32, (1, rows), 1)
    column = segments(lengths, pack, down)
    row = segments(lengths, pack, along)
    return jnp.concatenate([column] * (rows // 128), axis=1) == row


def head_lanes(shape, head):
    lane = lax.broadcasted_iota(jnp.int32, shape, 1)
    return (lane >= head * HD) & (lane < (head + 1) * HD)


def by_lanes(heads):
    chosen = heads[-1]
    for head in reversed(range(len(heads) - 1)):
        chosen = jnp.where(head_lanes(chosen.shape, head), heads[head], chosen)
    return chosen


def only(values, head):
    return jnp.where(head_lanes(values.shape, head), values, jnp.zeros_like(values))


def attend_kernel(pack, lengths, query, key, value, *refs):
    attended, kept = refs[-2:]
    rows = query.shape[0]
    same = same_segment(lengths, pack, rows)
    flat = jnp.transpose(value[...].astype(F32)).astype(BF16)
    mixed = []
    for head in range(HEADS):
        scores = dot_nt(key[...], only(query[...], head))
        scores = jnp.where(same, scores, MASKED)
        top = jnp.max(scores, axis=0, keepdims=True)
        powers = jnp.exp(scores - top)
        total = jnp.sum(powers, axis=0, keepdims=True)
        weights = (powers * (1.0 / total)).astype(BF16)
        mixed.append(dot(flat[head * HD : (head + 1) * HD], weights))
        kept[head] = weights
    attended[...] = jnp.transpose(jnp.concatenate(mixed, axis=0)).astype(BF16)


def pair_block(rows, pack, first=0):
    return pl.BlockSpec((rows, HEADS * HD), lambda h: (pack, h + first))


def kept_block(rows, first=0):
    return pl.BlockSpec((HEADS, rows, rows), lambda h: (h + first, 0, 0))


def attend(lengths, query, key, value, pack, earlier=()):
    packs = lengths.shape[0]
    count, width = query.shape
    rows, pairs = count // packs, width // (HEADS * HD)
    return pl.pallas_call(
        functools.partial(attend_kernel, pack),
        grid=(pairs,),
        in_specs=[SMEM] + [pair_block(rows, pack)] * 3 + [ANY] * len(earlier),
        out_specs=[pair_block(rows, pack), kept_block(rows)],
        out_shape=[
            jax.ShapeDtypeStruct(query.shape, BF16),
            jax.ShapeDtypeStruct((HEADS * pairs, rows, rows), BF16),
        ],
        input_output_aliases={4 + i: i for i in range(len(earlier))},
        compiler_params=params(60),
        cost_estimate=cost(16 * rows * rows * width, 8 * rows * width) if earlier else cost(0, 0),
        name="attend",
    )(lengths, query, key, value, *earlier)


def attend_back_kernel(query, key, value, grad, kept, *refs):
    grad_q, grad_k, grad_v = refs[-3:]
    flat_key = jnp.transpose(key[...].astype(F32)).astype(BF16)
    by_query, by_key, by_value = [], [], []
    for head in range(HEADS):
        weights = kept[head]
        probs = weights.astype(F32)
        by_value.append(dot(weights, grad[...]))
        grad_probs = dot_nt(value[...], only(grad[...], head))
        centre = jnp.sum(grad_probs * probs, axis=0, keepdims=True)
        grad_scores = (probs * (grad_probs - centre)).astype(BF16)
        by_key.append(dot(grad_scores, query[...]))
        by_query.append(dot(flat_key[head * HD : (head + 1) * HD], grad_scores))
    grad_k[...] = by_lanes(by_key).astype(BF16)
    grad_v[...] = by_lanes(by_value).astype(BF16)
    grad_q[...] = jnp.transpose(jnp.concatenate(by_query, axis=0)).astype(BF16) * 0.125


def attend_back(query, key, value, grad, kept, pack, first, last, earlier=()):
    rows = kept.shape[1]
    width = query.shape[1]
    part = last - first
    return pl.pallas_call(
        attend_back_kernel,
        grid=(part,),
        in_specs=[pair_block(rows, pack, first)] * 4
        + [kept_block(rows, first)]
        + [ANY] * len(earlier),
        out_specs=[pair_block(rows, pack, first)] * 3,
        out_shape=[jax.ShapeDtypeStruct(query.shape, BF16)] * 3,
        input_output_aliases={5 + i: i for i in range(len(earlier))},
        compiler_params=params(60),
        cost_estimate=cost(32 * rows * rows * HEADS * HD * part, 14 * rows * HEADS * HD * part, 0),
        name="attend_back",
    )(query, key, value, grad, kept, *earlier)


def live_rows(lengths, shape):
    tiles = pl.num_programs(0) // lengths.shape[0]
    step = pl.program_id(0)
    pack = step // tiles
    end = 0
    for slot in range(lengths.shape[1] - 1):
        end = end + lengths[pack, slot]
    position = lax.broadcasted_iota(jnp.int32, shape, 0) + (step - pack * tiles) * shape[0]
    return position < end


def hidden_kernel(out_plan, up_plans, sizes, place, lengths, rows, mixed, cotangent, table, *refs):
    sources, refs = refs[: sum(sizes)], refs[sum(sizes) :]
    one, two = sources[: sizes[0]], sources[sizes[0] :]
    branch_out, normed, active, slope, grad_down, out_w, up_w, sems = refs
    made = [copies(place[0], one, out_plan, out_w, sems, 0)]
    first = len(out_plan)
    for m, plan in enumerate(up_plans):
        made.append(copies(place[0], two, plan, up_w.at[m], sems, first))
        first += len(plan)

    @pl.when(pl.program_id(0) == 0)
    def _():
        for group in made:
            start_all(group)
        wait_all(made[0])

    branch = dot(mixed[...], out_w[...]) + vector(table, OUT_B)
    branch_out[...] = branch
    middle = rows[...].astype(F32) + vector(table, ATTN_S) * branch
    unit_rows, _ = centred_rows(middle)
    low = (unit_rows * vector(table, LN2_G) + vector(table, LN2_B)).astype(BF16)
    normed[...] = low
    live = live_rows(lengths, cotangent.shape)
    grad_out = jnp.where(live, cotangent[...].astype(F32), 0.0)
    grad_down[...] = (grad_out * vector(table, MLP_S)).astype(BF16)

    width = low.shape[1]
    for m in range(len(up_plans)):

        @pl.when(pl.program_id(0) == 0)
        def _(m=m):
            wait_all(made[m + 1])

        part = slice(m * width, (m + 1) * width)
        up = dot(low, up_w[m]) + vector(table, UP_B + m)
        value, rate = gelu_pair(up)
        active[:, part] = value.astype(BF16)
        slope[:, part] = rate.astype(BF16)


def hidden(place, lengths, rows, mixed, cotangent, table, group_one, group_two):
    count, width = rows.shape
    hidden_units = width * len(group_two[1])
    out_plan, up_plans = group_one[1][3], group_two[1]
    sizes = (len(group_one[0]), len(group_two[0]))
    return pl.pallas_call(
        functools.partial(hidden_kernel, out_plan, up_plans, sizes),
        grid=(count // TILE,),
        in_specs=[SMEM, SMEM]
        + [tile_of(width)] * 3
        + [whole(table.shape)]
        + [ANY] * sum(sizes),
        out_specs=[tile_of(width)] * 2 + [tile_of(hidden_units)] * 2 + [tile_of(width)],
        out_shape=[
            jax.ShapeDtypeStruct(rows.shape, F32),
            jax.ShapeDtypeStruct(rows.shape, BF16),
            jax.ShapeDtypeStruct((count, hidden_units), BF16),
            jax.ShapeDtypeStruct((count, hidden_units), BF16),
            jax.ShapeDtypeStruct(rows.shape, BF16),
        ],
        scratch_shapes=[
            pltpu.VMEM((width, width), BF16),
            pltpu.VMEM((len(up_plans), width, width), BF16),
            pltpu.SemaphoreType.DMA((len(out_plan) + sum(len(p) for p in up_plans),)),
        ],
        compiler_params=params(60),
        cost_estimate=cost(14 * count * width * hidden_units // 4, 26 * count * width, 2 * count * hidden_units),
        name="hidden",
    )(place, lengths, rows, mixed, cotangent, table, *group_one[0], *group_two[0])


STATS_UP, STATS_ONE = 6, 10


def back_kernel(
    out_plan, up_plans, down_plan, sizes, place, lengths, rows, branch_in, active, slope, grad_down, cotangent,
    table, *refs,
):
    sources, refs = refs[: sum(sizes)], refs[sum(sizes) :]
    one, two = sources[: sizes[0]], sources[sizes[0] : sizes[0] + sizes[1]]
    three = sources[sizes[0] + sizes[1] :]
    result, grad_hidden, grad_middle_out, grad_branch, grad_mixed, stats = refs[:6]
    out_w, up_w, down_w, sems = refs[6:]
    made = [copies(place[0], three, down_plan, down_w, sems, 0)]
    first = len(down_plan)
    for m, plan in enumerate(up_plans):
        made.append(copies(place[0], two, plan, up_w.at[m], sems, first))
        first += len(plan)
    made.append(copies(place[0], one, out_plan, out_w, sems, first))

    @pl.when(pl.program_id(0) == 0)
    def _():
        for group in made:
            start_all(group)
        stats[...] = jnp.zeros_like(stats)
        wait_all(made[0])

    live = live_rows(lengths, cotangent.shape)
    branch = branch_in[...]
    middle = rows[...].astype(F32) + vector(table, ATTN_S) * branch
    down_out = dot(active[...], down_w[...]) + vector(table, DOWN_B)
    result[...] = jnp.where(live, middle + vector(table, MLP_S) * down_out, 0.0).astype(BF16)
    grad_out = jnp.where(live, cotangent[...].astype(F32), 0.0)
    sums = [row_sum(grad_out * down_out), row_sum(grad_down[...].astype(F32))]

    @pl.when(pl.program_id(0) == 0)
    def _():
        for group in made[1:]:
            wait_all(group)

    width = middle.shape[1]
    grad_normed = jnp.zeros(middle.shape, F32)
    for m in range(len(up_plans)):
        part = slice(m * width, (m + 1) * width)
        grad_active = dot_nt(grad_down[...], down_w[part, :])
        low = (grad_active * slope[:, part].astype(F32)).astype(BF16)
        grad_hidden[:, part] = low
        stats[STATS_UP + m : STATS_UP + m + 1, :] += row_sum(low.astype(F32))
        grad_normed += dot_nt(low, up_w[m])
    unit_rows, inverse = centred_rows(middle)
    sums += [row_sum(grad_normed * unit_rows), row_sum(grad_normed)]
    grad_middle = grad_out + norm_back(grad_normed, unit_rows, inverse, vector(table, LN2_G))
    grad_middle_out[...] = grad_middle
    low = (grad_middle * vector(table, ATTN_S)).astype(BF16)
    grad_branch[...] = low
    sums += [row_sum(grad_middle * branch), row_sum(low.astype(F32))]
    grad_mixed[...] = dot_nt(low, out_w[...]).astype(BF16)
    for at, total in enumerate(sums):
        stats[at : at + 1, :] += total


def back(place, lengths, rows, branch, active, slope, grad_down, cotangent, table, one, two, three):
    count, width = rows.shape
    hidden_units = active.shape[1]
    plans = (one[1][3], two[1], three[1][0])
    sizes = (len(one[0]), len(two[0]), len(three[0]))
    return pl.pallas_call(
        functools.partial(back_kernel, *plans, sizes),
        grid=(count // TILE,),
        in_specs=[SMEM, SMEM]
        + [tile_of(width)] * 2
        + [tile_of(hidden_units)] * 2
        + [tile_of(width)] * 2
        + [whole(table.shape)]
        + [ANY] * sum(sizes),
        out_specs=[tile_of(width), tile_of(hidden_units)]
        + [tile_of(width)] * 3
        + [whole((16, width))],
        out_shape=[
            jax.ShapeDtypeStruct(rows.shape, BF16),
            jax.ShapeDtypeStruct(active.shape, BF16),
            jax.ShapeDtypeStruct(rows.shape, F32),
            jax.ShapeDtypeStruct(rows.shape, BF16),
            jax.ShapeDtypeStruct(rows.shape, BF16),
            jax.ShapeDtypeStruct((16, width), F32),
        ],
        scratch_shapes=[
            pltpu.VMEM((width, width), BF16),
            pltpu.VMEM((len(plans[1]), width, width), BF16),
            pltpu.VMEM((hidden_units, width), BF16),
            pltpu.SemaphoreType.DMA(
                (len(plans[0]) + sum(len(p) for p in plans[1]) + len(plans[2]),)
            ),
        ],
        compiler_params=params(60),
        cost_estimate=cost(26 * count * width * hidden_units // 4, 40 * count * width),
        name="back",
    )(place, lengths, rows, branch, active, slope, grad_down, cotangent, table, *one[0], *two[0], *three[0])


def outer_kernel(spread, steps, place, *refs):
    lefts, refs = refs[: len(steps)], refs[len(steps) :]
    count = sum(len(own) for own in steps)
    rights, outs = refs[:count], refs[count:]
    step = pl.program_id(0)

    def put(left, right):
        value = dot_tn(left[...], right[...]).astype(BF16)
        if not spread:
            outs[0][...] = value
            return
        plane, core = place[0] // 2, place[0] % 2
        unit = value.shape[0] // 8
        for own in range(2):

            @pl.when(core == own)
            def _(own=own):
                for at in range(4):
                    for out, part in zip(outs, (own, 1 - own)):
                        first = (2 * at + part) * unit
                        out[at ^ plane, 0] = value[first : first + unit]

    first, at_right = 0, 0
    for left, own in zip(lefts, steps):
        for count in own:

            @pl.when((step >= first) & (step < first + count))
            def _(left=left, right=rights[at_right]):
                put(left, right)

            first += count
            at_right += 1


def outer(place, pairs, width):
    count, height = pairs[0][0].shape
    steps = [[right.shape[1] // width for right in rights] for _, rights in pairs]
    total = sum(sum(own) for own in steps)
    right_specs, first = [], 0
    for own in sum(steps, []):
        right_specs.append(
            pl.BlockSpec(
                (count, width),
                lambda i, first=first, own=own: (0, jnp.clip(i - first, 0, own - 1)),
            )
        )
        first += own
    if direct():
        block = pl.BlockSpec((4, 1, height // 8, width), lambda i: (0, i, 0, 0))
        shape = jax.ShapeDtypeStruct((4, total, height // 8, width), BF16)
        specs, shapes = [block, block], [shape, shape]
    else:
        specs = pl.BlockSpec((height, width), lambda i: (0, i))
        shapes = jax.ShapeDtypeStruct((height, total * width), BF16)
    return pl.pallas_call(
        functools.partial(outer_kernel, direct(), steps),
        grid=(total,),
        in_specs=[SMEM] + [whole((count, height))] * len(pairs) + right_specs,
        out_specs=specs,
        out_shape=shapes,
        compiler_params=params(54),
        cost_estimate=cost(2 * count * height * total * width, 2 * (count + height) * total * width),
        name="outer",
    )(place, *(left for left, _ in pairs), *(right for _, rights in pairs for right in rights))


def wide_outer_kernel(left, right, out):
    value = dot_tn(left[...], right[...]).astype(BF16)
    half = value.shape[1] // 2
    out[0] = value[:, :half]
    out[1] = value[:, half:]


def wide_outer(place, left, right):
    count, height = left.shape
    columns = right.shape[1]
    steps = 8
    step = columns // steps
    return pl.pallas_call(
        wide_outer_kernel,
        grid=(steps // 2,),
        in_specs=[whole(left.shape), pl.BlockSpec((count, 2 * step), lambda i: (0, i))],
        out_specs=pl.BlockSpec((2, height, step), lambda i: (i, 0, 0)),
        out_shape=jax.ShapeDtypeStruct((steps, height, step), BF16),
        compiler_params=params(60),
        cost_estimate=cost(2 * count * height * columns, 2 * (count + height) * (height + columns)),
        name="wide_outer",
    )(left, right)


def inputs_kernel(plans, place, rows, grad_middle, grad_q, grad_k, grad_v, table, earlier, *refs):
    count = len(refs) - 2 - 2
    sources, (grad_rows, stats, weights, sems) = refs[:count], refs[count:]
    made, first = [], 0
    for m in range(3):
        made.append(copies(place[0], sources, plans[m], weights.at[m], sems, first))
        first += len(plans[m])

    @pl.when(pl.program_id(0) == 0)
    def _():
        for group in made:
            start_all(group)
        stats[...] = earlier[...]
        for group in made:
            wait_all(group)

    grad = dot_nt(grad_q[...], weights[0])
    grad += dot_nt(grad_k[...], weights[1])
    grad += dot_nt(grad_v[...], weights[2])
    unit_rows, inverse = centred_rows(rows[...].astype(F32))
    grad_rows[...] = grad_middle[...] + norm_back(grad, unit_rows, inverse, vector(table, LN1_G))
    sums = [row_sum(grad * unit_rows), row_sum(grad)]
    sums += [row_sum(grad_q[...].astype(F32)), row_sum(grad_v[...].astype(F32))]
    for at, total in enumerate(sums):
        stats[STATS_ONE + at : STATS_ONE + at + 1, :] += total


def inputs_back(place, rows, grad_middle, grad_q, grad_k, grad_v, table, earlier, group):
    arrays, plans = group
    count, width = rows.shape
    return pl.pallas_call(
        functools.partial(inputs_kernel, plans),
        grid=(count // TILE,),
        in_specs=[SMEM] + [tile_of(width)] * 5 + [whole(table.shape)] * 2 + [ANY] * len(arrays),
        out_specs=[tile_of(width), whole((16, width))],
        out_shape=[
            jax.ShapeDtypeStruct(rows.shape, F32),
            jax.ShapeDtypeStruct((16, width), F32),
        ],
        scratch_shapes=[
            pltpu.VMEM((3, width, width), BF16),
            pltpu.SemaphoreType.DMA((sum(len(p) for p in plans[:3]),)),
        ],
        compiler_params=params(60),
        cost_estimate=cost(6 * count * width * width, 20 * count * width),
        name="inputs_back",
    )(place, rows, grad_middle, grad_q, grad_k, grad_v, table, earlier, *arrays)


def add_low(left, right):
    return (left.astype(F32) + right.astype(F32)).astype(left.dtype)


def split_cores(stacked):
    stacked = flip_own(stacked)
    pieces = stacked.reshape((-1, 2) + stacked.shape[1:])
    return pieces[:, 0], pieces[:, 1]


def quarters(held):
    held = held.reshape((-1, 4) + held.shape[1:])
    return tuple(held[:, i] for i in range(4))


def add_kernel(mine, other, own, by_x, by_y, near, far):
    total = (mine[...].astype(F32) + other[...].astype(F32)).astype(BF16)
    own[0] = total[0]
    early = pl.program_id(0) < pl.num_programs(0) // 2

    @pl.when(early)
    def _():
        by_x[0] = total[3]
        by_x[1] = total[1]
        far[0] = total[2]

    @pl.when(jnp.logical_not(early))
    def _():
        by_y[0] = total[3]
        by_y[1] = total[2]
        near[0] = total[1]


def sums_of_cores(mine, other):
    rows, columns = mine.shape[1:]
    half = rows // 2
    if not direct():
        own, near, far, corner = quarters(add_low(mine, other))
        by_x = jnp.stack([corner[:, :half], near[:, :half]], axis=1)
        by_y = jnp.stack([corner[:, half:], far[:, half:]], axis=1)
        return own, by_x, by_y, near[:, half:], far[:, :half]
    shapes = [(1, rows, columns), (2, half, columns), (2, half, columns), (1, half, columns), (1, half, columns)]
    steps = 2
    step = rows // steps
    spots = [
        lambda i: i,
        lambda i: jnp.minimum(i, steps // 2 - 1),
        lambda i: jnp.maximum(i - steps // 2, 0),
        lambda i: jnp.maximum(i - steps // 2, 0),
        lambda i: jnp.minimum(i, steps // 2 - 1),
    ]
    own, by_x, by_y, near, far = pl.pallas_call(
        add_kernel,
        grid=(steps,),
        in_specs=[pl.BlockSpec((4, step, columns), lambda i: (0, i, 0))] * 2,
        out_specs=[
            pl.BlockSpec((shape[0], step, columns), lambda i, spot=spot: (0, spot(i), 0))
            for shape, spot in zip(shapes, spots)
        ],
        out_shape=[jax.ShapeDtypeStruct(shape, BF16) for shape in shapes],
        compiler_params=params(24),
        cost_estimate=cost(4 * rows * columns, 24 * rows * columns),
        name="core_add",
    )(mine, other)
    return own, by_x[None], by_y[None], near, far


def second_sends(held, first):
    by_x, by_y = first
    return [add_low(held[3], by_y[:, 0]), add_low(held[4], by_x[:, 0])]


def own_sum(own, first, second):
    (by_x, by_y), (near, far) = first, second
    total = own.astype(F32) + jnp.concatenate([by_x[:, 1], near], axis=1).astype(F32)
    total = total + jnp.concatenate([far, by_y[:, 1]], axis=1).astype(F32)
    return total.astype(BF16)


def halve(total):
    for bit in reversed(range(3, wide_bits())):
        count = total.shape[0] // 2
        total = add_low(total[:count], cross(total[count:], bit))
    return total[0]


def spread_blocks(stacked):
    size = stacked.shape[0]
    here = lax.axis_index("narrow")
    steps = sorted(range(1, size), key=lambda step: min(step, size - step))
    blocks = [
        lax.dynamic_index_in_dim(stacked, lax.rem(here + step, size), keepdims=False)
        for step in steps
    ]
    return blocks, [lambda v, step=step: shift(v, step) for step in steps]


def add_blocks(stacked, moved):
    total = lax.dynamic_index_in_dim(stacked, lax.axis_index("narrow"), keepdims=False)
    total = total.astype(F32)
    for block in moved:
        total = total + block.astype(F32)
    return total


def column_starts(columns, part, layers):
    starts = [at * part // 128 * 128 for at in range(layers)]
    room = max(-(-(at + 1) * part // 128) * 128 - starts[at] for at in range(layers))
    return [min(start, columns - room) for start in starts], room


def columns_blocks(blocks, part, layers):
    here = lax.axis_index("narrow")
    starts, room = column_starts(blocks.shape[1], part, layers)
    choices = [blocks[:, start : start + room] for start in starts]

    def block_of(index):
        chosen = choices[-1]
        for at in reversed(range(layers - 1)):
            chosen = jnp.where(index == at, choices[at], chosen)
        return chosen

    own, *sends = [block_of(lax.rem(here + step, layers)) for step in range(layers)]
    return own, sends, shifts(layers)


def own_columns(own, moved, part, columns):
    layers = len(moved) + 1
    here = lax.axis_index("narrow")
    starts, _ = column_starts(columns, part, layers)
    total = own.astype(F32)
    for block in moved:
        total = total + block.astype(F32)
    cuts = [total[:, at * part - start : (at + 1) * part - start] for at, start in enumerate(starts)]
    result = cuts[-1]
    for at in reversed(range(layers - 1)):
        result = jnp.where(here == at, cuts[at], result)
    return result


def by_core(grad, parts):
    if direct():
        return tuple(piece.reshape(4, -1, piece.shape[3]) for piece in grad)
    places = lax.axis_size("wide")
    height, columns = grad.shape
    stacked = grad.reshape(places, height // places, parts, columns // parts).transpose(0, 2, 1, 3)
    return split_cores(stacked.reshape(places, -1, columns // parts))


def own_spot(places, layers, piece, width):
    start = (lax.axis_index("wide") * layers + lax.axis_index("narrow")) * piece
    return start // width, start % width


def shards(
    patches, lengths, w_qkv, w_out, w_up, w_down, ln1_gain, ln1_bias, q_bias, v_bias, out_bias, attn_scale,
    ln2_gain, ln2_bias, up_bias, down_bias, mlp_scale, cotangent,
):
    places, layers = lax.axis_size("wide"), lax.axis_size("narrow")
    place = lax.axis_index("wide").astype(jnp.int32).reshape(1)
    short, width = w_up.shape
    part = w_qkv.shape[1]
    quarter = w_out.shape[1]
    packs, pack_rows, _ = patches.shape
    rows = patches.reshape(-1, width)
    cotangent = cotangent.reshape(-1, width)

    small = [ln1_gain, ln1_bias, q_bias, v_bias, out_bias, attn_scale, ln2_gain, ln2_bias, down_bias, mlp_scale]
    piece, long = ln1_gain.shape[0], up_bias.shape[0]
    small_spot = own_spot(places, layers, piece, width)
    up_spot = own_spot(places, layers, long, width)
    extra = jnp.pad(jnp.stack(small), ((0, 0), (0, part - piece)))
    extra = jnp.concatenate([extra, jnp.pad(up_bias[None], ((0, 5), (0, part - long)))])
    extra = jnp.pad(extra, ((0, 0), (0, quarter)))
    early = jnp.concatenate([jnp.concatenate([w_qkv, w_out], axis=1), extra])

    moved = [move(early) for move in shifts(layers)]
    one = by_origin([early, *moved])
    extra = side_by_side(one[:, short : short + 10, :piece])
    extra = jnp.pad(extra, ((0, 6), (0, width - layers * piece)))
    long_row = side_by_side(one[:, short + 10 : short + 11, :long])
    long_row = jnp.pad(long_row, ((10, 5), (0, width - layers * long)))
    qkv, out = side_by_side(one[:, :short, :part]), side_by_side(one[:, :short, part:])
    one = jnp.concatenate([*jnp.split(qkv, 3, axis=1), out, extra + long_row])
    held = double(one)
    sends = [held, held] + [w_up] * (layers - 1)
    (near, far, *two) = [move(send) for move, send in zip(planes() + shifts(layers), sends)]
    near, far, two = lax.optimization_barrier((near, far, two))
    half = near.shape[1] // 32 * 16
    sends = [near[:, :half], far[:, half:], jnp.concatenate([held, near, far])]
    two = by_origin([w_up, *two]).reshape(-1, width)
    two, sends = lax.optimization_barrier((two, sends))
    two = in_order(lax.all_gather(two, "wide"), layers)
    moves = corners() + [lambda v: cross(v, 0)]
    moved = lax.optimization_barrier([move(send) for move, send in zip(moves, sends)])
    planes_one = held, near, far, jnp.concatenate(moved[:2], axis=1)
    side_down = jnp.concatenate(jnp.split(w_down, layers, axis=0), axis=1)
    side_down = after(side_down, moved)
    one, extras = matrices(planes_one, (moved[2], cross(planes_one[3], 0)), 4, layers * piece, layers * long)

    (normed, query, key, value, table), three = beside(
        lambda v: project(place, v, extras, one), rows, [side_down] * (layers - 1), shifts(layers)
    )
    three = by_origin([side_down, *three])
    three = jnp.concatenate(
        [side_by_side(three[:, :, i * quarter : (i + 1) * quarter]) for i in range(layers)]
    )
    query, three = lax.optimization_barrier((query, three))
    three = in_order(lax.all_gather(three, "wide"), 1)
    kept, mixed = [], ()
    for pack in range(packs):
        mixed, weights = attend(lengths, query, key, value, pack, mixed)
        mixed = (mixed,)
        kept.append(weights)
    (mixed,) = mixed
    branch, normed_two, active, slope, grad_down = hidden(
        place, lengths, rows, mixed, cotangent, table, one, two
    )
    grad_w_down = wide_outer(place, grad_down, active)
    active = after(active, grad_w_down)
    if places != 8:
        grad_w_down = grad_w_down.reshape(8, width, places // 8, -1).transpose(0, 2, 1, 3)
    total_down = lax.psum_scatter(grad_w_down.reshape(places, width, -1), "wide")

    result, grad_hidden, grad_middle, grad_branch, grad_mixed, stats = back(
        place, lengths, rows, branch, active, slope, grad_down, cotangent, table, one, two, three
    )
    mine, theirs = by_core(
        outer(place, [(normed_two, [grad_hidden]), (mixed, [grad_branch])], width), layers + 1
    )
    def heads_back(grads, value, spans):
        for pack, first, last in spans:
            grads = attend_back(query, key, value_rows, value, kept[pack], pack, first, last, grads)
        return grads

    groups = width // (HEADS * HD)
    spans = [(0, 0, groups - 1), (0, groups - 1, groups)] + [(pack, 0, groups) for pack in range(1, packs)]
    value_rows = value
    grads, (other,) = beside(
        lambda v: heads_back((), v, spans[:1]), grad_mixed, [theirs], [lambda v: cross(v, 0)]
    )
    up_held = sums_of_cores(mine, other)
    total_down, grads = lax.optimization_barrier((total_down, grads))
    total_down = lax.psum_scatter(total_down.reshape(layers, quarter, -1), "narrow")
    grads, up_moved = beside(
        lambda v: heads_back(v, grad_mixed, spans[1:]), grads, up_held[1:3], planes()
    )
    sends = second_sends(up_held, up_moved)
    grads, sends = lax.optimization_barrier((grads, sends))
    mine_theirs, moved = beside(
        lambda v: outer(place, [(normed, v)], width), grads, sends, planes()
    )
    mine_theirs, total_down = lax.optimization_barrier((mine_theirs, total_down))
    mine, theirs = by_core(mine_theirs, 3)
    total_up = halve(own_sum(up_held[0], up_moved, moved))
    total_out = total_up[layers * short :].reshape(short, layers, quarter).transpose(1, 0, 2)
    total_up = total_up[: layers * short].reshape(layers, short, width)
    total_up = jnp.concatenate([total_up, total_out], axis=2)
    total_up, theirs = lax.optimization_barrier((total_up, theirs))
    total_up = lax.psum_scatter(total_up, "narrow")
    held = sums_of_cores(mine, cross(theirs, 0))
    grad_q, grad_k, grad_v = grads
    (grad_rows, sums), first = beside(
        lambda v: inputs_back(place, rows, grad_middle, v, grad_k, grad_v, table, stats, one),
        grad_q,
        held[1:3],
        planes(),
    )
    both = [lambda v: exchange(v, "wide", lambda i: i ^ 6)]
    sums, moved = beside(
        lambda v: v, sums, [*second_sends(held, first), sums, sums, sums], planes() + planes() + both
    )
    second = moved[:2]
    for piece_sums in moved[2:]:
        sums = sums + piece_sums
    total_qkv = halve(own_sum(held[0], first, second))
    blocks = jnp.concatenate([total_qkv[i * short : (i + 1) * short] for i in range(3)], axis=1)
    own_block, sends, moves = columns_blocks(blocks, part, layers)
    def last_part(value):
        sums, total_up, total_down = value
        return sums, total_up.astype(F32), total_down.astype(F32).T

    (sums, total_up, total_down), moved = beside(
        last_part, (sums, total_up, total_down), [*sends, *[sums] * (layers - 1)], moves + shifts(layers)
    )
    total_qkv = own_columns(own_block, moved[: layers - 1], part, blocks.shape[1])
    for piece_sums in moved[layers - 1 :]:
        sums = sums + piece_sums
    for bit in (0, *range(3, wide_bits())):
        sums = sums + cross(sums, bit)

    own = lax.dynamic_slice(sums, (0, small_spot[1]), (16, piece))
    own_up = lax.dynamic_slice(sums, (STATS_UP + up_spot[0], up_spot[1]), (1, long))[0]
    return (
        result.reshape(patches.shape),
        grad_rows.reshape(patches.shape),
        total_qkv,
        total_up[:, width:],
        total_up[:, :width],
        total_down,
        own[STATS_ONE],
        own[STATS_ONE + 1],
        own[STATS_ONE + 2],
        own[STATS_ONE + 3],
        own[5],
        own[4],
        own[2],
        own[3],
        own_up,
        own[1],
        own[0],
    )


def solution(mesh):
    return jax.shard_map(
        shards,
        mesh=mesh,
        in_specs=(
            P(("wide", "narrow"), None, None),
            P(("wide", "narrow"), None),
            P("wide", "narrow"),
            P("wide", "narrow"),
            P("wide", "narrow"),
            P("wide", "narrow"),
            P(("wide", "narrow")),
            P(("wide", "narrow")),
            P(("wide", "narrow")),
            P(("wide", "narrow")),
            P(("wide", "narrow")),
            P(("wide", "narrow")),
            P(("wide", "narrow")),
            P(("wide", "narrow")),
            P(("wide", "narrow")),
            P(("wide", "narrow")),
            P(("wide", "narrow")),
            P(("wide", "narrow"), None, None),
        ),
        out_specs=(
            P(("wide", "narrow"), None, None),
            P(("wide", "narrow"), None, None),
            P("wide", "narrow"),
            P("wide", "narrow"),
            P("wide", "narrow"),
            P("wide", "narrow"),
            P(("wide", "narrow")),
            P(("wide", "narrow")),
            P(("wide", "narrow")),
            P(("wide", "narrow")),
            P(("wide", "narrow")),
            P(("wide", "narrow")),
            P(("wide", "narrow")),
            P(("wide", "narrow")),
            P(("wide", "narrow")),
            P(("wide", "narrow")),
            P(("wide", "narrow")),
        ),
        check_vma=False,
    )
```
